32 devices in a mesh: dp: 8 (over z, y), head: 4 (over x, core).
Axes of the slice: x: 2, y: 2, z: 4, core: 2. Of those that a mesh axis runs over, the one named last changes fastest.
Arguments:
- block_in: bfloat16 [12544, 768], P('dp'), may hold values from -6 to 6
- resolution: int32 [16], P('dp'), may hold values from 0 to 1
- cotangent: bfloat16 [12544, 768], P(('dp', 'head')), may hold values from -6 to 6
- w_qkv: float32 [768, 3, 768], P('dp', None, 'head'), may hold values from -0.21875 to 0.21875
- w_proj: float32 [768, 768], P('head', 'dp'), may hold values from -1.75 to 1.75
- w_fc1: float32 [768, 3072], P('dp', 'head'), may hold values from -0.21875 to 0.21875
- w_fc2: float32 [3072, 768], P('head', 'dp'), may hold values from -0.109375 to 0.109375
- mom_qkv: float32 [768, 3, 768], P('dp', None, 'head'), may hold values from -160 to 160
- mom_proj: float32 [768, 768], P('head', 'dp'), may hold values from -40 to 40
- mom_fc1: float32 [768, 3072], P('dp', 'head'), may hold values from -160 to 160
- mom_fc2: float32 [3072, 768], P('head', 'dp'), may hold values from -320 to 320
- avg_qkv: float32 [768, 3, 768], P('dp', None, 'head'), may hold values from -0.21875 to 0.21875
- avg_proj: float32 [768, 768], P('head', 'dp'), may hold values from -1.75 to 1.75
- avg_fc1: float32 [768, 3072], P('dp', 'head'), may hold values from -0.21875 to 0.21875
- avg_fc2: float32 [3072, 768], P('head', 'dp'), may hold values from -0.109375 to 0.109375
- gains: float32 [2, 768], replicated, may hold values from 0.5 to 1.5
- gain_mom: float32 [2, 768], replicated, may hold values from -160 to 160
- gain_avg: float32 [2, 768], replicated, may hold values from 0.5 to 1.5
- biases: float32 [7680], replicated, may hold values from -1.75 to 1.75
- bias_mom: float32 [7680], replicated, may hold values from -160 to 160
- bias_avg: float32 [7680], replicated, may hold values from -1.75 to 1.75
Outputs:
- block_out: bfloat16 [12544, 768], P(('dp', 'head'))
- input_grad: float32 [12544, 768], P(('dp', 'head'))
- qkv_grad: float32 [768, 3, 768], P('dp', None, 'head')
- qkv_mom: float32 [768, 3, 768], P('dp', None, 'head')
- qkv_new: float32 [768, 3, 768], P('dp', None, 'head')
- qkv_avg: float32 [768, 3, 768], P('dp', None, 'head')
- proj_grad: float32 [768, 768], P('head', 'dp')
- proj_mom: float32 [768, 768], P('head', 'dp')
- proj_new: float32 [768, 768], P('head', 'dp')
- proj_avg: float32 [768, 768], P('head', 'dp')
- fc1_grad: float32 [768, 3072], P('dp', 'head')
- fc1_mom: float32 [768, 3072], P('dp', 'head')
- fc1_new: float32 [768, 3072], P('dp', 'head')
- fc1_avg: float32 [768, 3072], P('dp', 'head')
- fc2_grad: float32 [3072, 768], P('head', 'dp')
- fc2_mom: float32 [3072, 768], P('head', 'dp')
- fc2_new: float32 [3072, 768], P('head', 'dp')
- fc2_avg: float32 [3072, 768], P('head', 'dp')
- gain_grad: float32 [2, 768], replicated
- gain_mom_new: float32 [2, 768], replicated
- gain_new: float32 [2, 768], replicated
- gain_avg_new: float32 [2, 768], replicated
- bias_grad: float32 [7680], replicated
- bias_mom_new: float32 [7680], replicated
- bias_new: float32 [7680], replicated
- bias_avg_new: float32 [7680], replicated
The draws below stay inside these ranges and needn't reach their ends.
Inputs may be any that keep to these rules, and one draw needn't show every extreme that they name: `resolution`: 1 marks a slot holding one image of 784 patches, 0 a slot holding 784 // 196 images of 196 patches.
All inputs are finite; a program needn't handle non-finite values.
Results may differ from the reference program's by a relative error of at most 0.015.
Values may be sent and summed in bfloat16 or wider, within the bound.
No kernel may reach another device: no remote copies, remote signals or barrier semaphores. Data moves between devices by JAX's collectives and lax.ppermute only.
A program may use at most 128 MiB of HBM per device.

```python
import jax
import jax.numpy as jnp
from jax import lax

D = 768
ATTENTION_HEADS = 12
HEAD_WIDTH = 64
FF = 3072
SLOT_PATCHES = 784
LOWRES = 196
TOTAL_SLOTS = 16
TOKENS = 12544
N_HEAD = 4


def plant(drawn, own_key, smallest, largest):
    extent = drawn.shape
    spot = [jax.random.randint(jax.random.fold_in(own_key, axis), (), 0, extent[axis]) for axis in range(len(extent))]
    drawn = drawn.at[tuple(spot)].set(smallest)
    longest = extent.index(max(extent))
    spot[longest] = (spot[longest] + 1) % extent[longest]
    return drawn.at[tuple(spot)].set(largest)


def shard_levels(key, dims, shards, low, top_value):
    factor_of, own = 1.0, jax.random.fold_in(key, 6)
    for position, parts in shards:
        heights = jnp.exp(jax.random.uniform(jax.random.fold_in(own, position), (parts,), jnp.float32, low / len(shards), top_value / len(shards)))
        factor_of = factor_of * jnp.repeat(heights, dims[position] // parts).reshape([-1 if axis == position else 1 for axis in range(len(dims))])
    return factor_of


def scatter_about(rng, shape, scale, limit, shards=(), kind=jnp.bfloat16):
    level = shard_levels(rng, shape, shards, -0.22, 0.18) if shards else 1.0
    array = jax.random.normal(rng, shape, jnp.float32) * scale * level
    return jnp.minimum(jnp.maximum(array, -limit), limit).astype(kind)


def setup_inputs(seed: int = 0) -> dict:
    keys = jax.random.split(jax.random.key(seed), 22)
    return {
        "block_in": scatter_about(keys[0], (TOKENS, D), 1.0, 6.0, ((0, 8),)),
        "resolution": plant(jax.random.randint(keys[1], (TOTAL_SLOTS,), 0, 2), jax.random.fold_in(keys[1], 1), 0, 1).astype(jnp.int32),
        "cotangent": scatter_about(keys[2], (TOKENS, D), 1.0, 6.0, ((0, 32),)),
        "w_qkv": scatter_about(keys[3], (D, 3, ATTENTION_HEADS * HEAD_WIDTH), D ** -0.5, 0.21875, ((0, 8), (2, 4)), jnp.float32),
        "w_proj": scatter_about(keys[4], (ATTENTION_HEADS * HEAD_WIDTH, D), (D // 64) ** -0.5, 1.75, ((0, 4), (1, 8)), jnp.float32),
        "w_fc1": scatter_about(keys[5], (D, FF), D ** -0.5, 0.21875, ((0, 8), (1, 4)), jnp.float32),
        "w_fc2": scatter_about(keys[6], (FF, D), FF ** -0.5, 0.109375, ((0, 4), (1, 8)), jnp.float32),
        "mom_qkv": scatter_about(keys[7], (D, 3, ATTENTION_HEADS * HEAD_WIDTH), (TOKENS ** 0.5 // 4), 160.0, ((0, 8), (2, 4)), jnp.float32),
        "mom_proj": scatter_about(keys[8], (ATTENTION_HEADS * HEAD_WIDTH, D), (TOKENS ** 0.5 // 16), 40.0, ((0, 4), (1, 8)), jnp.float32),
        "mom_fc1": scatter_about(keys[9], (D, FF), (TOKENS ** 0.5 // 4), 160.0, ((0, 8), (1, 4)), jnp.float32),
        "mom_fc2": scatter_about(keys[10], (FF, D), (TOKENS ** 0.5 // 2), 320.0, ((0, 4), (1, 8)), jnp.float32),
        "avg_qkv": scatter_about(keys[11], (D, 3, ATTENTION_HEADS * HEAD_WIDTH), D ** -0.5, 0.21875, ((0, 8), (2, 4)), jnp.float32),
        "avg_proj": scatter_about(keys[12], (ATTENTION_HEADS * HEAD_WIDTH, D), (D // 64) ** -0.5, 1.75, ((0, 4), (1, 8)), jnp.float32),
        "avg_fc1": scatter_about(keys[13], (D, FF), D ** -0.5, 0.21875, ((0, 8), (1, 4)), jnp.float32),
        "avg_fc2": scatter_about(keys[14], (FF, D), FF ** -0.5, 0.109375, ((0, 4), (1, 8)), jnp.float32),
        "gains": jnp.clip(1.0 + 0.1 * jax.random.normal(keys[15], (2, D), jnp.float32), 0.5, 1.5),
        "gain_mom": scatter_about(keys[16], (2, D), (TOKENS ** 0.5 // 4), 160.0, (), jnp.float32),
        "gain_avg": jnp.clip(1.0 + 0.1 * jax.random.normal(keys[17], (2, D), jnp.float32), 0.5, 1.5),
        "biases": scatter_about(keys[18], (4 * D + 2 * ATTENTION_HEADS * HEAD_WIDTH + FF,), 0.3, 1.75, (), jnp.float32),
        "bias_mom": scatter_about(keys[19], (4 * D + 2 * ATTENTION_HEADS * HEAD_WIDTH + FF,), (TOKENS ** 0.5 // 4), 160.0, (), jnp.float32),
        "bias_avg": scatter_about(keys[20], (4 * D + 2 * ATTENTION_HEADS * HEAD_WIDTH + FF,), 0.3, 1.75, (), jnp.float32),
    }


@jax.custom_vjp
def low(v):
    return lax.optimization_barrier(v.astype(jnp.bfloat16)).astype(jnp.float32)

@jax.custom_vjp
def low_back(v):
    return v

def low_keep(v):
    return (low(v), None)

def low_pass(kept, grad):
    return (grad,)

def back_keep(v):
    return (v, None)

def back_low(kept, grad):
    return (low(grad),)
low.defvjp(low_keep, low_pass)
low_back.defvjp(back_keep, back_low)
EPSILON = 1e-06
MOMENTUM_RATE = 0.9
AVERAGING = 0.75
WEIGHT_DECAY = 0.05
RATE_QKV = 0.001
RATE_PROJ = 0.01
RATE_FC1 = 0.0006
RATE_FC2 = 0.0003
RATE_SMALL = 0.003
MASKED = -1000000000.0
HIGHEST = lax.Precision.HIGHEST

def layer_norm(inputs, gain_row, shift_row):
    mean_row = lax.optimization_barrier(jnp.mean(inputs, axis=-1, keepdims=True))
    centred = inputs - mean_row
    spread = lax.optimization_barrier(jnp.mean(centred * centred, axis=-1, keepdims=True))
    return centred * lax.rsqrt(spread + EPSILON) * gain_row + shift_row

def attend(pieces):
    queries, key_rows, value_rows, slot_kind = pieces
    scores = jnp.einsum('qhc,khc->hqk', queries, key_rows, precision=HIGHEST) * HEAD_WIDTH ** (-0.5)
    scores = low_back(scores)
    segment = jnp.arange(SLOT_PATCHES, dtype=jnp.int32) // LOWRES
    allowed = (segment[:, None] == segment[None, :]) | (slot_kind > 0)
    weights = low(jax.nn.softmax(jnp.where(allowed, scores, MASKED), axis=-1))
    return jnp.einsum('hqk,khc->qhc', weights, value_rows, precision=HIGHEST)

def forward(layer_input, w_qkv, w_proj, w_fc1, w_fc2, gains, biases, resolution):
    all_cols = ATTENTION_HEADS * HEAD_WIDTH
    ln1_shift = biases[0:D]
    ln2_shift = biases[D:2 * D]
    proj_bias = biases[2 * D:3 * D]
    fc2_bias = biases[3 * D:4 * D]
    query_bias = biases[4 * D:4 * D + all_cols]
    value_bias = biases[4 * D + all_cols:4 * D + 2 * all_cols]
    fc1_bias = biases[4 * D + 2 * all_cols:]
    normed = low(layer_norm(layer_input, gains[0], ln1_shift))
    mixed = jnp.einsum('td,dkc->tkc', normed, low(w_qkv), precision=HIGHEST)
    queries = low_back(low(mixed[:, 0] + query_bias))
    key_rows = low_back(low(mixed[:, 1]))
    value_rows = low_back(low(mixed[:, 2] + value_bias))
    slot_arrangement = (TOTAL_SLOTS, SLOT_PATCHES, ATTENTION_HEADS, HEAD_WIDTH)
    context = lax.map(jax.checkpoint(attend), (queries.reshape(slot_arrangement), key_rows.reshape(slot_arrangement), value_rows.reshape(slot_arrangement), resolution))
    context = low_back(low(context.reshape(TOKENS, all_cols)))
    grouped = context.reshape(TOKENS, N_HEAD, all_cols // N_HEAD)
    proj_groups = low(w_proj).reshape(N_HEAD, all_cols // N_HEAD, D)
    attn_parts = jnp.einsum('tgc,gcd->gtd', grouped, proj_groups, precision=HIGHEST)
    middle = layer_input + (low_back(lax.optimization_barrier(jnp.sum(low(attn_parts), axis=0))) + proj_bias)
    normed_mid = low(layer_norm(middle, gains[1], ln2_shift))
    pre_act = low_back(jnp.dot(normed_mid, low(w_fc1), precision=HIGHEST) + fc1_bias)
    hidden = low(jax.nn.gelu(pre_act, approximate=False))
    hidden_groups = hidden.reshape(TOKENS, N_HEAD, FF // N_HEAD)
    fc2_groups = low(w_fc2).reshape(N_HEAD, FF // N_HEAD, D)
    mlp_parts = jnp.einsum('tgf,gfd->gtd', hidden_groups, fc2_groups, precision=HIGHEST)
    return middle + lax.optimization_barrier(jnp.sum(low(mlp_parts), axis=0)) + fc2_bias

def update(weight, gradient, moment, average, step_rate, decay_rate):
    step_grad = gradient + decay_rate * weight
    moment_new = MOMENTUM_RATE * moment + step_grad
    weight_new = weight - step_rate * (step_grad + MOMENTUM_RATE * moment_new)
    return (moment_new, weight_new, AVERAGING * average + (1.0 - AVERAGING) * weight_new)

def reference(block_in, resolution, cotangent, w_qkv, w_proj, w_fc1, w_fc2, mom_qkv, mom_proj, mom_fc1, mom_fc2, avg_qkv, avg_proj, avg_fc1, avg_fc2, gains, gain_mom, gain_avg, biases, bias_mom, bias_avg):

    def layer(layer_input, qkv_now, proj_now, fc1_now, fc2_now, gains_now, biases_now):
        return forward(layer_input, qkv_now, proj_now, fc1_now, fc2_now, gains_now, biases_now, resolution)
    output, pullback = jax.vjp(layer, block_in.astype(jnp.float32), w_qkv, w_proj, w_fc1, w_fc2, gains, biases)
    grads = pullback(cotangent.astype(jnp.float32))
    qkv_mom, qkv_new, qkv_avg = update(w_qkv, grads[1], mom_qkv, avg_qkv, RATE_QKV, WEIGHT_DECAY)
    proj_mom, proj_new, proj_avg = update(w_proj, grads[2], mom_proj, avg_proj, RATE_PROJ, WEIGHT_DECAY)
    fc1_mom, fc1_new, fc1_avg = update(w_fc1, grads[3], mom_fc1, avg_fc1, RATE_FC1, WEIGHT_DECAY)
    fc2_mom, fc2_new, fc2_avg = update(w_fc2, grads[4], mom_fc2, avg_fc2, RATE_FC2, WEIGHT_DECAY)
    gain_mom_new, gain_new, gain_avg_new = update(gains, grads[5], gain_mom, gain_avg, RATE_SMALL, 0.0)
    bias_mom_new, bias_new, bias_avg_new = update(biases, grads[6], bias_mom, bias_avg, RATE_SMALL, 0.0)
    return (output.astype(jnp.bfloat16), grads[0], grads[1], qkv_mom, qkv_new, qkv_avg, grads[2], proj_mom, proj_new, proj_avg, grads[3], fc1_mom, fc1_new, fc1_avg, grads[4], fc2_mom, fc2_new, fc2_avg, grads[5], gain_mom_new, gain_new, gain_avg_new, grads[6], bias_mom_new, bias_new, bias_avg_new)
```

```python
from functools import partial

import jax
import jax.numpy as jnp
from jax import lax
from jax.sharding import PartitionSpec as P

HEAD_WIDTH = 64
SLOT_PATCHES = 784
LOWRES = 196


EPSILON = 1e-06
MOMENTUM_RATE = 0.9
AVERAGING = 0.75
WEIGHT_DECAY = 0.05
RATE_QKV = 0.001
RATE_PROJ = 0.01
RATE_FC1 = 0.0006
RATE_FC2 = 0.0003
RATE_SMALL = 0.003
MASKED = -1000000000.0
F32 = jnp.float32
BF16 = jnp.bfloat16


def normalize(inputs):
    mean_row = jnp.mean(inputs, axis=-1, keepdims=True)
    centred = inputs - mean_row
    spread = jnp.mean(centred * centred, axis=-1, keepdims=True)
    inv_std = lax.rsqrt(spread + EPSILON)
    return (centred * inv_std, inv_std)


def norm_back(grad_out, centred, inv_std, gain_row):
    scaled = grad_out * gain_row
    return inv_std * (
        scaled
        - jnp.mean(scaled, axis=-1, keepdims=True)
        - centred * jnp.mean(scaled * centred, axis=-1, keepdims=True)
    )


def visible(slot_kind):
    segment = jnp.arange(SLOT_PATCHES, dtype=jnp.int32) // LOWRES
    return (segment[:, None] == segment[None, :]) | (slot_kind > 0)


def update(weight, gradient, moment, average, step_rate, decay_rate):
    step_grad = gradient + decay_rate * weight
    moment_new = MOMENTUM_RATE * moment + step_grad
    weight_new = weight - step_rate * (step_grad + MOMENTUM_RATE * moment_new)
    return (moment_new, weight_new, AVERAGING * average + (1.0 - AVERAGING) * weight_new)


def swap(value, axis, mask):
    return lax.ppermute(value, axis, [(i, i ^ mask) for i in range(lax.axis_size(axis))])


def line_masks(count):
    masks, mask = [], count // 2
    while mask > 1:
        masks.append(mask)
        mask //= 2
    return masks


def line_order(count):
    order = [0]
    for mask in line_masks(count):
        order = order + [r ^ mask for r in order]
    return order


def gather(shard, count, me):
    rows, cols = shard.shape
    half = rows // 2
    line = shard[None]
    for mask in line_masks(count):
        line = jnp.concatenate([line, swap(line, "dp", mask)])
    over_x = swap(line, "head", 2)
    over_y = swap(line, "dp", 1)
    both = jnp.concatenate(
        [swap(over_y[:, :half], "head", 2), swap(over_x[:, half:], "dp", 1)], axis=1
    )
    order = line_order(count) + [r ^ 1 for r in line_order(count)]
    place = [order.index(r) for r in range(count)]
    pick = jnp.array(place, jnp.int32)[jnp.arange(count, dtype=jnp.int32) ^ me]

    def whole(first, second):
        return jnp.concatenate([first, second])[pick].reshape(count * rows, cols)

    return whole(line, over_y), whole(over_x, both)


def scatter(own, other, count, me):
    rows = own.shape[0] // count
    cols = own.shape[1]
    half = rows // 2
    order = jnp.array(line_order(count) + [r ^ 1 for r in line_order(count)], jnp.int32)
    own = own.reshape(count, rows, cols)[order ^ me]
    other = other.reshape(count, rows, cols)[order ^ me]
    near = count // 2

    def low(value):
        return value.astype(BF16)

    a_sum = own[:, :half] + swap(low(other[:, :half]), "head", 2)
    b_send = jnp.stack([own[near:, half:], other[near:, half:]])
    b_sum = jnp.stack([own[:near, half:], other[:near, half:]]) + swap(low(b_send), "dp", 1)
    a_sum = a_sum[:near] + swap(low(a_sum[near:]), "dp", 1)
    b_sum = b_sum[0] + swap(low(b_sum[1]), "head", 2)
    total = jnp.concatenate([a_sum, b_sum], axis=1)
    for mask in reversed(line_masks(count)):
        keep = total.shape[0] // 2
        total = total[:keep] + swap(low(total[keep:]), "dp", mask)
    return total[0]


def shards(
    block_in,
    resolution,
    cotangent,
    w_qkv,
    w_proj,
    w_fc1,
    w_fc2,
    mom_qkv,
    mom_proj,
    mom_fc1,
    mom_fc2,
    avg_qkv,
    avg_proj,
    avg_fc1,
    avg_fc2,
    gains,
    gain_mom,
    gain_avg,
    biases,
    bias_mom,
    bias_avg,
):
    members = lax.axis_size("head")
    count = lax.axis_size("dp")
    member = lax.axis_index("head")
    me = lax.axis_index("dp")
    slot = member // 2
    core = member % 2
    model_width = block_in.shape[1]
    head_cols = w_qkv.shape[2]
    hidden_cols = w_fc1.shape[1]
    all_cols = head_cols * members
    row_share = cotangent.shape[0]
    local_heads = head_cols // HEAD_WIDTH
    scale_factor = HEAD_WIDTH ** (-0.5)
    row_start = core * row_share
    shard_rows = w_qkv.shape[0]
    groups = (member, member ^ 2)

    qkvp = jnp.concatenate(
        [w_qkv.astype(BF16).reshape(shard_rows, 3 * head_cols), w_proj.astype(BF16).T], axis=1
    )
    full_qkvp = gather(qkvp, count, me)
    full_fc1 = gather(w_fc1.astype(BF16), count, me)
    full_fc2 = gather(w_fc2.astype(BF16).T, count, me)

    ln1_shift = biases[0:model_width]
    ln2_shift = biases[model_width : 2 * model_width]
    proj_bias = biases[2 * model_width : 3 * model_width]
    fc2_bias = biases[3 * model_width : 4 * model_width]

    def bias_of(start, width, group):
        return lax.dynamic_slice_in_dim(biases, start + group * width, width)

    layer_input = lax.dynamic_slice_in_dim(
        block_in, slot * SLOT_PATCHES, SLOT_PATCHES, 0
    ).astype(F32)
    slot_kind = lax.dynamic_index_in_dim(resolution, slot, keepdims=False)
    peer = swap(cotangent, "head", 1)
    grad_out = jnp.where(
        core == 0, jnp.concatenate([cotangent, peer]), jnp.concatenate([peer, cotangent])
    )

    xhat1, inv1 = normalize(layer_input)
    normed = (xhat1 * gains[0] + ln1_shift).astype(BF16)

    def heads(rows):
        return rows.reshape(SLOT_PATCHES, local_heads, HEAD_WIDTH)

    saved, attn = [], []
    for group, full in zip(groups, full_qkvp):
        mixed = jnp.dot(normed, full[:, : 3 * head_cols], preferred_element_type=F32)
        query = heads(
            (mixed[:, :head_cols] + bias_of(4 * model_width, head_cols, group)).astype(BF16)
        )
        keys = heads(mixed[:, head_cols : 2 * head_cols].astype(BF16))
        value = heads(
            (
                mixed[:, 2 * head_cols :] + bias_of(4 * model_width + all_cols, head_cols, group)
            ).astype(BF16)
        )
        scores = jnp.einsum("qhc,khc->hqk", query, keys, preferred_element_type=F32) * scale_factor
        scores = jnp.where(visible(slot_kind), scores, MASKED)
        largest = jnp.max(scores, axis=-1, keepdims=True)
        expon = jnp.exp(scores - largest)
        summed = jnp.sum(expon, axis=-1, keepdims=True)
        probs = (expon / summed).astype(BF16)
        context = jnp.einsum("hqk,khc->qhc", probs, value, preferred_element_type=F32)
        context = context.astype(BF16).reshape(SLOT_PATCHES, head_cols)
        saved.append((query, keys, value, largest, summed, context))
        attn.append(
            jnp.einsum(
                "tc,dc->td", context, full[:, 3 * head_cols :], preferred_element_type=F32
            ).astype(BF16)
        )

    def both_cores(parts):
        mine = sum(p.astype(F32) for p in parts)
        return mine + sum(swap(p, "head", 1).astype(F32) for p in parts)

    middle = layer_input + (both_cores(attn) + proj_bias)
    xhat2, inv2 = normalize(middle)
    normed_mid = (xhat2 * gains[1] + ln2_shift).astype(BF16)

    mlp, dmid_parts, fc1_local, fc2_local, fc1_bias_grads = 0.0, 0.0, [], [], []
    for group, fc1, fc2 in zip(groups, full_fc1, full_fc2):
        pre_act = jnp.dot(normed_mid, fc1, preferred_element_type=F32) + bias_of(
            4 * model_width + 2 * all_cols, hidden_cols, group
        )
        hidden = jax.nn.gelu(pre_act, approximate=False).astype(BF16)
        mlp += jnp.einsum("tf,df->td", hidden, fc2, preferred_element_type=F32)
        dhidden = jnp.dot(grad_out, fc2, preferred_element_type=F32)
        gelu_pull = jax.vjp(partial(jax.nn.gelu, approximate=False), pre_act)[1]
        dpre = gelu_pull(dhidden)[0].astype(BF16)
        fc2_local.append(
            jnp.einsum("td,tf->df", grad_out, hidden, preferred_element_type=F32)
        )
        fc1_local.append(
            jnp.einsum("td,tf->df", normed_mid, dpre, preferred_element_type=F32)
        )
        fc1_bias_grads.append(jnp.sum(dpre.astype(F32), axis=0))
        dmid_parts += jnp.einsum("tf,df->td", dpre, fc1, preferred_element_type=F32)

    mine, theirs = (
        lax.dynamic_slice_in_dim(mlp, start, row_share, 0)
        for start in (row_start, row_share - row_start)
    )
    output_rows = (
        lax.dynamic_slice_in_dim(middle, row_start, row_share, 0)
        + (mine + swap(theirs.astype(BF16), "head", 1).astype(F32))
        + fc2_bias
    )
    dmid = both_cores([dmid_parts.astype(BF16)])
    dmiddle = grad_out.astype(F32) + norm_back(dmid, xhat2, inv2, gains[1])
    dmiddle_low = dmiddle.astype(BF16)

    qkvp_local, dfirst_parts, query_grads, value_grads = [], 0.0, [], []
    for full, (query, keys, value, largest, summed, context) in zip(full_qkvp, saved):
        proj_local = jnp.einsum("td,tc->dc", dmiddle_low, context, preferred_element_type=F32)
        dcontext = heads(
            jnp.dot(dmiddle_low, full[:, 3 * head_cols :], preferred_element_type=F32).astype(BF16)
        )
        scores = jnp.einsum("qhc,khc->hqk", query, keys, preferred_element_type=F32) * scale_factor
        scores = jnp.where(visible(slot_kind), scores, MASKED)
        probs = jnp.exp(scores - largest) / summed
        dprob = jnp.einsum("qhc,khc->hqk", dcontext, value, preferred_element_type=F32)
        row_dot = jnp.sum(probs * dprob, axis=-1, keepdims=True)
        dscore = (probs * (dprob - row_dot)).astype(BF16)
        dquery = (
            jnp.einsum("hqk,khc->qhc", dscore, keys, preferred_element_type=F32) * scale_factor
        )
        dkey = jnp.einsum("hqk,qhc->khc", dscore, query, preferred_element_type=F32) * scale_factor
        dvalue = jnp.einsum(
            "hqk,qhc->khc", probs.astype(BF16), dcontext, preferred_element_type=F32
        )
        dqkv = jnp.concatenate(
            [g.astype(BF16).reshape(SLOT_PATCHES, head_cols) for g in (dquery, dkey, dvalue)],
            axis=1,
        )
        qkv_local = jnp.einsum("td,tc->dc", normed, dqkv, preferred_element_type=F32)
        query_grads.append(jnp.sum(dqkv[:, :head_cols].astype(F32), axis=0))
        value_grads.append(jnp.sum(dqkv[:, 2 * head_cols :].astype(F32), axis=0))
        dfirst_parts += jnp.einsum(
            "tc,dc->td", dqkv, full[:, : 3 * head_cols], preferred_element_type=F32
        )
        qkvp_local.append(jnp.concatenate([qkv_local, proj_local], axis=1))

    mine, theirs = (
        lax.dynamic_slice_in_dim(dfirst_parts, start, row_share, 0)
        for start in (row_start, row_share - row_start)
    )
    dfirst = mine + swap(theirs.astype(BF16), "head", 1).astype(F32)
    xhat1_rows, inv1_rows, dmiddle_rows = (
        lax.dynamic_slice_in_dim(v, row_start, row_share, 0) for v in (xhat1, inv1, dmiddle)
    )
    input_grad = dmiddle_rows + norm_back(dfirst, xhat1_rows, inv1_rows, gains[0])

    fc2_grad = scatter(*fc2_local, count, me).T
    fc1_grad = scatter(*fc1_local, count, me)
    qkvp_grad = scatter(*qkvp_local, count, me)
    qkv_grad = qkvp_grad[:, : 3 * head_cols].reshape(w_qkv.shape)
    proj_grad = qkvp_grad[:, 3 * head_cols :].T

    once = jnp.where(core == 0, 1.0, 0.0)
    head_part = jnp.zeros((2 * all_cols + members * hidden_cols,), F32)
    for group, of_query, of_value, of_fc1 in zip(groups, query_grads, value_grads, fc1_bias_grads):
        head_part = lax.dynamic_update_slice_in_dim(head_part, of_query, group * head_cols, 0)
        head_part = lax.dynamic_update_slice_in_dim(
            head_part, of_value, all_cols + group * head_cols, 0
        )
        head_part = lax.dynamic_update_slice_in_dim(
            head_part, of_fc1, 2 * all_cols + group * hidden_cols, 0
        )
    small = jnp.concatenate(
        [
            jnp.sum(dfirst * xhat1_rows, axis=0),
            once * jnp.sum(dmid * xhat2, axis=0),
            jnp.sum(dfirst, axis=0),
            once * jnp.sum(dmid, axis=0),
            once * jnp.sum(dmiddle, axis=0),
            jnp.sum(cotangent.astype(F32), axis=0),
            head_part,
        ]
    )
    for mask in (1, 2):
        small = small + swap(small, "head", mask)
    for mask in [1] + line_masks(count):
        small = small + swap(small, "dp", mask)
    gain_grad = small[: 2 * model_width].reshape(gains.shape)
    bias_grad = small[2 * model_width :]

    qkv_mom, qkv_new, qkv_avg = update(w_qkv, qkv_grad, mom_qkv, avg_qkv, RATE_QKV, WEIGHT_DECAY)
    proj_mom, proj_new, proj_avg = update(
        w_proj, proj_grad, mom_proj, avg_proj, RATE_PROJ, WEIGHT_DECAY
    )
    fc1_mom, fc1_new, fc1_avg = update(w_fc1, fc1_grad, mom_fc1, avg_fc1, RATE_FC1, WEIGHT_DECAY)
    fc2_mom, fc2_new, fc2_avg = update(w_fc2, fc2_grad, mom_fc2, avg_fc2, RATE_FC2, WEIGHT_DECAY)
    gain_mom_new, gain_new, gain_avg_new = update(
        gains, gain_grad, gain_mom, gain_avg, RATE_SMALL, 0.0
    )
    bias_mom_new, bias_new, bias_avg_new = update(
        biases, bias_grad, bias_mom, bias_avg, RATE_SMALL, 0.0
    )
    return (
        output_rows.astype(BF16),
        input_grad,
        qkv_grad,
        qkv_mom,
        qkv_new,
        qkv_avg,
        proj_grad,
        proj_mom,
        proj_new,
        proj_avg,
        fc1_grad,
        fc1_mom,
        fc1_new,
        fc1_avg,
        fc2_grad,
        fc2_mom,
        fc2_new,
        fc2_avg,
        gain_grad,
        gain_mom_new,
        gain_new,
        gain_avg_new,
        bias_grad,
        bias_mom_new,
        bias_new,
        bias_avg_new,
    )
def solution(mesh):
    return jax.shard_map(
        shards,
        mesh=mesh,
        in_specs=(
            P("dp", None),
            P("dp"),
            P(("dp", "head"), None),
            P("dp", None, "head"),
            P("head", "dp"),
            P("dp", "head"),
            P("head", "dp"),
            P("dp", None, "head"),
            P("head", "dp"),
            P("dp", "head"),
            P("head", "dp"),
            P("dp", None, "head"),
            P("head", "dp"),
            P("dp", "head"),
            P("head", "dp"),
            P(),
            P(),
            P(),
            P(),
            P(),
            P(),
        ),
        out_specs=(
            P(("dp", "head"), None),
            P(("dp", "head"), None),
            P("dp", None, "head"),
            P("dp", None, "head"),
            P("dp", None, "head"),
            P("dp", None, "head"),
            P("head", "dp"),
            P("head", "dp"),
            P("head", "dp"),
            P("head", "dp"),
            P("dp", "head"),
            P("dp", "head"),
            P("dp", "head"),
            P("dp", "head"),
            P("head", "dp"),
            P("head", "dp"),
            P("head", "dp"),
            P("head", "dp"),
            P(),
            P(),
            P(),
            P(),
            P(),
            P(),
            P(),
            P(),
        ),
        check_vma=False,
    )
```

```python
import jax
import jax.numpy as jnp
from jax import lax
from jax.experimental import pallas as pl
from jax.experimental.pallas import tpu as pltpu
from jax.sharding import PartitionSpec as P

HEAD_WIDTH = 64
SLOT_PATCHES = 784
LOWRES = 196


EPSILON = 1e-06
MOMENTUM_RATE = 0.9
AVERAGING = 0.75
WEIGHT_DECAY = 0.05
RATE_QKV = 0.001
RATE_PROJ = 0.01
RATE_FC1 = 0.0006
RATE_FC2 = 0.0003
RATE_SMALL = 0.003
MASKED = -1e30
SCALE = HEAD_WIDTH**-0.5
F32 = jnp.float32
BF16 = jnp.bfloat16
QUERY_ROWS = SLOT_PATCHES // 2
VMEM_LIMIT = 44 << 20
ME, CORE, KIND, SLOT, MEMBER = range(5)

IN_VMEM = pl.BlockSpec(memory_space=pltpu.VMEM)
IN_SMEM = pl.BlockSpec(memory_space=pltpu.SMEM)
ANYWHERE = pl.BlockSpec(memory_space=pl.ANY)


def update(weight, gradient, moment, average, step_rate, decay_rate):
    step_grad = gradient + decay_rate * weight
    moment_new = MOMENTUM_RATE * moment + step_grad
    weight_new = weight - step_rate * (step_grad + MOMENTUM_RATE * moment_new)
    return (moment_new, weight_new, AVERAGING * average + (1.0 - AVERAGING) * weight_new)


def swap(value, axis, mask):
    return lax.ppermute(value, axis, [(i, i ^ mask) for i in range(lax.axis_size(axis))])


def line_masks(count):
    masks, mask = [], count // 2
    while mask > 1:
        masks.append(mask)
        mask //= 2
    return masks


def line_order(count):
    order = [0]
    for mask in line_masks(count):
        order = order + [r ^ mask for r in order]
    return order


def halves(count):
    order = line_order(count)
    cut = len(order) // 2
    return order[:cut], order[cut:]


def flip(order):
    return [r ^ 1 for r in order]


def gather(shard, count):
    near, far = halves(count)
    first = shard[None]
    masks = line_masks(count)
    for mask in masks[:-1]:
        first = jnp.concatenate([first, swap(first, "dp", mask)])
    second = swap(first, "dp", masks[-1])
    x_first, y_first = swap(first, "head", 2), swap(first, "dp", 1)
    x_second, y_second = swap(second, "head", 2), swap(second, "dp", 1)
    xy_first, xy_second = swap(y_first, "head", 2), swap(x_second, "dp", 1)
    rels = (near, far, flip(near), flip(far))
    own = (first, second, y_first, y_second)
    other = (x_first, x_second, xy_first, xy_second)
    return tuple(zip(own, rels)), tuple(zip(other, rels))


def joined(pieces, count, me):
    order = [r for _, rel in pieces for r in rel]
    place = jnp.array([order.index(r) for r in range(count)], jnp.int32)
    return jnp.concatenate([a for a, _ in pieces])[place[jnp.arange(count, dtype=jnp.int32) ^ me]]


def parted(whole, count, me):
    near, far = halves(count)
    return tuple(
        whole[jnp.array(rel, jnp.int32) ^ me] for rel in (near + flip(near), far, flip(far))
    )


def plus(*terms):
    return sum(t.astype(F32) for t in terms)


def scatter(own, other, count):
    (a_own, b_own, b_own_y), (a_other, b_other, b_other_y) = own, other
    cut = a_own.shape[0] // 2
    over_x = swap(a_other, "head", 2)
    over_y, over_y_other = swap(b_own_y, "dp", 1), swap(b_other_y, "dp", 1)
    a_next = swap(plus(a_own[cut:], over_x[cut:]).astype(BF16), "dp", 1)
    b_next = swap(plus(b_other, over_y_other).astype(BF16), "head", 2)
    b_sum = plus(b_own, over_y, b_next).astype(BF16)
    masks = line_masks(count)
    total = plus(a_own[:cut], over_x[:cut], a_next, swap(b_sum, "dp", masks[-1]))
    for mask in reversed(masks[:-1]):
        keep = total.shape[0] // 2
        total = total[:keep] + swap(total[keep:].astype(BF16), "dp", mask)
    return total[0]


def dot(a, b):
    return jnp.dot(a, b, preferred_element_type=F32)


def dot_t(a, b):
    return lax.dot_general(a, b, (((1,), (1,)), ((), ())), preferred_element_type=F32)


def t_dot(a, b):
    return lax.dot_general(a, b, (((0,), (0,)), ((), ())), preferred_element_type=F32)


def normalize(inputs):
    mean_row = jnp.mean(inputs, axis=-1, keepdims=True)
    centred = inputs - mean_row
    spread = jnp.mean(centred * centred, axis=-1, keepdims=True)
    inv_std = lax.rsqrt(spread + EPSILON)
    return (centred * inv_std, inv_std)


def norm_back(grad_out, centred, inv_std, gain_row):
    scaled = grad_out * gain_row
    return inv_std * (
        scaled
        - jnp.mean(scaled, axis=-1, keepdims=True)
        - centred * jnp.mean(scaled * centred, axis=-1, keepdims=True)
    )


def piece_copies(info, refs, rels, dest, sems, out=False, at=()):
    copies = []
    for ref, rel in zip(refs, rels):
        for j, r in enumerate(rel):
            rows = ref.shape[-2]
            start = 0 if r is None else pl.multiple_of((info[ME] ^ r) * rows, rows)
            there, here = ref.at[(j, *at)], dest.at[pl.ds(start, rows)]
            copies.append((here, there) if out else (there, here))
    copies = [
        pltpu.make_async_copy(a, b, sems.at[i]) for i, (a, b) in enumerate(copies)
    ]
    for copy in copies:
        copy.start()
    return copies


def wait_all(copies):
    for copy in copies:
        copy.wait()


def lanes():
    return lax.broadcasted_iota(jnp.int32, (1, 2 * HEAD_WIDTH), 1)


def segments(shape, axis, start, info):
    run = (lax.broadcasted_iota(jnp.int32, shape, axis) + start) // LOWRES
    return jnp.where(info[KIND] > 0, 0, run)


def column_sum(rows):
    return jnp.sum(rows, axis=0, keepdims=True)


def prepare_kernel(info, block, mine, peer, gains, biases, a1, a1_t, dy, dy_t, x_rows, rows):
    share = mine.shape[0]
    start = pl.multiple_of(info[CORE] * share, 8)
    x = block[...].astype(F32)
    rows[...] = x
    x_rows[...] = rows[pl.ds(start, share), :]
    xhat, _ = normalize(x)
    normed = xhat * gains[0:1, :] + biases[0:1, :]
    a1[...] = normed.astype(BF16)
    a1_t[...] = normed.astype(BF16).T
    rows[pl.ds(start, share), :] = mine[...].astype(F32)
    rows[pl.ds(pl.multiple_of(share - start, 8), share), :] = peer[...].astype(F32)
    low = rows[...].astype(BF16)
    dy[...] = low
    dy_t[...] = low.T


def attend_kernel(info, a1, bias, *rest, rels):
    count = len(rels)
    pieces, (qkv, out, lse, proj, w, sems) = rest[:count], rest[count:]
    wait_all(piece_copies(info, pieces, rels, w, sems))
    lane = lanes()
    low = lane < HEAD_WIDTH
    zero = jnp.zeros((), BF16)
    m = dot(a1[...], w[:, :640]) + bias[...]
    k01, v01 = m[:, 128:256].astype(BF16), m[:, 256:384].astype(BF16)
    pair = m[:, 384:512]
    k2 = pltpu.roll(pair, HEAD_WIDTH, 1).astype(BF16)
    v2 = m[:, 512:640].astype(BF16)
    qkv[:, 0:128] = (m[:, 0:128] * SCALE).astype(BF16)
    qkv[:, 128:256] = k01
    qkv[:, 256:384] = v01
    qkv[:, 384:512] = jnp.where(low, pair * SCALE, 0.0).astype(BF16)
    qkv[:, 512:640] = k2
    qkv[:, 640:768] = v2
    columns = segments((1, SLOT_PATCHES), 1, 0, info)
    for start in range(0, SLOT_PATCHES, QUERY_ROWS):
        rows = slice(start, start + QUERY_ROWS)
        seen = segments((QUERY_ROWS, 1), 0, start, info) == columns
        q01 = qkv[rows, 0:128]
        outs, logs = [], []
        for query, keys, value in (
            (jnp.where(low, q01, zero), k01, v01),
            (jnp.where(low, zero, q01), k01, v01),
            (qkv[rows, 384:512], k2, v2),
        ):
            scores = jnp.where(seen, dot_t(query, keys), MASKED)
            largest = jnp.max(scores, axis=-1, keepdims=True)
            expon = jnp.exp(scores - largest)
            summed = jnp.sum(expon, axis=-1, keepdims=True)
            probs = (expon * (1.0 / summed)).astype(BF16)
            outs.append(dot(probs, value))
            logs.append(largest + jnp.log(summed))
        third = jnp.where(low, 0.0, pltpu.roll(outs[2], HEAD_WIDTH, 1))
        out[rows, 0:128] = third.astype(BF16)
        out[rows, 128:256] = jnp.where(low, outs[0], outs[1]).astype(BF16)
        lse[rows, :] = jnp.where(lane == 0, logs[0], jnp.where(lane == 1, logs[1], logs[2]))
    proj[...] = dot_t(out[...], w[:, 512:768]).astype(BF16)


def middle_kernel(info, block, own, other, peer_own, peer_other, gains, biases, h1, a2, a2_t):
    both = plus(own[...], other[...]) + plus(peer_own[...], peer_other[...])
    middle = block[...].astype(F32) + (both + biases[2:3, :])
    h1[...] = middle
    xhat, _ = normalize(middle)
    normed = (xhat * gains[1:2, :] + biases[1:2, :]).astype(BF16)
    a2[...] = normed
    a2_t[...] = normed.T


def split_rows(info, total, scratch, keep, send):
    share = keep.shape[0]
    start = pl.multiple_of(info[CORE] * share, 8)
    scratch[...] = total
    keep[...] = scratch[pl.ds(start, share), :].astype(keep.dtype)
    send[...] = scratch[pl.ds(pl.multiple_of(share - start, 8), share), :].astype(send.dtype)


def mlp_kernel(info, a2, a2_t, dy, dy_t, biases, order, *rest, rels, out_rels, group_mask):
    count, outs = len(rels), len(out_rels)
    pieces, rest = rest[:count], rest[count:]
    parts, (keep, send, da2, dbias, w1, w2, dw1, dw2, rows, sems) = rest[:outs], rest[outs:]
    first = piece_copies(info, pieces, rels, w1, sems.at[0], at=(0,))
    second = piece_copies(info, pieces, rels, w2, sems.at[1], at=(1,))
    wait_all(first)
    bias = biases[pl.ds(6 + (info[MEMBER] ^ group_mask), 1), :]
    u = dot(a2[...], w1[...]) + bias
    phi = 0.5 + 0.5 * lax.erf(u * (2.0**-0.5))
    hidden = (u * phi).astype(BF16)
    slope = phi + u * (jnp.exp(-0.5 * u * u) * 0.3989422804014327)
    wait_all(second)
    dpre = (dot(dy[...], w2[...]) * slope).astype(BF16)
    dw2[...] = dot(dy_t[...], hidden).astype(BF16)
    second = piece_copies(info, parts, out_rels, dw2, sems.at[1], out=True, at=(1,))
    dw1[...] = dot(a2_t[...], dpre).astype(BF16)
    first = piece_copies(info, parts, out_rels, dw1, sems.at[0], out=True, at=(0,))
    da2[...] = dot_t(dpre, w1[...]).astype(BF16)
    split_rows(info, dot_t(hidden, w2[...]), rows, keep, send)
    dbias[...] = column_sum(dpre.astype(F32))
    wait_all(first)
    wait_all(second)


def middle_back_kernel(
    info, h1, dy, own, other, peer_own, peer_other, f0, f1, f2, f3, gains, biases, order,
    e, e_t, dh1_rows, block_out, sums, rows,
):
    share = block_out.shape[0]
    start = pl.multiple_of(info[CORE] * share, 8)
    xhat, inv_std = normalize(h1[...])
    da2 = plus(own[...], other[...]) + plus(peer_own[...], peer_other[...])
    dh1 = dy[...].astype(F32) + norm_back(da2, xhat, inv_std, gains[1:2, :])
    low = dh1.astype(BF16)
    e[...] = low
    e_t[...] = low.T
    rows[...] = dh1
    dh1_rows[...] = rows[pl.ds(start, share), :]
    sums[0:1, :] = column_sum(da2 * xhat)
    sums[1:2, :] = column_sum(da2)
    sums[2:3, :] = column_sum(dh1)
    mlp = plus(f0[...], f1[...]) + plus(f2[...], f3[...])
    block_out[...] = ((h1[pl.ds(start, share), :] + mlp) + biases[3:4, :]).astype(BF16)


def attend_back_kernel(info, e, e_t, a1_t, qkv, out, lse, order, *rest, rels, out_rels):
    count, outs = len(rels), len(out_rels)
    pieces, rest = rest[:count], rest[count:]
    parts, (keep, send, sums, w, dw, grads, rows, sems) = rest[:outs], rest[outs:]
    wait_all(piece_copies(info, pieces, rels, w, sems))
    low = lanes() < HEAD_WIDTH
    zero = jnp.zeros((), BF16)
    dout = dot(e[...], w[:, 512:768])
    do2 = jnp.where(low, pltpu.roll(dout[:, 0:128], HEAD_WIDTH, 1), 0.0).astype(BF16)
    do01 = dout[:, 128:256].astype(BF16)
    q01, k01, v01 = qkv[:, 0:128], qkv[:, 128:256], qkv[:, 256:384]
    q2, k2, v2 = qkv[:, 384:512], qkv[:, 512:640], qkv[:, 640:768]
    lse_t = jnp.transpose(lse[...], (1, 0))
    seen = segments((SLOT_PATCHES, 1), 0, 0, info) == segments((1, SLOT_PATCHES), 1, 0, info)
    dq, dk, dv = [], [], []
    for head, (query, keys, value, dcontext) in enumerate(
        (
            (q01, jnp.where(low, k01, zero), jnp.where(low, v01, zero), do01),
            (q01, jnp.where(low, zero, k01), jnp.where(low, zero, v01), do01),
            (q2, k2, jnp.where(low, v2, zero), do2),
        )
    ):
        scores = jnp.where(seen, dot_t(keys, query), MASKED)
        probs = jnp.exp(scores - lse_t[head : head + 1, :])
        dprob = dot_t(value, dcontext)
        row_dot = column_sum(probs * dprob)
        dscore = (probs * (dprob - row_dot)).astype(BF16)
        dv.append(dot(probs.astype(BF16), dcontext))
        dk.append(dot(dscore, query))
        dq.append(t_dot(dscore, keys))
    grads[:, 0:128] = (jnp.where(low, dq[0], dq[1]) * SCALE).astype(BF16)
    grads[:, 128:256] = jnp.where(low, dk[0], dk[1]).astype(BF16)
    grads[:, 256:384] = jnp.where(low, dv[0], dv[1]).astype(BF16)
    shifted = pltpu.roll(dk[2], HEAD_WIDTH, 1)
    grads[:, 384:512] = jnp.where(low, dq[2] * SCALE, shifted).astype(BF16)
    grads[:, 512:640] = jnp.where(low, dv[2], 0.0).astype(BF16)
    dw[:, 0:512] = dot(a1_t[...], grads[:, 0:512]).astype(BF16)
    dw[:, 512:640] = (dot(a1_t[...], grads[:, 512:640]) + dot(e_t[...], out[:, 0:128])).astype(BF16)
    dw[:, 640:768] = dot(e_t[...], out[:, 128:256]).astype(BF16)
    copies = piece_copies(info, parts, out_rels, dw, sems, out=True)
    split_rows(info, dot_t(grads[...], w[:, 0:640]), rows, keep, send)
    sums[...] = column_sum(grads[...].astype(F32))
    wait_all(copies)


def last_kernel(
    info, x_rows, dh1_rows, mine, k0, k1, r0, r1, gains, mid, db0, db1, s0, s1, input_grad, small
):
    xhat, inv_std = normalize(x_rows[...])
    da1 = plus(k0[...], k1[...]) + plus(r0[...], r1[...])
    input_grad[...] = dh1_rows[...] + norm_back(da1, xhat, inv_std, gains[0:1, :])
    once = jnp.where(info[CORE] == 0, 1.0, 0.0)
    member = info[MEMBER]
    small[...] = jnp.zeros_like(small)
    small[0:1, :] = column_sum(da1 * xhat)
    small[1:2, :] = once * mid[0:1, :]
    small[2:3, :] = column_sum(da1)
    small[3:4, :] = once * mid[1:2, :]
    small[4:5, :] = once * mid[2:3, :]
    small[5:6, :] = column_sum(mine[...].astype(F32))
    low = lanes() < HEAD_WIDTH
    for row, pair, single in ((6, 0, 384), (7, 256, 512)):
        for group in range(0, 4, 2):
            even, odd = (
                tuple(
                    jnp.where(
                        member == which,
                        s0[:, at : at + 128],
                        jnp.where(member == which ^ 2, s1[:, at : at + 128], 0.0),
                    )
                    for at in (pair, single)
                )
                for which in (group, group + 1)
            )
            turned = pltpu.roll(odd[0], HEAD_WIDTH, 1)
            at = group * 192
            small[row : row + 1, at : at + 128] = even[0]
            small[row : row + 1, at + 128 : at + 256] = jnp.where(low, even[1], turned)
            small[row : row + 1, at + 256 : at + 384] = jnp.where(
                low, turned, pltpu.roll(odd[1], HEAD_WIDTH, 1)
            )
    small[pl.ds(8 + member, 1), :] = db0[...]
    small[pl.ds(8 + (member ^ 2), 1), :] = db1[...]


def call(kernel, name, outs, inputs, specs=None, scratch=(), flops=0, **fixed):
    results = [jax.ShapeDtypeStruct(s, d) for s, d, *_ in outs]
    out_specs = [ANYWHERE if rest else IN_VMEM for _, _, *rest in outs]
    specs = specs or {}
    size = sum(v.size * v.dtype.itemsize for v in (*inputs, *results))

    def body(*refs):
        kernel(*refs, **fixed)

    body.__name__ = name
    return pl.pallas_call(
        body,
        out_shape=results,
        grid_spec=pltpu.PrefetchScalarGridSpec(
            num_scalar_prefetch=1,
            grid=(1,),
            in_specs=[specs.get(i, IN_VMEM) for i in range(1, len(inputs))],
            out_specs=out_specs,
            scratch_shapes=list(scratch),
        ),
        compiler_params=pltpu.CompilerParams(vmem_limit_bytes=VMEM_LIMIT),
        cost_estimate=pl.CostEstimate(flops=flops, bytes_accessed=size, transcendentals=0),
        name=name,
    )(*inputs)


def shards(
    block_in,
    resolution,
    cotangent,
    w_qkv,
    w_proj,
    w_fc1,
    w_fc2,
    mom_qkv,
    mom_proj,
    mom_fc1,
    mom_fc2,
    avg_qkv,
    avg_proj,
    avg_fc1,
    avg_fc2,
    gains,
    gain_mom,
    gain_avg,
    biases,
    bias_mom,
    bias_avg,
):
    members = lax.axis_size("head")
    count = lax.axis_size("dp")
    member = lax.axis_index("head")
    me = lax.axis_index("dp")
    slot = member // 2
    core = member % 2
    width = block_in.shape[1]
    head_cols = w_qkv.shape[2]
    hidden_cols = w_fc1.shape[1]
    share = cotangent.shape[0]
    shard_rows = w_qkv.shape[0]
    aligned = shard_rows % 16 == 0
    paired = 2 * HEAD_WIDTH
    kind = lax.dynamic_index_in_dim(resolution, slot, keepdims=False)
    info = jnp.stack([me, core, kind, slot, member]).astype(jnp.int32)

    low_qkv, low_proj = w_qkv.astype(BF16), w_proj.astype(BF16).T
    attn_shard = jnp.concatenate(
        [low_qkv[:, i, :paired] for i in range(3)]
        + [low_qkv[:, i, paired:] for i in range(3)]
        + [low_proj[:, paired:], low_proj[:, :paired]],
        axis=1,
    )
    mlp_shard = jnp.stack([w_fc1.astype(BF16), w_fc2.astype(BF16).T])
    attn_own, attn_other = gather(attn_shard, count)
    mlp_own, mlp_other = gather(mlp_shard, count)
    near, far = halves(count)
    out_rels = (near + flip(near), far, flip(far))
    out_pieces = [len(r) for r in out_rels]
    if not aligned:
        attn_own, attn_other = (
            ((joined(p, count, me).reshape(1, width, width), (None,)),) for p in (attn_own, attn_other)
        )
        mlp_own, mlp_other = (
            (
                (
                    jnp.swapaxes(joined(p, count, me), 0, 1).reshape(1, 2, width, width),
                    (None,),
                ),
            )
            for p in (mlp_own, mlp_other)
        )
        out_rels, out_pieces = ((None,),), [1]
    part_rows = shard_rows if aligned else width

    def parts(stacked, pieces):
        if aligned:
            return tuple(pieces)
        whole = pieces[0][0]
        if stacked:
            whole = jnp.swapaxes(whole.reshape(2, count, shard_rows, width), 0, 1)
        else:
            whole = whole.reshape(count, shard_rows, width)
        return parted(whole, count, me)

    bias_rows = biases.reshape(-1, width)
    q_bias, v_bias = (bias_rows[i].reshape(members, head_cols) for i in (4, 5))
    none = jnp.zeros_like(q_bias)
    group_bias = jnp.concatenate(
        [
            q_bias[:, :paired],
            none[:, :paired],
            v_bias[:, :paired],
            q_bias[:, paired:],
            none[:, paired:],
            v_bias[:, paired:],
            none[:, paired:],
        ],
        axis=1,
    )
    own_bias, other_bias = (
        lax.dynamic_slice_in_dim(group_bias, g, 1, 0) for g in (member, member ^ 2)
    )

    tall, turned = (SLOT_PATCHES, width), (width, SLOT_PATCHES)
    of_slot = pl.BlockSpec(tall, lambda i, info: (info[SLOT], 0))
    peer = swap(cotangent, "head", 1)
    a1, a1_t, dy, dy_t, x_rows = call(
        prepare_kernel,
        "prepare",
        [(tall, BF16), (turned, BF16), (tall, BF16), (turned, BF16), ((share, width), F32)],
        (info, block_in, cotangent, peer, gains, bias_rows),
        specs={1: of_slot},
        scratch=[pltpu.VMEM(tall, F32)],
    )

    def attend(pieces, bias):
        return call(
            attend_kernel,
            "attend",
            [
                (tall, BF16),
                ((SLOT_PATCHES, 2 * paired), BF16),
                ((SLOT_PATCHES, paired), F32),
                (tall, BF16),
            ],
            (info, a1, bias, *(a for a, _ in pieces)),
            specs={i: ANYWHERE for i in range(3, 3 + len(pieces))},
            scratch=[pltpu.VMEM((width, width), BF16), pltpu.SemaphoreType.DMA((count,))],
            flops=2 * SLOT_PATCHES * (width * width + 12 * SLOT_PATCHES * HEAD_WIDTH),
            rels=[r for _, r in pieces],
        )

    own_saved = attend(attn_own, own_bias)
    other_saved = attend(attn_other, other_bias)
    own_proj, other_proj = own_saved[3], other_saved[3]
    h1, a2, a2_t = call(
        middle_kernel,
        "middle",
        [(tall, F32), (tall, BF16), (turned, BF16)],
        (
            info,
            block_in,
            own_proj,
            other_proj,
            swap(own_proj, "head", 1),
            swap(other_proj, "head", 1),
            gains,
            bias_rows,
        ),
        specs={1: of_slot},
    )

    def mlp(pieces, group_mask, order):
        first = 7
        *grads, keep, send, da2, dbias = call(
            mlp_kernel,
            "mlp",
            [((n, 2, part_rows, width), BF16, ANYWHERE) for n in out_pieces]
            + [
                ((share, width), BF16),
                ((share, width), BF16),
                (tall, BF16),
                ((1, hidden_cols), F32),
            ],
            (info, a2, a2_t, dy, dy_t, bias_rows, order, *(a for a, _ in pieces)),
            specs={i: ANYWHERE for i in range(first - 1, first + len(pieces))},
            scratch=[pltpu.VMEM((width, hidden_cols), BF16) for _ in range(4)]
            + [pltpu.VMEM(tall, F32), pltpu.SemaphoreType.DMA((2, count))],
            flops=12 * SLOT_PATCHES * width * hidden_cols,
            rels=[r for _, r in pieces],
            out_rels=out_rels,
            group_mask=group_mask,
        )
        return parts(True, grads), keep, send, da2, dbias

    own_mlp = mlp(mlp_own, 0, gains)
    other_mlp = mlp(mlp_other, 2, own_mlp[4])
    mlp_grad = scatter(own_mlp[0], other_mlp[0], count)

    e, e_t, dh1_rows, block_out, mid_sums = call(
        middle_back_kernel,
        "middle_back",
        [
            (tall, BF16),
            (turned, BF16),
            ((share, width), F32),
            ((share, width), BF16),
            ((3, width), F32),
        ],
        (
            info,
            h1,
            dy,
            own_mlp[3],
            other_mlp[3],
            swap(own_mlp[3], "head", 1),
            swap(other_mlp[3], "head", 1),
            own_mlp[1],
            other_mlp[1],
            swap(own_mlp[2], "head", 1),
            swap(other_mlp[2], "head", 1),
            gains,
            bias_rows,
            gains,
        ),
        scratch=[pltpu.VMEM(tall, F32)],
    )

    def attend_back(pieces, saved, order):
        qkv, out, lse, _ = saved
        first = 8
        *grads, keep, send, sums = call(
            attend_back_kernel,
            "attend_back",
            [((n, part_rows, width), BF16, ANYWHERE) for n in out_pieces]
            + [((share, width), BF16), ((share, width), BF16), ((1, 5 * paired), F32)],
            (info, e, e_t, a1_t, qkv, out, lse, order, *(a for a, _ in pieces)),
            specs={i: ANYWHERE for i in range(first - 1, first + len(pieces))},
            scratch=[
                pltpu.VMEM((width, width), BF16),
                pltpu.VMEM((width, width), BF16),
                pltpu.VMEM((SLOT_PATCHES, 5 * paired), BF16),
                pltpu.VMEM(tall, F32),
                pltpu.SemaphoreType.DMA((count,)),
            ],
            flops=2 * SLOT_PATCHES * (2 * width * width + 60 * SLOT_PATCHES * HEAD_WIDTH),
            rels=[r for _, r in pieces],
            out_rels=out_rels,
        )
        return parts(False, grads), keep, send, sums

    other_back = attend_back(attn_other, other_saved, gains)
    own_back = attend_back(attn_own, own_saved, other_back[3])
    attn_grad = scatter(own_back[0], other_back[0], count)
    input_grad, small = call(
        last_kernel,
        "last",
        [((share, width), F32), ((12, width), F32)],
        (
            info,
            x_rows,
            dh1_rows,
            cotangent,
            own_back[1],
            other_back[1],
            swap(own_back[2], "head", 1),
            swap(other_back[2], "head", 1),
            gains,
            mid_sums,
            own_mlp[4],
            other_mlp[4],
            own_back[3],
            other_back[3],
        ),
    )
    for mask in (1, 2):
        small = small + swap(small, "head", mask)
    for mask in [1] + line_masks(count):
        small = small + swap(small, "dp", mask)
    gain_grad = small[:2]
    bias_grad = small[2:].reshape(biases.shape)

    fc1_grad, fc2_grad = mlp_grad[0], mlp_grad[1].T
    qkv_grad = jnp.stack(
        [
            jnp.concatenate(
                [
                    attn_grad[:, i * paired : (i + 1) * paired],
                    attn_grad[:, 3 * paired + i * HEAD_WIDTH : 3 * paired + (i + 1) * HEAD_WIDTH],
                ],
                axis=1,
            )
            for i in range(3)
        ],
        axis=1,
    )
    proj_grad = jnp.concatenate(
        [attn_grad[:, 5 * paired :], attn_grad[:, 5 * paired - HEAD_WIDTH : 5 * paired]], axis=1
    ).T

    qkv_mom, qkv_new, qkv_avg = update(w_qkv, qkv_grad, mom_qkv, avg_qkv, RATE_QKV, WEIGHT_DECAY)
    proj_mom, proj_new, proj_avg = update(
        w_proj, proj_grad, mom_proj, avg_proj, RATE_PROJ, WEIGHT_DECAY
    )
    fc1_mom, fc1_new, fc1_avg = update(w_fc1, fc1_grad, mom_fc1, avg_fc1, RATE_FC1, WEIGHT_DECAY)
    fc2_mom, fc2_new, fc2_avg = update(w_fc2, fc2_grad, mom_fc2, avg_fc2, RATE_FC2, WEIGHT_DECAY)
    gain_mom_new, gain_new, gain_avg_new = update(
        gains, gain_grad, gain_mom, gain_avg, RATE_SMALL, 0.0
    )
    bias_mom_new, bias_new, bias_avg_new = update(
        biases, bias_grad, bias_mom, bias_avg, RATE_SMALL, 0.0
    )
    return (
        block_out,
        input_grad,
        qkv_grad,
        qkv_mom,
        qkv_new,
        qkv_avg,
        proj_grad,
        proj_mom,
        proj_new,
        proj_avg,
        fc1_grad,
        fc1_mom,
        fc1_new,
        fc1_avg,
        fc2_grad,
        fc2_mom,
        fc2_new,
        fc2_avg,
        gain_grad,
        gain_mom_new,
        gain_new,
        gain_avg_new,
        bias_grad,
        bias_mom_new,
        bias_new,
        bias_avg_new,
    )
def solution(mesh):
    return jax.shard_map(
        shards,
        mesh=mesh,
        in_specs=(
            P("dp", None),
            P("dp"),
            P(("dp", "head"), None),
            P("dp", None, "head"),
            P("head", "dp"),
            P("dp", "head"),
            P("head", "dp"),
            P("dp", None, "head"),
            P("head", "dp"),
            P("dp", "head"),
            P("head", "dp"),
            P("dp", None, "head"),
            P("head", "dp"),
            P("dp", "head"),
            P("head", "dp"),
            P(),
            P(),
            P(),
            P(),
            P(),
            P(),
        ),
        out_specs=(
            P(("dp", "head"), None),
            P(("dp", "head"), None),
            P("dp", None, "head"),
            P("dp", None, "head"),
            P("dp", None, "head"),
            P("dp", None, "head"),
            P("head", "dp"),
            P("head", "dp"),
            P("head", "dp"),
            P("head", "dp"),
            P("dp", "head"),
            P("dp", "head"),
            P("dp", "head"),
            P("dp", "head"),
            P("head", "dp"),
            P("head", "dp"),
            P("head", "dp"),
            P("head", "dp"),
            P(),
            P(),
            P(),
            P(),
            P(),
            P(),
            P(),
            P(),
        ),
        check_vma=False,
    )
```

```python
import jax
import jax.numpy as jnp
from jax import lax
from jax.experimental import pallas as pl
from jax.experimental.pallas import tpu as pltpu
from jax.sharding import PartitionSpec as P

HEAD_WIDTH = 64
SLOT_PATCHES = 784
LOWRES = 196


EPSILON = 1e-06
MOMENTUM_RATE = 0.9
AVERAGING = 0.75
WEIGHT_DECAY = 0.05
RATE_QKV = 0.001
RATE_PROJ = 0.01
RATE_FC1 = 0.0006
RATE_FC2 = 0.0003
RATE_SMALL = 0.003
MASKED = -1e30
SCALE = HEAD_WIDTH**-0.5
F32 = jnp.float32
BF16 = jnp.bfloat16
QUERY_ROWS = SLOT_PATCHES // 2
VMEM_LIMIT = 60 << 20
COST = 16
ME, CORE, KIND, SLOT, MEMBER = range(5)

IN_VMEM = pl.BlockSpec(memory_space=pltpu.VMEM)
IN_SMEM = pl.BlockSpec(memory_space=pltpu.SMEM)
ANYWHERE = pl.BlockSpec(memory_space=pl.ANY)


def update(weight, gradient, moment, average, step_rate, decay_rate):
    step_grad = gradient + decay_rate * weight
    moment_new = MOMENTUM_RATE * moment + step_grad
    weight_new = weight - step_rate * (step_grad + MOMENTUM_RATE * moment_new)
    return (moment_new, weight_new, AVERAGING * average + (1.0 - AVERAGING) * weight_new)


def swap(value, axis, mask):
    return lax.ppermute(value, axis, [(i, i ^ mask) for i in range(lax.axis_size(axis))])


def line_masks(count):
    masks, mask = [], count // 2
    while mask > 1:
        masks.append(mask)
        mask //= 2
    return masks


def line_order(count):
    order = [0]
    for mask in line_masks(count):
        order = order + [r ^ mask for r in order]
    return order


def z_sets(count):
    order = line_order(count)
    eighth = count // 8
    return order[:eighth], order[eighth : 2 * eighth], order[2 * eighth :]


def flip(order):
    return [r ^ 1 for r in order]


def after(value, *others):
    return lax.optimization_barrier((value, *others))[0]


def both_after(values, *others):
    return lax.optimization_barrier((*values, *others))[: len(values)]


def over_x(value):
    return swap(value, "head", 2)


def over_y(value):
    return swap(value, "dp", 1)


def plane_swap(value):
    members = lax.axis_size("head")
    total = members * lax.axis_size("dp")
    return lax.ppermute(value, ("dp", "head"), [(i, i ^ members ^ 2) for i in range(total)])


def over_z(value):
    return swap(value, "dp", 2)


def over_far(value, count):
    return swap(value, "dp", line_masks(count)[-2])


class Gather:
    def __init__(self, shard, count):
        base = shard[None]
        for mask in line_masks(count)[:-2]:
            base = jnp.concatenate([base, swap(base, "dp", mask)])
        self.base, self.count = base, count

    def far(self, *later):
        self.base = both_after((self.base,), *later)[0]
        self.first = jnp.concatenate([self.base, over_far(self.base, self.count)])

    def near(self, *later):
        self.first = both_after((self.first,), *later)[0]
        self.second = over_z(self.first)
        self.x_first, self.y_first = over_x(self.first), over_y(self.first)

    def turn(self, *later):
        cut = self.base.shape[0]
        x_first, y_first = both_after((self.x_first, self.y_first), *later)
        self.d_base, self.d_away = over_x(y_first[:cut]), over_y(x_first[cut:])

    def rest(self, *later):
        second = both_after((self.second,), *later)[0]
        self.x_second, self.y_second = over_x(second), over_y(second)

    def last(self, *later):
        base, away = both_after((self.d_base, self.d_away), *later)
        self.d_second = over_z(jnp.concatenate([base, away]))

    def pieces(self):
        base, away, near = z_sets(self.count)
        own = (
            (self.first, base + away),
            (self.second, near),
            (self.y_first, flip(base + away)),
            (self.y_second, flip(near)),
        )
        other = (
            (self.x_first, base + away),
            (self.x_second, near),
            (self.d_base, flip(base)),
            (self.d_away, flip(away)),
            (self.d_second, flip(near)),
        )
        return own, other


def joined(pieces, count, me):
    order = [r for _, rel in pieces for r in rel]
    place = jnp.array([order.index(r) for r in range(count)], jnp.int32)
    return jnp.concatenate([a for a, _ in pieces])[place[jnp.arange(count, dtype=jnp.int32) ^ me]]


def part_rels(count):
    base, away, near = z_sets(count)
    own = (base, away, near, flip(base), flip(away + near))
    other = (away, base + near, flip(base), flip(away), flip(near))
    return own, other


def parted(whole, rels, me):
    return tuple(whole[jnp.array(rel, jnp.int32) ^ me] for rel in rels)


def plus(*terms):
    return sum(t.astype(F32) for t in terms)


def low_plus(*terms):
    return plus(*terms).astype(BF16)


class Scatter:
    def __init__(self, count):
        self.count = count

    def own(self, parts, *later):
        self.base, self.away, self.near, self.y_base, y_rest = parts
        self.from_y = over_y(after(y_rest, *later))

    def other(self, parts, *later):
        self.x_away, x_rest, self.d_base, self.d_away, d_near = parts
        x_rest, d_near = both_after((x_rest, d_near), *later)
        self.from_d, self.from_x = over_z(d_near), over_x(x_rest)

    def turn(self, *later):
        cut = self.d_base.shape[0]
        self.d_base, self.d_away = both_after((self.d_base, self.d_away), *later)
        self.to_y = over_x(low_plus(self.d_base, self.from_d[:cut]))
        self.to_x = over_y(low_plus(self.d_away, self.from_d[cut:]))

    def near_sum(self, *later):
        cut = self.base.shape[0]
        near = both_after((self.near,), *later)[0]
        self.from_near = over_z(low_plus(near, self.from_y[cut:], self.from_x[cut:]))

    def last_xy(self, *later):
        self.y_base, self.x_away = both_after((self.y_base, self.x_away), *later)
        self.from_y_base = over_y(low_plus(self.y_base, self.to_y))
        self.from_x_away = over_x(low_plus(self.x_away, self.to_x))

    def far(self, *later):
        cut = self.base.shape[0]
        self.away = both_after((self.away,), *later)[0]
        away = low_plus(self.away, self.from_x_away, self.from_y[:cut], self.from_near[cut:])
        self.from_away = over_far(away, self.count)

    def terms(self):
        cut = self.base.shape[0]
        terms = (
            self.base, self.from_x[:cut], self.from_y_base, self.from_near[:cut], self.from_away
        )
        masks = line_masks(self.count)[:-2]
        if not masks:
            return terms
        total = plus(*terms)
        for mask in reversed(masks):
            keep = total.shape[0] // 2
            total = total[:keep] + swap(total[keep:].astype(BF16), "dp", mask)
        return (total[:1],)


def dot(a, b):
    return jnp.dot(a, b, preferred_element_type=F32)


def dot_t(a, b):
    return lax.dot_general(a, b, (((1,), (1,)), ((), ())), preferred_element_type=F32)


def t_dot(a, b):
    return lax.dot_general(a, b, (((0,), (0,)), ((), ())), preferred_element_type=F32)


def normalize(inputs):
    mean_row = jnp.mean(inputs, axis=-1, keepdims=True)
    centred = inputs - mean_row
    spread = jnp.mean(centred * centred, axis=-1, keepdims=True)
    inv_std = lax.rsqrt(spread + EPSILON)
    return (centred * inv_std, inv_std)


def norm_back(grad_out, centred, inv_std, gain_row):
    scaled = grad_out * gain_row
    return inv_std * (
        scaled
        - jnp.mean(scaled, axis=-1, keepdims=True)
        - centred * jnp.mean(scaled * centred, axis=-1, keepdims=True)
    )


def piece_copies(info, refs, rels, dest, sems, out=False, at=()):
    copies = []
    for ref, rel in zip(refs, rels):
        for j, r in enumerate(rel):
            rows = ref.shape[-2]
            start = 0 if r is None else pl.multiple_of((info[ME] ^ r) * rows, rows)
            there, here = ref.at[(j, *at)], dest.at[pl.ds(start, rows)]
            copies.append((here, there) if out else (there, here))
    copies = [
        pltpu.make_async_copy(a, b, sems.at[i]) for i, (a, b) in enumerate(copies)
    ]
    for copy in copies:
        copy.start()
    return copies


def wait_all(copies):
    for copy in copies:
        copy.wait()


def lanes():
    return lax.broadcasted_iota(jnp.int32, (1, 2 * HEAD_WIDTH), 1)


def segments(shape, axis, start, info):
    run = (lax.broadcasted_iota(jnp.int32, shape, axis) + start) // LOWRES
    return jnp.where(info[KIND] > 0, 0, run)


def column_sum(rows):
    return jnp.sum(rows, axis=0, keepdims=True)


def cast_kernel(w_qkv, w_proj, w_fc1, w_fc2, attn, mlp):
    wide = 2 * HEAD_WIDTH
    for i in range(3):
        attn[:, i * wide : (i + 1) * wide] = w_qkv[i, :, :wide].astype(BF16)
    single = [w_qkv[i, :, wide:] for i in range(3)]
    proj = w_proj[...].T
    attn[:, 3 * wide : 4 * wide] = jnp.concatenate(single[:2], axis=1).astype(BF16)
    attn[:, 4 * wide : 5 * wide] = jnp.concatenate([single[2], proj[:, wide:]], axis=1).astype(BF16)
    attn[:, 5 * wide : 6 * wide] = proj[:, :wide].astype(BF16)
    mlp[0] = w_fc1[...].astype(BF16)
    mlp[1] = w_fc2[...].astype(BF16)


def prepare_kernel(info, block, gains, biases, a1, a1_t, x_rows, rows):
    share = x_rows.shape[0]
    x = block[...].astype(F32)
    rows[...] = x
    x_rows[...] = rows[pl.ds(pl.multiple_of(info[CORE] * share, 8), share), :]
    xhat, _ = normalize(x)
    normed = (xhat * gains[0:1, :] + biases[0:1, :]).astype(BF16)
    a1[...] = normed
    a1_t[...] = normed.T


def join_kernel(info, mine, peer, dy, dy_t, rows):
    share = mine.shape[0]
    start = pl.multiple_of(info[CORE] * share, 8)
    rows[pl.ds(start, share), :] = mine[...].astype(F32)
    rows[pl.ds(pl.multiple_of(share - start, 8), share), :] = peer[...].astype(F32)
    low = rows[...].astype(BF16)
    dy[...] = low
    dy_t[...] = low.T


def attend_kernel(info, a1, bias, *rest, rels, added):
    before, rest = rest[:added], rest[added:]
    count = len(rels)
    pieces, (qkv, out, lse, proj, w, sems) = rest[:count], rest[count:]
    wait_all(piece_copies(info, pieces, rels, w, sems))
    lane = lanes()
    low = lane < HEAD_WIDTH
    zero = jnp.zeros((), BF16)
    m = dot(a1[...], w[:, :640]) + bias[...]
    k01, v01 = m[:, 128:256].astype(BF16), m[:, 256:384].astype(BF16)
    pair = m[:, 384:512]
    k2 = pltpu.roll(pair, HEAD_WIDTH, 1).astype(BF16)
    v2 = m[:, 512:640].astype(BF16)
    qkv[:, 0:128] = (m[:, 0:128] * SCALE).astype(BF16)
    qkv[:, 128:256] = k01
    qkv[:, 256:384] = v01
    qkv[:, 384:512] = jnp.where(low, pair * SCALE, 0.0).astype(BF16)
    qkv[:, 512:640] = k2
    qkv[:, 640:768] = v2
    columns = segments((1, SLOT_PATCHES), 1, 0, info)
    for start in range(0, SLOT_PATCHES, QUERY_ROWS):
        rows = slice(start, start + QUERY_ROWS)
        seen = segments((QUERY_ROWS, 1), 0, start, info) == columns
        q01 = qkv[rows, 0:128]
        outs, logs = [], []
        for query, keys, value in (
            (jnp.where(low, q01, zero), k01, v01),
            (jnp.where(low, zero, q01), k01, v01),
            (qkv[rows, 384:512], k2, v2),
        ):
            scores = jnp.where(seen, dot_t(query, keys), MASKED)
            largest = jnp.max(scores, axis=-1, keepdims=True)
            expon = jnp.exp(scores - largest)
            summed = jnp.sum(expon, axis=-1, keepdims=True)
            probs = (expon * (1.0 / summed)).astype(BF16)
            outs.append(dot(probs, value))
            logs.append(largest + jnp.log(summed))
        third = jnp.where(low, 0.0, pltpu.roll(outs[2], HEAD_WIDTH, 1))
        out[rows, 0:128] = third.astype(BF16)
        out[rows, 128:256] = jnp.where(low, outs[0], outs[1]).astype(BF16)
        lse[rows, :] = jnp.where(lane == 0, logs[0], jnp.where(lane == 1, logs[1], logs[2]))
    total = dot_t(out[...], w[:, 512:768])
    proj[...] = plus(total, *(b[...] for b in before)).astype(BF16)


def middle_kernel(info, block, mine, peer, gains, biases, h1, a2, a2_t):
    both = plus(mine[...], peer[...])
    middle = block[...].astype(F32) + (both + biases[2:3, :])
    h1[...] = middle
    xhat, _ = normalize(middle)
    normed = (xhat * gains[1:2, :] + biases[1:2, :]).astype(BF16)
    a2[...] = normed
    a2_t[...] = normed.T


def split_rows(info, total, scratch, keep, send, before, at=0):
    share = keep.shape[0]
    start = pl.multiple_of(info[CORE] * share, 8)
    scratch[...] = total
    kept = scratch[pl.ds(start, share), :]
    keep[...] = plus(kept, *(b[...] for b in before[:1])).astype(keep.dtype)
    theirs = scratch[pl.ds(pl.multiple_of(share - start, 8), share), :]
    sent = plus(theirs, *(b[at : at + share, :] for b in before[1:]))
    send[at : at + share, :] = sent.astype(send.dtype)


def mlp_kernel(info, a2, a2_t, dy, dy_t, biases, order, *rest, rels, out_rels, group_mask, added):
    before, rest = rest[:added], rest[added:]
    count, outs = len(rels), len(out_rels)
    pieces, rest = rest[:count], rest[count:]
    parts, (keep, send, dbias, w1, w2, dw1, dw2, rows, sems) = rest[:outs], rest[outs:]
    first = piece_copies(info, pieces, rels, w1, sems.at[0], at=(0,))
    second = piece_copies(info, pieces, rels, w2, sems.at[1], at=(1,))
    wait_all(first)
    bias = biases[pl.ds(6 + (info[MEMBER] ^ group_mask), 1), :]
    u = dot(a2[...], w1[...]) + bias
    phi = 0.5 + 0.5 * lax.erf(u * (2.0**-0.5))
    hidden = (u * phi).astype(BF16)
    slope = phi + u * (jnp.exp(-0.5 * u * u) * 0.3989422804014327)
    wait_all(second)
    dpre = (dot(dy[...], w2[...]) * slope).astype(BF16)
    dw2[...] = dot(dy_t[...], hidden).astype(BF16)
    second = piece_copies(info, parts, out_rels, dw2, sems.at[1], out=True, at=(1,))
    dw1[...] = dot(a2_t[...], dpre).astype(BF16)
    first = piece_copies(info, parts, out_rels, dw1, sems.at[0], out=True, at=(0,))
    da2 = plus(dot_t(dpre, w1[...]), *(b[:SLOT_PATCHES, :] for b in before[1:]))
    send[:SLOT_PATCHES, :] = da2.astype(BF16)
    split_rows(info, dot_t(hidden, w2[...]), rows, keep, send, before, SLOT_PATCHES)
    dbias[...] = column_sum(dpre.astype(F32))
    wait_all(first)
    wait_all(second)


def middle_back_kernel(
    info, h1, dy, mine, peer, kept, gains, biases, order,
    e, e_t, dh1_rows, block_out, sums, rows,
):
    share = block_out.shape[0]
    start = pl.multiple_of(info[CORE] * share, 8)
    xhat, inv_std = normalize(h1[...])
    da2 = plus(mine[:SLOT_PATCHES, :], peer[:SLOT_PATCHES, :])
    dh1 = dy[...].astype(F32) + norm_back(da2, xhat, inv_std, gains[1:2, :])
    low = dh1.astype(BF16)
    e[...] = low
    e_t[...] = low.T
    rows[...] = dh1
    dh1_rows[...] = rows[pl.ds(start, share), :]
    sums[0:1, :] = column_sum(da2 * xhat)
    sums[1:2, :] = column_sum(da2)
    sums[2:3, :] = column_sum(dh1)
    mlp = plus(kept[...], peer[SLOT_PATCHES:, :])
    block_out[...] = ((h1[pl.ds(start, share), :] + mlp) + biases[3:4, :]).astype(BF16)


def attend_back_kernel(info, e, e_t, a1_t, qkv, out, lse, order, *rest, rels, out_rels, added):
    before, rest = rest[:added], rest[added:]
    count, outs = len(rels), len(out_rels)
    pieces, rest = rest[:count], rest[count:]
    parts, (keep, send, sums, w, dw, grads, rows, sems) = rest[:outs], rest[outs:]
    wait_all(piece_copies(info, pieces, rels, w, sems))
    low = lanes() < HEAD_WIDTH
    zero = jnp.zeros((), BF16)
    dout = dot(e[...], w[:, 512:768])
    do2 = jnp.where(low, pltpu.roll(dout[:, 0:128], HEAD_WIDTH, 1), 0.0).astype(BF16)
    do01 = dout[:, 128:256].astype(BF16)
    q01, k01, v01 = qkv[:, 0:128], qkv[:, 128:256], qkv[:, 256:384]
    q2, k2, v2 = qkv[:, 384:512], qkv[:, 512:640], qkv[:, 640:768]
    lse_t = jnp.transpose(lse[...], (1, 0))
    seen = segments((SLOT_PATCHES, 1), 0, 0, info) == segments((1, SLOT_PATCHES), 1, 0, info)
    dq, dk, dv = [], [], []
    for head, (query, keys, value, dcontext) in enumerate(
        (
            (q01, jnp.where(low, k01, zero), jnp.where(low, v01, zero), do01),
            (q01, jnp.where(low, zero, k01), jnp.where(low, zero, v01), do01),
            (q2, k2, jnp.where(low, v2, zero), do2),
        )
    ):
        scores = jnp.where(seen, dot_t(keys, query), MASKED)
        probs = jnp.exp(scores - lse_t[head : head + 1, :])
        dprob = dot_t(value, dcontext)
        row_dot = column_sum(probs * dprob)
        dscore = (probs * (dprob - row_dot)).astype(BF16)
        dv.append(dot(probs.astype(BF16), dcontext))
        dk.append(dot(dscore, query))
        dq.append(t_dot(dscore, keys))
    grads[:, 0:128] = (jnp.where(low, dq[0], dq[1]) * SCALE).astype(BF16)
    grads[:, 128:256] = jnp.where(low, dk[0], dk[1]).astype(BF16)
    grads[:, 256:384] = jnp.where(low, dv[0], dv[1]).astype(BF16)
    shifted = pltpu.roll(dk[2], HEAD_WIDTH, 1)
    grads[:, 384:512] = jnp.where(low, dq[2] * SCALE, shifted).astype(BF16)
    grads[:, 512:640] = jnp.where(low, dv[2], 0.0).astype(BF16)
    dw[:, 0:512] = dot(a1_t[...], grads[:, 0:512]).astype(BF16)
    dw[:, 512:640] = (dot(a1_t[...], grads[:, 512:640]) + dot(e_t[...], out[:, 0:128])).astype(BF16)
    dw[:, 640:768] = dot(e_t[...], out[:, 128:256]).astype(BF16)
    copies = piece_copies(info, parts, out_rels, dw, sems, out=True)
    split_rows(info, dot_t(grads[...], w[:, 0:640]), rows, keep, send, before)
    sums[...] = column_sum(grads[...].astype(F32))
    wait_all(copies)


def last_kernel(
    info, x_rows, dh1_rows, mine, kept, peer, gains, mid, db0, db1, s0, s1, input_grad, small
):
    xhat, inv_std = normalize(x_rows[...])
    da1 = plus(kept[...], peer[...])
    input_grad[...] = dh1_rows[...] + norm_back(da1, xhat, inv_std, gains[0:1, :])
    once = jnp.where(info[CORE] == 0, 1.0, 0.0)
    member = info[MEMBER]
    small[...] = jnp.zeros_like(small)
    small[0:1, :] = column_sum(da1 * xhat)
    small[1:2, :] = once * mid[0:1, :]
    small[2:3, :] = column_sum(da1)
    small[3:4, :] = once * mid[1:2, :]
    small[4:5, :] = once * mid[2:3, :]
    small[5:6, :] = column_sum(mine[...].astype(F32))
    low = lanes() < HEAD_WIDTH
    for row, pair, single in ((6, 0, 384), (7, 256, 512)):
        for group in range(0, 4, 2):
            even, odd = (
                tuple(
                    jnp.where(
                        member == which,
                        s0[:, at : at + 128],
                        jnp.where(member == which ^ 2, s1[:, at : at + 128], 0.0),
                    )
                    for at in (pair, single)
                )
                for which in (group, group + 1)
            )
            turned = pltpu.roll(odd[0], HEAD_WIDTH, 1)
            at = group * 192
            small[row : row + 1, at : at + 128] = even[0]
            small[row : row + 1, at + 128 : at + 256] = jnp.where(low, even[1], turned)
            small[row : row + 1, at + 256 : at + 384] = jnp.where(
                low, turned, pltpu.roll(odd[1], HEAD_WIDTH, 1)
            )
    small[pl.ds(8 + member, 1), :] = db0[...]
    small[pl.ds(8 + (member ^ 2), 1), :] = db1[...]


def step(weight, gradient, moment, average, outs, rate):
    for ref, value in zip(
        outs, (gradient, *update(weight, gradient, moment, average, rate, WEIGHT_DECAY))
    ):
        ref[...] = value.reshape(ref.shape)


def finish_mlp_kernel(w1, m1, a1, w2, m2, a2, *rest):
    terms, outs = rest[:-8], rest[-8:]
    first, second = (plus(*(t[0, i] for t in terms)) for i in range(2))
    step(w1[...], first, m1[...], a1[...], outs[:4], RATE_FC1)
    step(w2[...], second, m2[...], a2[...], outs[4:], RATE_FC2)


def finish_attn_kernel(w1, m1, a1, w2, m2, a2, *rest):
    terms, outs = rest[:-8], rest[-8:]
    total = plus(*(t[0] for t in terms))
    wide = 2 * HEAD_WIDTH
    for i in range(3):
        single = 3 * wide + i * HEAD_WIDTH
        gradient = jnp.concatenate(
            [total[:, i * wide : (i + 1) * wide], total[:, single : single + HEAD_WIDTH]], axis=1
        )
        step(w1[i], gradient, m1[i], a1[i], [o.at[i] for o in outs[:4]], RATE_QKV)
    gradient = jnp.concatenate(
        [total[:, 5 * wide :], total[:, 5 * wide - HEAD_WIDTH : 5 * wide]], axis=1
    ).T
    step(w2[...], gradient, m2[...], a2[...], outs[4:], RATE_PROJ)


def call(kernel, name, outs, inputs, specs=None, scratch=(), flops=0, scalars=1, **fixed):
    results = [jax.ShapeDtypeStruct(s, d) for s, d, *_ in outs]
    out_specs = [ANYWHERE if rest else IN_VMEM for _, _, *rest in outs]
    specs = specs or {}
    size = sum(v.size * v.dtype.itemsize for v in (*inputs, *results))

    def body(*refs):
        kernel(*refs, **fixed)

    body.__name__ = name
    return pl.pallas_call(
        body,
        out_shape=results,
        grid_spec=pltpu.PrefetchScalarGridSpec(
            num_scalar_prefetch=scalars,
            grid=(1,),
            in_specs=[specs.get(i, IN_VMEM) for i in range(scalars, len(inputs))],
            out_specs=out_specs,
            scratch_shapes=list(scratch),
        ),
        compiler_params=pltpu.CompilerParams(vmem_limit_bytes=VMEM_LIMIT),
        cost_estimate=pl.CostEstimate(flops=flops // COST, bytes_accessed=size // COST, transcendentals=0),
        name=name,
    )(*inputs)


def shards(
    block_in,
    resolution,
    cotangent,
    w_qkv,
    w_proj,
    w_fc1,
    w_fc2,
    mom_qkv,
    mom_proj,
    mom_fc1,
    mom_fc2,
    avg_qkv,
    avg_proj,
    avg_fc1,
    avg_fc2,
    gains,
    gain_mom,
    gain_avg,
    biases,
    bias_mom,
    bias_avg,
):
    members = lax.axis_size("head")
    count = lax.axis_size("dp")
    member = lax.axis_index("head")
    me = lax.axis_index("dp")
    slot = member // 2
    core = member % 2
    width = block_in.shape[1]
    head_cols = w_qkv.shape[2]
    hidden_cols = w_fc1.shape[1]
    share = cotangent.shape[0]
    shard_rows = w_qkv.shape[0]
    aligned = shard_rows % 16 == 0
    paired = 2 * HEAD_WIDTH
    kind = lax.dynamic_index_in_dim(resolution, slot, keepdims=False)
    info = jnp.stack([me, core, kind, slot, member]).astype(jnp.int32)

    attn_shard, mlp_shard = call(
        cast_kernel,
        "cast",
        [((shard_rows, width), BF16), ((2, shard_rows, width), BF16)],
        (jnp.swapaxes(w_qkv, 0, 1), w_proj, w_fc1, w_fc2.T),
        scalars=0,
    )
    attn_w, mlp_w = Gather(attn_shard, count), Gather(mlp_shard, count)
    attn_w.far()

    def settle(pieces, stacked):
        if aligned:
            return pieces
        whole = joined(pieces, count, me)
        if stacked:
            whole = jnp.swapaxes(whole, 0, 1).reshape(1, 2, width, width)
        else:
            whole = whole.reshape(1, width, width)
        return ((whole, (None,)),)

    own_rels, other_rels = part_rels(count)
    part_rows = shard_rows if aligned else width

    def written(rels):
        return rels if aligned else ((None,),)

    def parts(stacked, pieces, rels):
        if aligned:
            return tuple(pieces)
        whole = pieces[0][0]
        if stacked:
            whole = jnp.swapaxes(whole.reshape(2, count, shard_rows, width), 0, 1)
        else:
            whole = whole.reshape(count, shard_rows, width)
        return parted(whole, rels, me)

    bias_rows = biases.reshape(-1, width)
    q_bias, v_bias = (bias_rows[i].reshape(members, head_cols) for i in (4, 5))
    none = jnp.zeros_like(q_bias)
    group_bias = jnp.concatenate(
        [
            q_bias[:, :paired],
            none[:, :paired],
            v_bias[:, :paired],
            q_bias[:, paired:],
            none[:, paired:],
            v_bias[:, paired:],
            none[:, paired:],
        ],
        axis=1,
    )
    own_bias, other_bias = (
        lax.dynamic_slice_in_dim(group_bias, g, 1, 0) for g in (member, member ^ 2)
    )

    tall, turned = (SLOT_PATCHES, width), (width, SLOT_PATCHES)
    of_slot = pl.BlockSpec(tall, lambda i, info: (info[SLOT], 0))
    a1, a1_t, x_rows = call(
        prepare_kernel,
        "prepare",
        [(tall, BF16), (turned, BF16), ((share, width), F32)],
        (info, block_in, gains, bias_rows),
        specs={1: of_slot},
        scratch=[pltpu.VMEM(tall, F32)],
    )
    dy, dy_t = call(
        join_kernel,
        "join",
        [(tall, BF16), (turned, BF16)],
        (info, cotangent, swap(cotangent, "head", 1)),
        scratch=[pltpu.VMEM(tall, F32)],
    )

    attn_w.near(a1)
    attn_w.turn()
    attn_w.rest()
    attn_w.last()
    mlp_w.far(attn_w.d_base, attn_w.d_away)
    attn_own, attn_other = (settle(p, False) for p in attn_w.pieces())

    def attend(pieces, bias, a1, *before):
        return call(
            attend_kernel,
            "attend",
            [
                (tall, BF16),
                ((SLOT_PATCHES, 2 * paired), BF16),
                ((SLOT_PATCHES, paired), F32),
                (tall, BF16),
            ],
            (info, a1, bias, *before, *(a for a, _ in pieces)),
            specs={i + len(before): ANYWHERE for i in range(3, 3 + len(pieces))},
            scratch=[pltpu.VMEM((width, width), BF16), pltpu.SemaphoreType.DMA((count,))],
            flops=2 * SLOT_PATCHES * (width * width + 12 * SLOT_PATCHES * HEAD_WIDTH),
            rels=[r for _, r in pieces],
            added=len(before),
        )

    own_saved = attend(attn_own, own_bias, after(a1, attn_w.x_second))
    mlp_w.near(own_saved[3], attn_w.d_second)
    other_saved = attend(attn_other, other_bias, after(a1, mlp_w.first), own_saved[3])
    mlp_w.turn()
    mlp_w.rest()
    proj = after(other_saved[3], mlp_w.second, mlp_w.x_first, mlp_w.y_first)
    h1, a2, a2_t = call(
        middle_kernel,
        "middle",
        [(tall, F32), (tall, BF16), (turned, BF16)],
        (
            info,
            block_in,
            proj,
            swap(proj, "head", 1),
            gains,
            bias_rows,
        ),
        specs={1: of_slot},
    )

    def mlp(pieces, group_mask, rels, order, *before):
        first = 7 + len(before)
        *grads, keep, send, dbias = call(
            mlp_kernel,
            "mlp",
            [((len(r), 2, part_rows, width), BF16, ANYWHERE) for r in written(rels)]
            + [
                ((share, width), BF16),
                ((SLOT_PATCHES + share, width), BF16),
                ((1, hidden_cols), F32),
            ],
            (info, a2, a2_t, dy, dy_t, bias_rows, order, *before, *(a for a, _ in pieces)),
            specs={i: ANYWHERE for i in (6, *range(first, first + len(pieces)))},
            scratch=[pltpu.VMEM((width, hidden_cols), BF16) for _ in range(4)]
            + [pltpu.VMEM(tall, F32), pltpu.SemaphoreType.DMA((2, count))],
            flops=12 * SLOT_PATCHES * width * hidden_cols,
            rels=[r for _, r in pieces],
            out_rels=written(rels),
            group_mask=group_mask,
            added=len(before),
        )
        return parts(True, grads, rels), keep, send, dbias

    mlp_w.last(a2)
    mlp_own, mlp_other = (settle(p, True) for p in mlp_w.pieces())
    mlp_sum, attn_sum = Scatter(count), Scatter(count)
    own_mlp = mlp(mlp_own, 0, own_rels, after(gains, mlp_w.d_base, mlp_w.d_away))
    mlp_sum.own(own_mlp[0])
    other_mlp = mlp(mlp_other, 2, other_rels, own_mlp[3], own_mlp[1], own_mlp[2])
    peer_mlp = swap(other_mlp[2], "head", 1)
    mlp_sum.other(other_mlp[0], peer_mlp)
    e, e_t, dh1_rows, block_out, mid_sums = call(
        middle_back_kernel,
        "middle_back",
        [
            (tall, BF16),
            (turned, BF16),
            ((share, width), F32),
            ((share, width), BF16),
            ((3, width), F32),
        ],
        (
            info,
            h1,
            dy,
            other_mlp[2],
            peer_mlp,
            other_mlp[1],
            gains,
            bias_rows,
            gains,
        ),
        scratch=[pltpu.VMEM(tall, F32)],
    )

    def attend_back(pieces, saved, rels, order, *before):
        qkv, out, lse, _ = saved
        first = 8 + len(before)
        *grads, keep, send, sums = call(
            attend_back_kernel,
            "attend_back",
            [((len(r), part_rows, width), BF16, ANYWHERE) for r in written(rels)]
            + [((share, width), BF16), ((share, width), BF16), ((1, 5 * paired), F32)],
            (info, e, e_t, a1_t, qkv, out, lse, order, *before, *(a for a, _ in pieces)),
            specs={i: ANYWHERE for i in (7, *range(first, first + len(pieces)))},
            scratch=[
                pltpu.VMEM((width, width), BF16),
                pltpu.VMEM((width, width), BF16),
                pltpu.VMEM((SLOT_PATCHES, 5 * paired), BF16),
                pltpu.VMEM(tall, F32),
                pltpu.SemaphoreType.DMA((count,)),
            ],
            flops=2 * SLOT_PATCHES * (2 * width * width + 60 * SLOT_PATCHES * HEAD_WIDTH),
            rels=[r for _, r in pieces],
            out_rels=written(rels),
            added=len(before),
        )
        return parts(False, grads, rels), keep, send, sums

    mlp_sum.turn(e)
    other_back = attend_back(attn_other, other_saved, other_rels, after(gains, mlp_sum.from_d))
    attn_sum.other(other_back[0])
    mlp_sum.last_xy(other_back[3])
    mlp_sum.near_sum(other_back[3])
    own_back = attend_back(
        attn_own,
        own_saved,
        own_rels,
        after(other_back[3], mlp_sum.from_x, mlp_sum.from_y),
        other_back[1],
        other_back[2],
    )
    done = (mlp_sum.from_y_base, mlp_sum.from_x_away, mlp_sum.from_near)
    attn_sum.own(own_back[0], *done, attn_sum.from_x, attn_sum.from_d)
    mlp_sum.far()
    attn_sum.turn(own_back[3])
    attn_sum.near_sum()
    attn_sum.last_xy()
    attn_sum.far()
    input_grad, small = call(
        last_kernel,
        "last",
        [((share, width), F32), ((12, width), F32)],
        (
            info,
            x_rows,
            dh1_rows,
            cotangent,
            own_back[1],
            swap(after(own_back[2], *done), "head", 1),
            gains,
            mid_sums,
            own_mlp[3],
            other_mlp[3],
            own_back[3],
            other_back[3],
        ),
    )
    small = small + swap(small, "head", 1)
    over = over_x(small), over_y(small), plane_swap(small)
    small = (small + over[0]) + (over[1] + over[2])
    for mask in line_masks(count):
        small = small + swap(small, "dp", mask)
    gain_grad = small[:2]
    bias_grad = small[2:].reshape(biases.shape)

    by_row = (3, shard_rows, head_cols)
    fc1, fc2 = w_fc1.shape, w_fc2.T.shape
    *fc1_outs, fc2_grad, fc2_mom, fc2_new, fc2_avg = call(
        finish_mlp_kernel,
        "finish_mlp",
        [(fc1, F32)] * 4 + [(fc2, F32)] * 4,
        (w_fc1, mom_fc1, avg_fc1, w_fc2.T, mom_fc2.T, avg_fc2.T, *mlp_sum.terms()),
        scalars=0,
    )
    fc1_grad, fc1_mom, fc1_new, fc1_avg = fc1_outs
    fc2_grad, fc2_mom, fc2_new, fc2_avg = (v.T for v in (fc2_grad, fc2_mom, fc2_new, fc2_avg))
    *qkv_outs, proj_grad, proj_mom, proj_new, proj_avg = call(
        finish_attn_kernel,
        "finish_attn",
        [(by_row, F32)] * 4 + [(w_proj.shape, F32)] * 4,
        (
            *(jnp.swapaxes(v, 0, 1) for v in (w_qkv, mom_qkv, avg_qkv)),
            w_proj,
            mom_proj,
            avg_proj,
            *attn_sum.terms(),
        ),
        scalars=0,
    )
    qkv_grad, qkv_mom, qkv_new, qkv_avg = (jnp.swapaxes(v, 0, 1) for v in qkv_outs)

    gain_mom_new, gain_new, gain_avg_new = update(
        gains, gain_grad, gain_mom, gain_avg, RATE_SMALL, 0.0
    )
    bias_mom_new, bias_new, bias_avg_new = update(
        biases, bias_grad, bias_mom, bias_avg, RATE_SMALL, 0.0
    )
    return (
        block_out,
        input_grad,
        qkv_grad,
        qkv_mom,
        qkv_new,
        qkv_avg,
        proj_grad,
        proj_mom,
        proj_new,
        proj_avg,
        fc1_grad,
        fc1_mom,
        fc1_new,
        fc1_avg,
        fc2_grad,
        fc2_mom,
        fc2_new,
        fc2_avg,
        gain_grad,
        gain_mom_new,
        gain_new,
        gain_avg_new,
        bias_grad,
        bias_mom_new,
        bias_new,
        bias_avg_new,
    )
def solution(mesh):
    return jax.shard_map(
        shards,
        mesh=mesh,
        in_specs=(
            P("dp", None),
            P("dp"),
            P(("dp", "head"), None),
            P("dp", None, "head"),
            P("head", "dp"),
            P("dp", "head"),
            P("head", "dp"),
            P("dp", None, "head"),
            P("head", "dp"),
            P("dp", "head"),
            P("head", "dp"),
            P("dp", None, "head"),
            P("head", "dp"),
            P("dp", "head"),
            P("head", "dp"),
            P(),
            P(),
            P(),
            P(),
            P(),
            P(),
        ),
        out_specs=(
            P(("dp", "head"), None),
            P(("dp", "head"), None),
            P("dp", None, "head"),
            P("dp", None, "head"),
            P("dp", None, "head"),
            P("dp", None, "head"),
            P("head", "dp"),
            P("head", "dp"),
            P("head", "dp"),
            P("head", "dp"),
            P("dp", "head"),
            P("dp", "head"),
            P("dp", "head"),
            P("dp", "head"),
            P("head", "dp"),
            P("head", "dp"),
            P("head", "dp"),
            P("head", "dp"),
            P(),
            P(),
            P(),
            P(),
            P(),
            P(),
            P(),
            P(),
        ),
        check_vma=False,
    )
```

```python
import jax
import jax.numpy as jnp
from jax import lax
from jax.experimental import pallas as pl
from jax.experimental.pallas import tpu as pltpu
from jax.sharding import PartitionSpec as P

HEAD_WIDTH = 64
SLOT_PATCHES = 784
LOWRES = 196


EPSILON = 1e-06
MOMENTUM_RATE = 0.9
AVERAGING = 0.75
WEIGHT_DECAY = 0.05
RATE_QKV = 0.001
RATE_PROJ = 0.01
RATE_FC1 = 0.0006
RATE_FC2 = 0.0003
RATE_SMALL = 0.003
MASKED = -1e30
SCALE = HEAD_WIDTH**-0.5
F32 = jnp.float32
BF16 = jnp.bfloat16
QUERY_ROWS = SLOT_PATCHES // 2
VMEM_LIMIT = 60 << 20
COST = 16
ME, CORE, KIND, SLOT, MEMBER = range(5)

IN_VMEM = pl.BlockSpec(memory_space=pltpu.VMEM)
IN_SMEM = pl.BlockSpec(memory_space=pltpu.SMEM)
ANYWHERE = pl.BlockSpec(memory_space=pl.ANY)


def update(weight, gradient, moment, average, step_rate, decay_rate):
    step_grad = gradient + decay_rate * weight
    moment_new = MOMENTUM_RATE * moment + step_grad
    weight_new = weight - step_rate * (step_grad + MOMENTUM_RATE * moment_new)
    return (moment_new, weight_new, AVERAGING * average + (1.0 - AVERAGING) * weight_new)


def swap(value, axis, mask):
    return lax.ppermute(value, axis, [(i, i ^ mask) for i in range(lax.axis_size(axis))])


def line_masks(count):
    masks, mask = [], count // 2
    while mask > 1:
        masks.append(mask)
        mask //= 2
    return masks


def line_order(count):
    order = [0]
    for mask in line_masks(count):
        order = order + [r ^ mask for r in order]
    return order


def z_sets(count):
    order = line_order(count)
    eighth = count // 8
    return order[:eighth], order[eighth : 2 * eighth], order[2 * eighth :]


def flip(order):
    return [r ^ 1 for r in order]


def after(value, *others):
    return lax.optimization_barrier((value, *others))[0]


def both_after(values, *others):
    return lax.optimization_barrier((*values, *others))[: len(values)] if others else values


def over_x(value):
    return swap(value, "head", 2)


def over_y(value):
    return swap(value, "dp", 1)


def over_both(value):
    members = lax.axis_size("head")
    total = members * lax.axis_size("dp")
    return lax.ppermute(value, ("dp", "head"), [(i, i ^ members ^ 2) for i in range(total)])


def over_z(value):
    return swap(value, "dp", 2)


def over_far(value, count):
    return swap(value, "dp", line_masks(count)[-2])


class Gather:
    def __init__(self, shard, count):
        base = shard[None]
        for mask in line_masks(count)[:-2]:
            base = jnp.concatenate([base, swap(base, "dp", mask)])
        self.base, self.count = base, count

    def far(self, *later):
        self.base = both_after((self.base,), *later)[0]
        self.first = jnp.concatenate([self.base, over_far(self.base, self.count)])

    def near(self, *later):
        self.first = both_after((self.first,), *later)[0]
        self.second = over_z(self.first)
        self.x_first, self.y_first = over_x(self.first), over_y(self.first)

    def rest_own(self, *later):
        second, y_first = both_after((self.second, self.y_first), *later)
        self.y_second, self.d_first = over_y(second), over_x(after(y_first, self.x_first))

    def rest_other(self, *later):
        second, d_first = both_after((self.second, self.d_first), self.d_first, *later)
        self.x_second, self.d_second = over_x(second), over_z(d_first)

    def pieces(self):
        base, away, near = z_sets(self.count)
        rels = base + away, near
        own = (self.first, self.second, self.y_first, self.y_second)
        other = (self.x_first, self.x_second, self.d_first, self.d_second)
        turned = tuple(flip(r) for r in rels)
        return tuple(zip(own, rels + turned)), tuple(zip(other, rels + turned))


def joined(pieces, count, me):
    order = [r for _, rel in pieces for r in rel]
    place = jnp.array([order.index(r) for r in range(count)], jnp.int32)
    return jnp.concatenate([a for a, _ in pieces])[place[jnp.arange(count, dtype=jnp.int32) ^ me]]


def part_rels(count):
    base, away, near = z_sets(count)
    own = (base, away, near, flip(near), flip(base + away))
    other = (base + away + near, flip(near), flip(base + away))
    return own, other


def parted(whole, rels, me):
    return tuple(whole[jnp.array(rel, jnp.int32) ^ me] for rel in rels)


def plus(*terms):
    return sum(t.astype(F32) for t in terms)


def low_plus(*terms):
    return plus(*terms).astype(BF16)


class Scatter:
    def __init__(self, count):
        self.count = count

    def own(self, parts, *later):
        self.base, self.away, self.near, y_near, y_rest = parts
        y_near, y_rest = both_after((y_near, y_rest), *later)
        self.from_y_near, self.from_y = over_y(y_near), over_y(y_rest)

    def other(self, parts, *later):
        xs, d_near, self.d_rest = parts
        xs, d_near = both_after((xs, d_near), *later)
        self.from_d, self.from_x = over_z(d_near), over_x(xs)

    def turn(self, *later):
        rest, from_d = both_after((self.d_rest, self.from_d), *later)
        self.from_both = over_both(low_plus(rest, from_d))

    def near_sum(self, *later):
        near = both_after((self.near,), *later)[0]
        cut = 2 * self.base.shape[0]
        self.near_total = low_plus(near, self.from_y_near, self.from_x[cut:])
        self.from_near = over_z(self.near_total)

    def far(self, *later):
        cut = self.base.shape[0]
        away = both_after((self.away,), *later)[0]
        rest = (self.from_y, self.from_both, self.from_near, self.from_x)
        self.from_away = over_far(low_plus(away, *(r[cut : 2 * cut] for r in rest)), self.count)

    def terms(self):
        cut = self.base.shape[0]
        rest = (self.from_y, self.from_both, self.from_near, self.from_x)
        terms = (self.base, self.from_away, *(r[:cut] for r in rest))
        masks = line_masks(self.count)[:-2]
        if not masks:
            return (self.base, self.from_away, *rest)
        total = plus(*terms)
        for mask in reversed(masks):
            keep = total.shape[0] // 2
            total = total[:keep] + swap(total[keep:].astype(BF16), "dp", mask)
        return (total[:1],)


def dot(a, b):
    return jnp.dot(a, b, preferred_element_type=F32)


def dot_t(a, b):
    return lax.dot_general(a, b, (((1,), (1,)), ((), ())), preferred_element_type=F32)


def t_dot(a, b):
    return lax.dot_general(a, b, (((0,), (0,)), ((), ())), preferred_element_type=F32)


def normalize(inputs):
    mean_row = jnp.mean(inputs, axis=-1, keepdims=True)
    centred = inputs - mean_row
    spread = jnp.mean(centred * centred, axis=-1, keepdims=True)
    inv_std = lax.rsqrt(spread + EPSILON)
    return (centred * inv_std, inv_std)


def norm_back(grad_out, centred, inv_std, gain_row):
    scaled = grad_out * gain_row
    return inv_std * (
        scaled
        - jnp.mean(scaled, axis=-1, keepdims=True)
        - centred * jnp.mean(scaled * centred, axis=-1, keepdims=True)
    )


def piece_copies(info, refs, rels, dest, sems, out=False, at=()):
    copies = []
    for ref, rel in zip(refs, rels):
        for j, r in enumerate(rel):
            rows = ref.shape[-2]
            start = 0 if r is None else pl.multiple_of((info[ME] ^ r) * rows, rows)
            there, here = ref.at[(j, *at)], dest.at[pl.ds(start, rows)]
            copies.append((here, there) if out else (there, here))
    copies = [
        pltpu.make_async_copy(a, b, sems.at[i]) for i, (a, b) in enumerate(copies)
    ]
    for copy in copies:
        copy.start()
    return copies


def wait_all(copies):
    for copy in copies:
        copy.wait()


class Lazy:
    def __init__(self, source, here, sem):
        self.here = here
        self.copy = pltpu.make_async_copy(source, here, sem)

    def start(self):
        self.copy.start()

    def ready(self):
        self.copy.wait()
        return self.here


class Early:
    def __init__(self, target, here, sem):
        self.here = here
        self.copy = pltpu.make_async_copy(here, target, sem)

    def flush(self):
        self.copy.start()


def start_all(values):
    for value in values:
        value.start()


def lanes():
    return lax.broadcasted_iota(jnp.int32, (1, 2 * HEAD_WIDTH), 1)


def segments(shape, axis, start, info):
    run = (lax.broadcasted_iota(jnp.int32, shape, axis) + start) // LOWRES
    return jnp.where(info[KIND] > 0, 0, run)


def column_sum(rows):
    return jnp.sum(rows, axis=0, keepdims=True)


def cast_kernel(w_qkv, w_proj, w_fc1, w_fc2, attn, mlp):
    wide = 2 * HEAD_WIDTH
    for i in range(3):
        attn[:, i * wide : (i + 1) * wide] = w_qkv[i, :, :wide].astype(BF16)
    single = [w_qkv[i, :, wide:] for i in range(3)]
    proj = w_proj[...].T
    attn[:, 3 * wide : 4 * wide] = jnp.concatenate(single[:2], axis=1).astype(BF16)
    attn[:, 4 * wide : 5 * wide] = jnp.concatenate([single[2], proj[:, wide:]], axis=1).astype(BF16)
    attn[:, 5 * wide : 6 * wide] = proj[:, :wide].astype(BF16)
    mlp[0] = w_fc1[...].astype(BF16)
    mlp[1] = w_fc2[...].astype(BF16)


def prepare_kernel(info, block, gains, biases, a1, a1_t, x_rows, rows):
    share = x_rows.shape[0]
    x = block[...].astype(F32)
    rows[...] = x
    x_rows[...] = rows[pl.ds(pl.multiple_of(info[CORE] * share, 8), share), :]
    xhat, _ = normalize(x)
    normed = (xhat * gains[0:1, :] + biases[0:1, :]).astype(BF16)
    a1[...] = normed
    a1_t[...] = normed.T


def join_kernel(info, mine, peer, dy, dy_t, rows):
    share = mine.shape[0]
    start = pl.multiple_of(info[CORE] * share, 8)
    rows[pl.ds(start, share), :] = mine[...].astype(F32)
    rows[pl.ds(pl.multiple_of(share - start, 8), share), :] = peer[...].astype(F32)
    low = rows[...].astype(BF16)
    dy[...] = low
    dy_t[...] = low.T


def attend_kernel(info, a1, bias, *rest, rels, added):
    before, rest = rest[:added], rest[added:]
    count = len(rels)
    pieces, (early_qkv, early_out, early_lse, proj, w, sems) = rest[:count], rest[count:]
    qkv, out, lse = early_qkv.here, early_out.here, early_lse.here
    copies = piece_copies(info, pieces, rels, w, sems)
    start_all((a1, *before))
    wait_all(copies)
    a1 = a1.ready()
    lane = lanes()
    low = lane < HEAD_WIDTH
    zero = jnp.zeros((), BF16)
    m = dot(a1[...], w[:, :640]) + bias[...]
    k01, v01 = m[:, 128:256].astype(BF16), m[:, 256:384].astype(BF16)
    pair = m[:, 384:512]
    k2 = pltpu.roll(pair, HEAD_WIDTH, 1).astype(BF16)
    v2 = m[:, 512:640].astype(BF16)
    qkv[:, 0:128] = (m[:, 0:128] * SCALE).astype(BF16)
    qkv[:, 128:256] = k01
    qkv[:, 256:384] = v01
    qkv[:, 384:512] = jnp.where(low, pair * SCALE, 0.0).astype(BF16)
    qkv[:, 512:640] = k2
    qkv[:, 640:768] = v2
    early_qkv.flush()
    columns = segments((1, SLOT_PATCHES), 1, 0, info)
    for start in range(0, SLOT_PATCHES, QUERY_ROWS):
        rows = slice(start, start + QUERY_ROWS)
        seen = segments((QUERY_ROWS, 1), 0, start, info) == columns
        q01 = qkv[rows, 0:128]
        outs, logs = [], []
        for query, keys, value in (
            (jnp.where(low, q01, zero), k01, v01),
            (jnp.where(low, zero, q01), k01, v01),
            (qkv[rows, 384:512], k2, v2),
        ):
            scores = jnp.where(seen, dot_t(query, keys), MASKED)
            largest = jnp.max(scores, axis=-1, keepdims=True)
            expon = jnp.exp(scores - largest)
            summed = jnp.sum(expon, axis=-1, keepdims=True)
            probs = (expon * (1.0 / summed)).astype(BF16)
            outs.append(dot(probs, value))
            logs.append(largest + jnp.log(summed))
        third = jnp.where(low, 0.0, pltpu.roll(outs[2], HEAD_WIDTH, 1))
        out[rows, 0:128] = third.astype(BF16)
        out[rows, 128:256] = jnp.where(low, outs[0], outs[1]).astype(BF16)
        lse[rows, :] = jnp.where(lane == 0, logs[0], jnp.where(lane == 1, logs[1], logs[2]))
    early_out.flush()
    early_lse.flush()
    total = dot_t(out[...], w[:, 512:768])
    proj[...] = plus(total, *(b.ready()[...] for b in before)).astype(BF16)


def middle_kernel(info, block, mine, peer, gains, biases, h1, a2, a2_t):
    both = plus(mine[...], peer[...])
    middle = block[...].astype(F32) + (both + biases[2:3, :])
    h1[...] = middle
    xhat, _ = normalize(middle)
    normed = (xhat * gains[1:2, :] + biases[1:2, :]).astype(BF16)
    a2[...] = normed
    a2_t[...] = normed.T


def split_rows(info, total, scratch, keep, send, before, at=0):
    share = keep.shape[0]
    start = pl.multiple_of(info[CORE] * share, 8)
    scratch[...] = total
    kept = scratch[pl.ds(start, share), :]
    keep[...] = plus(kept, *(b[...] for b in before[:1])).astype(keep.dtype)
    theirs = scratch[pl.ds(pl.multiple_of(share - start, 8), share), :]
    sent = plus(theirs, *(b[at : at + share, :] for b in before[1:]))
    send[at : at + share, :] = sent.astype(send.dtype)


def mlp_kernel(info, a2, a2_t, dy, dy_t, biases, order, *rest, rels, out_rels, group_mask, added):
    before, rest = rest[:added], rest[added:]
    count, outs = len(rels), len(out_rels)
    pieces, rest = rest[:count], rest[count:]
    parts, (keep, send, dbias, w1, w2, dw1, dw2, rows, sems) = rest[:outs], rest[outs:]
    first = piece_copies(info, pieces, rels, w1, sems.at[0], at=(0,))
    a2.start()
    second = piece_copies(info, pieces, rels, w2, sems.at[1], at=(1,))
    dy.start()
    wait_all(first)
    a2 = a2.ready()
    start_all((dy_t, a2_t, *before[1:]))
    bias = biases[pl.ds(6 + (info[MEMBER] ^ group_mask), 1), :]
    u = dot(a2[...], w1[...]) + bias
    phi = 0.5 + 0.5 * lax.erf(u * (2.0**-0.5))
    hidden = (u * phi).astype(BF16)
    slope = phi + u * (jnp.exp(-0.5 * u * u) * 0.3989422804014327)
    wait_all(second)
    dpre = (dot(dy.ready()[...], w2[...]) * slope).astype(BF16)
    dw2[...] = dot(dy_t.ready()[...], hidden).astype(BF16)
    second = piece_copies(info, parts, out_rels, dw2, sems.at[1], out=True, at=(1,))
    dw1[...] = dot(a2_t.ready()[...], dpre).astype(BF16)
    first = piece_copies(info, parts, out_rels, dw1, sems.at[0], out=True, at=(0,))
    before = before[:1] + tuple(b.ready() for b in before[1:])
    da2 = plus(dot_t(dpre, w1[...]), *(b[:SLOT_PATCHES, :] for b in before[1:]))
    send[:SLOT_PATCHES, :] = da2.astype(BF16)
    split_rows(info, dot_t(hidden, w2[...]), rows, keep, send, before, SLOT_PATCHES)
    dbias[...] = column_sum(dpre.astype(F32))
    wait_all(first)
    wait_all(second)


def middle_back(
    info, h1, dy, mine, peer, kept, gains, biases, e, e_t, dh1_rows, block_out, sums, rows
):
    share = block_out.shape[0]
    start = pl.multiple_of(info[CORE] * share, 8)
    h1 = h1.ready()
    xhat, inv_std = normalize(h1[...])
    mine, peer = mine.ready(), peer.ready()
    da2 = plus(mine[:SLOT_PATCHES, :], peer[:SLOT_PATCHES, :])
    dh1 = dy.ready()[...].astype(F32) + norm_back(da2, xhat, inv_std, gains[1:2, :])
    low = dh1.astype(BF16)
    e.here[...] = low
    e.flush()
    e_t.here[...] = low.T
    e_t.flush()
    rows[...] = dh1
    dh1_rows[...] = rows[pl.ds(start, share), :]
    sums[0:1, :] = column_sum(da2 * xhat)
    sums[1:2, :] = column_sum(da2)
    sums[2:3, :] = column_sum(dh1)
    mlp = plus(kept[...], peer[SLOT_PATCHES : SLOT_PATCHES + share, :])
    block_out[...] = ((h1[pl.ds(start, share), :] + mlp) + biases[3:4, :]).astype(BF16)


def first_back_kernel(
    info, h1, dy, mine, peer, kept, gains, biases, a1_t, qkv, out, lse, *rest, rels, out_rels
):
    count, outs = len(rels), len(out_rels)
    pieces, rest = rest[:count], rest[count:]
    parts, rest = rest[:outs], rest[outs:]
    keep, send, sums, e, e_t, dh1_rows, block_out, mid, w, dw, grads, rows, sems = rest
    start_all((h1, mine, peer, dy))
    copies = piece_copies(info, pieces, rels, w, sems)
    start_all((qkv, lse, out, a1_t))
    middle_back(
        info, h1, dy, mine, peer, kept, gains, biases, e, e_t, dh1_rows, block_out, mid, rows
    )
    wait_all(copies)
    attend_back(
        info, e.here, e_t, a1_t, qkv, out, lse, (), parts, out_rels, keep, send, sums,
        w, dw, grads, rows, sems,
    )


def second_back_kernel(info, e, e_t, a1_t, qkv, out, lse, kept, sent, *rest, rels, out_rels):
    count, outs = len(rels), len(out_rels)
    pieces, rest = rest[:count], rest[count:]
    parts, (keep, send, sums, w, dw, grads, rows, sems) = rest[:outs], rest[outs:]
    copies = piece_copies(info, pieces, rels, w, sems)
    start_all((e, qkv, lse, out, a1_t, e_t))
    wait_all(copies)
    attend_back(
        info, e.ready(), e_t, a1_t, qkv, out, lse, (kept, sent), parts, out_rels, keep, send, sums,
        w, dw, grads, rows, sems,
    )


def attend_back(
    info, e, e_t, a1_t, qkv, out, lse, before, parts, out_rels, keep, send, sums,
    w, dw, grads, rows, sems,
):
    qkv, lse = qkv.ready(), lse.ready()
    low = lanes() < HEAD_WIDTH
    zero = jnp.zeros((), BF16)
    dout = dot(e[...], w[:, 512:768])
    do2 = jnp.where(low, pltpu.roll(dout[:, 0:128], HEAD_WIDTH, 1), 0.0).astype(BF16)
    do01 = dout[:, 128:256].astype(BF16)
    q01, k01, v01 = qkv[:, 0:128], qkv[:, 128:256], qkv[:, 256:384]
    q2, k2, v2 = qkv[:, 384:512], qkv[:, 512:640], qkv[:, 640:768]
    lse_t = jnp.transpose(lse[...], (1, 0))
    seen = segments((SLOT_PATCHES, 1), 0, 0, info) == segments((1, SLOT_PATCHES), 1, 0, info)
    dq, dk, dv = [], [], []
    for head, (query, keys, value, dcontext) in enumerate(
        (
            (q01, jnp.where(low, k01, zero), jnp.where(low, v01, zero), do01),
            (q01, jnp.where(low, zero, k01), jnp.where(low, zero, v01), do01),
            (q2, k2, jnp.where(low, v2, zero), do2),
        )
    ):
        scores = jnp.where(seen, dot_t(keys, query), MASKED)
        probs = jnp.exp(scores - lse_t[head : head + 1, :])
        dprob = dot_t(value, dcontext)
        row_dot = column_sum(probs * dprob)
        dscore = (probs * (dprob - row_dot)).astype(BF16)
        dv.append(dot(probs.astype(BF16), dcontext))
        dk.append(dot(dscore, query))
        dq.append(t_dot(dscore, keys))
    grads[:, 0:128] = (jnp.where(low, dq[0], dq[1]) * SCALE).astype(BF16)
    grads[:, 128:256] = jnp.where(low, dk[0], dk[1]).astype(BF16)
    grads[:, 256:384] = jnp.where(low, dv[0], dv[1]).astype(BF16)
    shifted = pltpu.roll(dk[2], HEAD_WIDTH, 1)
    grads[:, 384:512] = jnp.where(low, dq[2] * SCALE, shifted).astype(BF16)
    grads[:, 512:640] = jnp.where(low, dv[2], 0.0).astype(BF16)
    a1_t, out = a1_t.ready(), out.ready()
    e_t = e_t.here if isinstance(e_t, Early) else e_t.ready()
    dw[:, 0:512] = dot(a1_t[...], grads[:, 0:512]).astype(BF16)
    dw[:, 512:640] = (dot(a1_t[...], grads[:, 512:640]) + dot(e_t[...], out[:, 0:128])).astype(BF16)
    dw[:, 640:768] = dot(e_t[...], out[:, 128:256]).astype(BF16)
    copies = piece_copies(info, parts, out_rels, dw, sems, out=True)
    split_rows(info, dot_t(grads[...], w[:, 0:640]), rows, keep, send, before)
    sums[...] = column_sum(grads[...].astype(F32))
    wait_all(copies)


def last_kernel(
    info, x_rows, dh1_rows, mine, kept, peer, gains, mid, db0, db1, s0, s1, input_grad, small
):
    xhat, inv_std = normalize(x_rows[...])
    da1 = plus(kept[...], peer[...])
    input_grad[...] = dh1_rows[...] + norm_back(da1, xhat, inv_std, gains[0:1, :])
    once = jnp.where(info[CORE] == 0, 1.0, 0.0)
    member = info[MEMBER]
    small[...] = jnp.zeros_like(small)
    small[0:1, :] = column_sum(da1 * xhat)
    small[1:2, :] = once * mid[0:1, :]
    small[2:3, :] = column_sum(da1)
    small[3:4, :] = once * mid[1:2, :]
    small[4:5, :] = once * mid[2:3, :]
    small[5:6, :] = column_sum(mine[...].astype(F32))
    low = lanes() < HEAD_WIDTH
    for row, pair, single in ((6, 0, 384), (7, 256, 512)):
        for group in range(0, 4, 2):
            even, odd = (
                tuple(
                    jnp.where(
                        member == which,
                        s0[:, at : at + 128],
                        jnp.where(member == which ^ 2, s1[:, at : at + 128], 0.0),
                    )
                    for at in (pair, single)
                )
                for which in (group, group + 1)
            )
            turned = pltpu.roll(odd[0], HEAD_WIDTH, 1)
            at = group * 192
            small[row : row + 1, at : at + 128] = even[0]
            small[row : row + 1, at + 128 : at + 256] = jnp.where(low, even[1], turned)
            small[row : row + 1, at + 256 : at + 384] = jnp.where(
                low, turned, pltpu.roll(odd[1], HEAD_WIDTH, 1)
            )
    small[pl.ds(8 + member, 1), :] = db0[...]
    small[pl.ds(8 + (member ^ 2), 1), :] = db1[...]


def step(weight, gradient, moment, average, outs, rate):
    for ref, value in zip(
        outs, (gradient, *update(weight, gradient, moment, average, rate, WEIGHT_DECAY))
    ):
        ref[...] = value.reshape(ref.shape)


def finish_mlp_kernel(w1, m1, a1, w2, m2, a2, *rest):
    terms, outs = rest[:-8], rest[-8:]
    first, second = (plus(*(t[0, i] for t in terms)) for i in range(2))
    step(w1[...], first, m1[...], a1[...], outs[:4], RATE_FC1)
    step(w2[...], second, m2[...], a2[...], outs[4:], RATE_FC2)


def finish_attn_kernel(w1, m1, a1, w2, m2, a2, *rest):
    terms, outs = rest[:-8], rest[-8:]
    total = plus(*(t[0] for t in terms))
    wide = 2 * HEAD_WIDTH
    for i in range(3):
        single = 3 * wide + i * HEAD_WIDTH
        gradient = jnp.concatenate(
            [total[:, i * wide : (i + 1) * wide], total[:, single : single + HEAD_WIDTH]], axis=1
        )
        step(w1[i], gradient, m1[i], a1[i], [o.at[i] for o in outs[:4]], RATE_QKV)
    gradient = jnp.concatenate(
        [total[:, 5 * wide :], total[:, 5 * wide - HEAD_WIDTH : 5 * wide]], axis=1
    ).T
    step(w2[...], gradient, m2[...], a2[...], outs[4:], RATE_PROJ)


def call(
    kernel, name, outs, inputs, specs=None, scratch=(), flops=0, scalars=1, lazy=(), early=(), **fixed
):
    results = [jax.ShapeDtypeStruct(s, d) for s, d, *_ in outs]
    out_specs = [ANYWHERE if rest else IN_VMEM for _, _, *rest in outs]
    specs = dict(specs or {})
    for i in lazy:
        specs[i] = ANYWHERE
    for i in early:
        out_specs[i] = ANYWHERE
    moved = [inputs[i] for i in lazy] + [results[i] for i in early]
    extra = [pltpu.VMEM(v.shape, v.dtype) for v in moved]
    extra += [pltpu.SemaphoreType.DMA((len(moved),))] if moved else []
    size = sum(v.size * v.dtype.itemsize for v in (*inputs, *results))

    def body(*refs):
        refs = list(refs)
        cut = len(refs) - len(extra)
        here, sems = refs[cut:], refs[-1]
        leaving = []
        for n, i in enumerate(lazy):
            refs[i] = Lazy(refs[i], here[n], sems.at[n])
        for n, i in enumerate(early, len(lazy)):
            value = Early(refs[len(inputs) + i], here[n], sems.at[n])
            refs[len(inputs) + i] = value
            leaving.append(value.copy)
        kernel(*refs[:cut], **fixed)
        wait_all(leaving)

    body.__name__ = name
    return pl.pallas_call(
        body,
        out_shape=results,
        grid_spec=pltpu.PrefetchScalarGridSpec(
            num_scalar_prefetch=scalars,
            grid=(1,),
            in_specs=[specs.get(i, IN_VMEM) for i in range(scalars, len(inputs))],
            out_specs=out_specs,
            scratch_shapes=[*scratch, *extra],
        ),
        compiler_params=pltpu.CompilerParams(vmem_limit_bytes=VMEM_LIMIT),
        cost_estimate=pl.CostEstimate(flops=flops // COST, bytes_accessed=size // COST, transcendentals=0),
        name=name,
    )(*inputs)


def shards(
    block_in,
    resolution,
    cotangent,
    w_qkv,
    w_proj,
    w_fc1,
    w_fc2,
    mom_qkv,
    mom_proj,
    mom_fc1,
    mom_fc2,
    avg_qkv,
    avg_proj,
    avg_fc1,
    avg_fc2,
    gains,
    gain_mom,
    gain_avg,
    biases,
    bias_mom,
    bias_avg,
):
    members = lax.axis_size("head")
    count = lax.axis_size("dp")
    member = lax.axis_index("head")
    me = lax.axis_index("dp")
    slot = member // 2
    core = member % 2
    width = block_in.shape[1]
    head_cols = w_qkv.shape[2]
    hidden_cols = w_fc1.shape[1]
    share = cotangent.shape[0]
    padded = -(-share // 16) * 16
    shard_rows = w_qkv.shape[0]
    aligned = shard_rows % 16 == 0
    paired = 2 * HEAD_WIDTH
    kind = lax.dynamic_index_in_dim(resolution, slot, keepdims=False)
    info = jnp.stack([me, core, kind, slot, member]).astype(jnp.int32)

    attn_shard, mlp_shard = call(
        cast_kernel,
        "cast",
        [((shard_rows, width), BF16), ((2, shard_rows, width), BF16)],
        (jnp.swapaxes(w_qkv, 0, 1), w_proj, w_fc1, w_fc2.T),
        scalars=0,
    )
    attn_w, mlp_w = Gather(attn_shard, count), Gather(mlp_shard, count)
    attn_w.far()

    def settle(pieces, stacked):
        if aligned:
            return pieces
        whole = joined(pieces, count, me)
        if stacked:
            whole = jnp.swapaxes(whole, 0, 1).reshape(1, 2, width, width)
        else:
            whole = whole.reshape(1, width, width)
        return ((whole, (None,)),)

    own_rels, other_rels = part_rels(count)
    part_rows = shard_rows if aligned else width

    def written(rels):
        return rels if aligned else ((None,),)

    def parts(stacked, pieces, rels):
        if aligned:
            return tuple(pieces)
        whole = pieces[0][0]
        if stacked:
            whole = jnp.swapaxes(whole.reshape(2, count, shard_rows, width), 0, 1)
        else:
            whole = whole.reshape(count, shard_rows, width)
        return parted(whole, rels, me)

    bias_rows = biases.reshape(-1, width)
    q_bias, v_bias = (bias_rows[i].reshape(members, head_cols) for i in (4, 5))
    none = jnp.zeros_like(q_bias)
    group_bias = jnp.concatenate(
        [
            q_bias[:, :paired],
            none[:, :paired],
            v_bias[:, :paired],
            q_bias[:, paired:],
            none[:, paired:],
            v_bias[:, paired:],
            none[:, paired:],
        ],
        axis=1,
    )
    own_bias, other_bias = (
        lax.dynamic_slice_in_dim(group_bias, g, 1, 0) for g in (member, member ^ 2)
    )

    tall, turned = (SLOT_PATCHES, width), (width, SLOT_PATCHES)
    of_slot = pl.BlockSpec(tall, lambda i, info: (info[SLOT], 0))
    a1, a1_t, x_rows = call(
        prepare_kernel,
        "prepare",
        [(tall, BF16), (turned, BF16), ((share, width), F32)],
        (info, block_in, gains, bias_rows),
        specs={1: of_slot},
        scratch=[pltpu.VMEM(tall, F32)],
    )
    dy, dy_t = call(
        join_kernel,
        "join",
        [(tall, BF16), (turned, BF16)],
        (info, cotangent, swap(cotangent, "head", 1)),
        scratch=[pltpu.VMEM(tall, F32)],
    )

    attn_w.near(a1)
    attn_w.rest_own()
    attn_w.rest_other()
    mlp_w.far(attn_w.d_first)
    attn_own, attn_other = (settle(p, False) for p in attn_w.pieces())

    def attend(pieces, bias, a1, *before):
        return call(
            attend_kernel,
            "attend",
            [
                (tall, BF16),
                ((SLOT_PATCHES, 2 * paired), BF16),
                ((SLOT_PATCHES, paired), F32),
                (tall, BF16),
            ],
            (info, a1, bias, *before, *(a for a, _ in pieces)),
            specs={i + len(before): ANYWHERE for i in range(3, 3 + len(pieces))},
            lazy=(1, *range(3, 3 + len(before))),
            early=(0, 1, 2),
            scratch=[pltpu.VMEM((width, width), BF16), pltpu.SemaphoreType.DMA((count,))],
            flops=2 * SLOT_PATCHES * (width * width + 12 * SLOT_PATCHES * HEAD_WIDTH),
            rels=[r for _, r in pieces],
            added=len(before),
        )

    own_saved = attend(attn_own, own_bias, a1)
    mlp_w.near(own_saved[3], attn_w.x_second, attn_w.d_second)
    other_saved = attend(attn_other, other_bias, after(a1, mlp_w.first), own_saved[3])
    mlp_w.rest_own(other_saved[3])
    proj = after(other_saved[3], mlp_w.second, mlp_w.x_first, mlp_w.y_first)
    h1, a2, a2_t = call(
        middle_kernel,
        "middle",
        [(tall, F32), (tall, BF16), (turned, BF16)],
        (
            info,
            block_in,
            proj,
            swap(proj, "head", 1),
            gains,
            bias_rows,
        ),
        specs={1: of_slot},
    )

    def mlp(pieces, group_mask, rels, order, *before):
        first = 7 + len(before)
        *grads, keep, send, dbias = call(
            mlp_kernel,
            "mlp",
            [((len(r), 2, part_rows, width), BF16, ANYWHERE) for r in written(rels)]
            + [
                ((share, width), BF16),
                ((SLOT_PATCHES + padded, width), BF16),
                ((1, hidden_cols), F32),
            ],
            (info, a2, a2_t, dy, dy_t, bias_rows, order, *before, *(a for a, _ in pieces)),
            specs={i: ANYWHERE for i in (6, *range(first, first + len(pieces)))},
            lazy=(1, 2, 3, 4, *range(8, 7 + len(before))),
            scratch=[pltpu.VMEM((width, hidden_cols), BF16) for _ in range(4)]
            + [pltpu.VMEM(tall, F32), pltpu.SemaphoreType.DMA((2, count))],
            flops=12 * SLOT_PATCHES * width * hidden_cols,
            rels=[r for _, r in pieces],
            out_rels=written(rels),
            group_mask=group_mask,
            added=len(before),
        )
        return parts(True, grads, rels), keep, send, dbias

    mlp_w.rest_other(a2, dy_t)
    mlp_own, mlp_other = (settle(p, True) for p in mlp_w.pieces())
    mlp_sum, attn_sum = Scatter(count), Scatter(count)
    own_mlp = mlp(mlp_own, 0, own_rels, after(gains, mlp_w.d_first))
    mlp_sum.own(own_mlp[0])
    other_mlp = mlp(mlp_other, 2, other_rels, own_mlp[3], own_mlp[1], own_mlp[2])
    peer_mlp = swap(other_mlp[2], "head", 1)
    mlp_sum.other(other_mlp[0], peer_mlp)
    back_outs = [((share, width), BF16), ((share, width), BF16), ((1, 5 * paired), F32)]
    back_scratch = [
        pltpu.VMEM((width, width), BF16),
        pltpu.VMEM((width, width), BF16),
        pltpu.VMEM((SLOT_PATCHES, 5 * paired), BF16),
        pltpu.VMEM(tall, F32),
        pltpu.SemaphoreType.DMA((count,)),
    ]
    back_flops = 2 * SLOT_PATCHES * (2 * width * width + 60 * SLOT_PATCHES * HEAD_WIDTH)

    def back_parts(rels):
        return [((len(r), part_rows, width), BF16, ANYWHERE) for r in written(rels)]

    *grads, keep, send, sums, e, e_t, dh1_rows, block_out, mid_sums = call(
        first_back_kernel,
        "first_back",
        back_parts(other_rels)
        + back_outs
        + [
            (tall, BF16),
            (turned, BF16),
            ((share, width), F32),
            ((share, width), BF16),
            ((3, width), F32),
        ],
        (
            info,
            h1,
            dy,
            other_mlp[2],
            peer_mlp,
            other_mlp[1],
            gains,
            bias_rows,
            a1_t,
            *other_saved[:3],
            *(a for a, _ in attn_other),
        ),
        specs={i: ANYWHERE for i in range(12, 12 + len(attn_other))},
        lazy=(1, 2, 3, 4, 8, 9, 10, 11),
        early=(len(written(other_rels)) + 3, len(written(other_rels)) + 4),
        scratch=back_scratch,
        flops=back_flops,
        rels=[r for _, r in attn_other],
        out_rels=written(other_rels),
    )
    other_back = parts(False, grads, other_rels), keep, send, sums
    attn_sum.other(other_back[0])
    mlp_sum.turn(e)
    mlp_sum.near_sum(other_back[3], mlp_sum.from_y)
    *grads, keep, send, sums = call(
        second_back_kernel,
        "second_back",
        back_parts(own_rels) + back_outs,
        (
            info,
            e,
            e_t,
            a1_t,
            *own_saved[:3],
            *other_back[1:3],
            *(a for a, _ in attn_own),
        ),
        specs={i: ANYWHERE for i in range(9, 9 + len(attn_own))},
        lazy=(1, 2, 3, 4, 5, 6),
        scratch=back_scratch,
        flops=back_flops,
        rels=[r for _, r in attn_own],
        out_rels=written(own_rels),
    )
    own_back = parts(False, grads, own_rels), keep, send, sums
    done = (mlp_sum.from_near, mlp_sum.from_both, attn_sum.from_x, attn_sum.from_d)
    peer_back = swap(after(own_back[2], *done), "head", 1)
    attn_sum.own(own_back[0], peer_back)
    mlp_sum.far()
    attn_sum.turn(own_back[3])
    input_grad, small = call(
        last_kernel,
        "last",
        [((share, width), F32), ((12, width), F32)],
        (
            info,
            x_rows,
            dh1_rows,
            cotangent,
            own_back[1],
            peer_back,
            gains,
            mid_sums,
            own_mlp[3],
            other_mlp[3],
            own_back[3],
            other_back[3],
        ),
    )
    by_row = (3, shard_rows, head_cols)
    fc1, fc2 = w_fc1.shape, w_fc2.T.shape
    *fc1_outs, fc2_grad, fc2_mom, fc2_new, fc2_avg = call(
        finish_mlp_kernel,
        "finish_mlp",
        [(fc1, F32)] * 4 + [(fc2, F32)] * 4,
        (w_fc1, mom_fc1, avg_fc1, w_fc2.T, mom_fc2.T, avg_fc2.T, *mlp_sum.terms()),
        scalars=0,
    )
    fc1_grad, fc1_mom, fc1_new, fc1_avg = fc1_outs
    fc2_grad, fc2_mom, fc2_new, fc2_avg = (v.T for v in (fc2_grad, fc2_mom, fc2_new, fc2_avg))
    attn_sum.near_sum(input_grad)
    attn_sum.far()
    small = small + swap(small, "head", 1)
    small = after(small, mlp_sum.from_away, attn_sum.from_both, attn_sum.from_y)
    over = over_x(small), over_y(small), over_both(small)
    small = after((small + over[0]) + (over[1] + over[2]), attn_sum.from_near)
    for mask in line_masks(count):
        small = small + swap(small, "dp", mask)
    gain_grad = small[:2]
    bias_grad = small[2:].reshape(biases.shape)

    *qkv_outs, proj_grad, proj_mom, proj_new, proj_avg = call(
        finish_attn_kernel,
        "finish_attn",
        [(by_row, F32)] * 4 + [(w_proj.shape, F32)] * 4,
        (
            *(jnp.swapaxes(v, 0, 1) for v in (w_qkv, mom_qkv, avg_qkv)),
            w_proj,
            mom_proj,
            avg_proj,
            *attn_sum.terms(),
        ),
        scalars=0,
    )
    qkv_grad, qkv_mom, qkv_new, qkv_avg = (jnp.swapaxes(v, 0, 1) for v in qkv_outs)

    gain_mom_new, gain_new, gain_avg_new = update(
        gains, gain_grad, gain_mom, gain_avg, RATE_SMALL, 0.0
    )
    bias_mom_new, bias_new, bias_avg_new = update(
        biases, bias_grad, bias_mom, bias_avg, RATE_SMALL, 0.0
    )
    return (
        block_out,
        input_grad,
        qkv_grad,
        qkv_mom,
        qkv_new,
        qkv_avg,
        proj_grad,
        proj_mom,
        proj_new,
        proj_avg,
        fc1_grad,
        fc1_mom,
        fc1_new,
        fc1_avg,
        fc2_grad,
        fc2_mom,
        fc2_new,
        fc2_avg,
        gain_grad,
        gain_mom_new,
        gain_new,
        gain_avg_new,
        bias_grad,
        bias_mom_new,
        bias_new,
        bias_avg_new,
    )
def solution(mesh):
    return jax.shard_map(
        shards,
        mesh=mesh,
        in_specs=(
            P("dp", None),
            P("dp"),
            P(("dp", "head"), None),
            P("dp", None, "head"),
            P("head", "dp"),
            P("dp", "head"),
            P("head", "dp"),
            P("dp", None, "head"),
            P("head", "dp"),
            P("dp", "head"),
            P("head", "dp"),
            P("dp", None, "head"),
            P("head", "dp"),
            P("dp", "head"),
            P("head", "dp"),
            P(),
            P(),
            P(),
            P(),
            P(),
            P(),
        ),
        out_specs=(
            P(("dp", "head"), None),
            P(("dp", "head"), None),
            P("dp", None, "head"),
            P("dp", None, "head"),
            P("dp", None, "head"),
            P("dp", None, "head"),
            P("head", "dp"),
            P("head", "dp"),
            P("head", "dp"),
            P("head", "dp"),
            P("dp", "head"),
            P("dp", "head"),
            P("dp", "head"),
            P("dp", "head"),
            P("head", "dp"),
            P("head", "dp"),
            P("head", "dp"),
            P("head", "dp"),
            P(),
            P(),
            P(),
            P(),
            P(),
            P(),
            P(),
            P(),
        ),
        check_vma=False,
    )
```

```python
import jax
import jax.numpy as jnp
from jax import lax
from jax.experimental import pallas as pl
from jax.experimental.pallas import tpu as pltpu
from jax.sharding import PartitionSpec as P

HEAD_WIDTH = 64
SLOT_PATCHES = 784
LOWRES = 196


EPSILON = 1e-06
MOMENTUM_RATE = 0.9
AVERAGING = 0.75
WEIGHT_DECAY = 0.05
RATE_QKV = 0.001
RATE_PROJ = 0.01
RATE_FC1 = 0.0006
RATE_FC2 = 0.0003
RATE_SMALL = 0.003
MASKED = -1e30
SCALE = HEAD_WIDTH**-0.5
F32 = jnp.float32
BF16 = jnp.bfloat16
QUERY_ROWS = SLOT_PATCHES // 2
VMEM_LIMIT = 60 << 20
COST = 16
GAINS, BIASES, KIND, PARAM_ROWS = 0, 2, 12, 16

IN_VMEM = pl.BlockSpec(memory_space=pltpu.VMEM)
ANYWHERE = pl.BlockSpec(memory_space=pl.ANY)


def update(weight, gradient, moment, average, step_rate, decay_rate):
    step_grad = gradient + decay_rate * weight
    moment_new = MOMENTUM_RATE * moment + step_grad
    weight_new = weight - step_rate * (step_grad + MOMENTUM_RATE * moment_new)
    return (moment_new, weight_new, AVERAGING * average + (1.0 - AVERAGING) * weight_new)


def swap(value, axis, mask):
    return lax.ppermute(value, axis, [(i, i ^ mask) for i in range(lax.axis_size(axis))])


def line_masks(count):
    masks, mask = [], count // 2
    while mask > 1:
        masks.append(mask)
        mask //= 2
    return masks


def line_order(count):
    order = [0]
    for mask in line_masks(count):
        order = order + [r ^ mask for r in order]
    return order


def z_sets(count):
    order = line_order(count)
    eighth = count // 8
    return order[:eighth], order[eighth : 2 * eighth], order[2 * eighth :]


def flip(order):
    return [r ^ 1 for r in order]


def after(value, *others):
    return lax.optimization_barrier((value, *others))[0]


def both_after(values, *others):
    return lax.optimization_barrier((*values, *others))[: len(values)] if others else values


def over_x(value):
    return swap(value, "head", 2)


def over_y(value):
    return swap(value, "dp", 1)


def over_both(value):
    members = lax.axis_size("head")
    total = members * lax.axis_size("dp")
    return lax.ppermute(value, ("dp", "head"), [(i, i ^ members ^ 2) for i in range(total)])


def over_z(value):
    return swap(value, "dp", 2)


def over_far(value, count):
    return swap(value, "dp", line_masks(count)[-2])


class Gather:
    def __init__(self, shard, count):
        base = shard[None]
        for mask in line_masks(count)[:-2]:
            base = jnp.concatenate([base, swap(base, "dp", mask)])
        self.base, self.count = base, count

    def far(self, *later):
        self.base = both_after((self.base,), *later)[0]
        self.first = jnp.concatenate([self.base, over_far(self.base, self.count)])

    def near(self, *later):
        self.first = both_after((self.first,), *later)[0]
        self.second = over_z(self.first)
        self.x_first, self.y_first = over_x(self.first), over_y(self.first)

    def rest_own(self, *later):
        second, y_first = both_after((self.second, self.y_first), *later)
        self.y_second, self.d_first = over_y(second), over_x(after(y_first, self.x_first))

    def rest_other(self, *later):
        second, d_first = both_after((self.second, self.d_first), self.d_first, *later)
        self.x_second, self.d_second = over_x(second), over_z(d_first)

    def pieces(self):
        base, away, near = z_sets(self.count)
        rels = base + away, near
        own = (self.first, self.second, self.y_first, self.y_second)
        other = (self.x_first, self.x_second, self.d_first, self.d_second)
        turned = tuple(flip(r) for r in rels)
        return tuple(zip(own, rels + turned)), tuple(zip(other, rels + turned))


def joined(pieces, count, me):
    order = [r for _, rel in pieces for r in rel]
    place = jnp.array([order.index(r) for r in range(count)], jnp.int32)
    return jnp.concatenate([a for a, _ in pieces])[place[jnp.arange(count, dtype=jnp.int32) ^ me]]


def part_rels(count):
    base, away, near = z_sets(count)
    own = (base, away, near, flip(near), flip(base + away))
    other = (base + away + near, flip(near), flip(base + away))
    return own, other


def parted(whole, rels, me):
    return tuple(whole[jnp.array(rel, jnp.int32) ^ me] for rel in rels)


def plus(*terms):
    return sum(t.astype(F32) for t in terms)


def low_plus(*terms):
    return plus(*terms).astype(BF16)


class Scatter:
    def __init__(self, count):
        self.count = count

    def own(self, parts, *later):
        self.base, self.away, self.near, y_near, y_rest = parts
        y_near, y_rest = both_after((y_near, y_rest), *later)
        self.from_y_near, self.y_rest = over_y(y_near), y_rest

    def own_rest(self, *later):
        self.from_y = over_y(both_after((self.y_rest,), *later)[0])

    def other(self, parts, *later):
        xs, d_near, self.d_rest = parts
        xs, d_near = both_after((xs, d_near), *later)
        self.from_d, self.from_x = over_z(d_near), over_x(xs)

    def turn(self, *later):
        rest, from_d = both_after((self.d_rest, self.from_d), *later)
        self.from_both = over_both(low_plus(rest, from_d))

    def near_sum(self, *later):
        near = both_after((self.near,), *later)[0]
        cut = 2 * self.base.shape[0]
        self.near_total = low_plus(near, self.from_y_near, self.from_x[cut:])
        self.from_near = over_z(self.near_total)

    def far(self, *later):
        cut = self.base.shape[0]
        away = both_after((self.away,), *later)[0]
        rest = (self.from_y, self.from_both, self.from_near, self.from_x)
        self.away_total = low_plus(away, *(r[cut : 2 * cut] for r in rest))
        self.from_away = over_far(self.away_total, self.count)

    def terms(self):
        cut = self.base.shape[0]
        rest = (self.from_y, self.from_both, self.from_near, self.from_x)
        terms = (self.base, self.from_away, *(r[:cut] for r in rest))
        masks = line_masks(self.count)[:-2]
        if not masks:
            return (self.base, self.from_away, *rest)
        total = plus(*terms)
        for mask in reversed(masks):
            keep = total.shape[0] // 2
            total = total[:keep] + swap(total[keep:].astype(BF16), "dp", mask)
        return (total[:1],)


def dot(a, b):
    return jnp.dot(a, b, preferred_element_type=F32)


def dot_t(a, b):
    return lax.dot_general(a, b, (((1,), (1,)), ((), ())), preferred_element_type=F32)


def t_dot(a, b):
    return lax.dot_general(a, b, (((0,), (0,)), ((), ())), preferred_element_type=F32)


def normalize(inputs):
    mean_row = jnp.mean(inputs, axis=-1, keepdims=True)
    centred = inputs - mean_row
    spread = jnp.mean(centred * centred, axis=-1, keepdims=True)
    inv_std = lax.rsqrt(spread + EPSILON)
    return (centred * inv_std, inv_std)


def norm_back(grad_out, centred, inv_std, gain_row):
    scaled = grad_out * gain_row
    return inv_std * (
        scaled
        - jnp.mean(scaled, axis=-1, keepdims=True)
        - centred * jnp.mean(scaled * centred, axis=-1, keepdims=True)
    )


def piece_copies(info, refs, rels, dest, sems, out=False, at=()):
    copies = []
    for ref, rel in zip(refs, rels):
        for j, r in enumerate(rel):
            rows = ref.shape[-2]
            start = 0 if r is None else pl.multiple_of((info.me ^ r) * rows, rows)
            there, here = ref.at[(j, *at)], dest.at[pl.ds(start, rows)]
            copies.append((here, there) if out else (there, here))
    copies = [
        pltpu.make_async_copy(a, b, sems.at[i]) for i, (a, b) in enumerate(copies)
    ]
    for copy in copies:
        copy.start()
    return copies


def wait_all(copies):
    for copy in copies:
        copy.wait()


class Info:
    def __init__(self, params):
        self.me, self.member = lax.axis_index("dp"), lax.axis_index("head")
        self.slot, self.core = self.member // 2, lax.rem(self.member, 2)
        self.params = params

    def kind(self):
        return self.params[KIND : KIND + 1, 0:1]

    def gain(self, i):
        return self.params[GAINS + i : GAINS + i + 1, :]

    def bias(self, i):
        return self.params[BIASES + i : BIASES + i + 1, :]


class Lazy:
    def __init__(self, source, here, sem):
        self.here, self.shape, self.waits = here, here.shape, True
        self.copy = pltpu.make_async_copy(source, here, sem)

    def start(self):
        self.copy.start()

    def ready(self):
        if self.waits:
            self.copy.wait()
            self.waits = False
        return self.here

    def __getitem__(self, at):
        return self.ready()[at]


class Early:
    def __init__(self, target, here, sem):
        self.here, self.shape, self.dtype, self.stays = here, here.shape, here.dtype, True
        self.copy = pltpu.make_async_copy(here, target, sem)

    def flush(self):
        if self.stays:
            self.copy.start()
            self.stays = False

    def __setitem__(self, at, value):
        self.here[at] = value

    def __getitem__(self, at):
        return self.here[at]


def start_all(values):
    for value in values:
        value.start()


def lanes():
    return lax.broadcasted_iota(jnp.int32, (1, 2 * HEAD_WIDTH), 1)


def segments(shape, axis, start, info):
    run = (lax.broadcasted_iota(jnp.int32, shape, axis) + start) // LOWRES
    return jnp.where(info.kind() > 0.0, 0, run)


def column_sum(rows):
    return jnp.sum(rows, axis=0, keepdims=True)


def cast_kernel(w_qkv, w_proj, w_fc1, w_fc2, attn, mlp):
    wide = 2 * HEAD_WIDTH
    for i in range(3):
        attn[:, i * wide : (i + 1) * wide] = w_qkv[i, :, :wide].astype(BF16)
    single = [w_qkv[i, :, wide:] for i in range(3)]
    proj = w_proj[...].T
    attn[:, 3 * wide : 4 * wide] = jnp.concatenate(single[:2], axis=1).astype(BF16)
    attn[:, 4 * wide : 5 * wide] = jnp.concatenate([single[2], proj[:, wide:]], axis=1).astype(BF16)
    attn[:, 5 * wide : 6 * wide] = proj[:, :wide].astype(BF16)
    mlp[0] = w_fc1[...].astype(BF16)
    mlp[1] = w_fc2[...].astype(BF16)


def prepare_kernel(info, block, a1, a1_t, x_rows, rows):
    share = x_rows.shape[0]
    x = block[...].astype(F32)
    rows[...] = x
    x_rows[...] = rows[pl.ds(pl.multiple_of(info.core * share, 8), share), :]
    x_rows.flush()
    xhat, _ = normalize(x)
    normed = (xhat * info.gain(0) + info.bias(0)).astype(BF16)
    a1[...] = normed
    a1.flush()
    a1_t[...] = normed.T


def join_kernel(info, mine, peer, dy, dy_t, total, rows):
    share = mine.shape[0]
    start = pl.multiple_of(info.core * share, 8)
    own = mine[...].astype(F32)
    rows[pl.ds(start, share), :] = own
    rows[pl.ds(pl.multiple_of(share - start, 8), share), :] = peer[...].astype(F32)
    low = rows[...].astype(BF16)
    dy[...] = low
    dy.flush()
    total[0:1, :] = column_sum(own)
    dy_t[...] = low.T


def attend_kernel(info, a1, bias, *rest, rels, added, group_mask):
    before, rest = rest[:added], rest[added:]
    count = len(rels)
    pieces, (qkv, out, lse, proj, w, sems) = rest[:count], rest[count:]
    copies = piece_copies(info, pieces, rels, w, sems)
    start_all(before)
    wait_all(copies)
    lane = lanes()
    low = lane < HEAD_WIDTH
    zero = jnp.zeros((), BF16)
    bias = bias.ready()[pl.ds(info.member ^ group_mask, 1), :]
    m = dot(a1[...], w[:, :640]) + bias
    k01, v01 = m[:, 128:256].astype(BF16), m[:, 256:384].astype(BF16)
    pair = m[:, 384:512]
    k2 = pltpu.roll(pair, HEAD_WIDTH, 1).astype(BF16)
    v2 = m[:, 512:640].astype(BF16)
    qkv[:, 0:128] = (m[:, 0:128] * SCALE).astype(BF16)
    qkv[:, 128:256] = k01
    qkv[:, 256:384] = v01
    qkv[:, 384:512] = jnp.where(low, pair * SCALE, 0.0).astype(BF16)
    qkv[:, 512:640] = k2
    qkv[:, 640:768] = v2
    qkv.flush()
    columns = segments((1, SLOT_PATCHES), 1, 0, info)
    for start in range(0, SLOT_PATCHES, QUERY_ROWS):
        rows = slice(start, start + QUERY_ROWS)
        seen = segments((QUERY_ROWS, 1), 0, start, info) == columns
        q01 = qkv[rows, 0:128]
        outs, logs = [], []
        for query, keys, value in (
            (jnp.where(low, q01, zero), k01, v01),
            (jnp.where(low, zero, q01), k01, v01),
            (qkv[rows, 384:512], k2, v2),
        ):
            scores = jnp.where(seen, dot_t(query, keys), MASKED)
            largest = jnp.max(scores, axis=-1, keepdims=True)
            expon = jnp.exp(scores - largest)
            summed = jnp.sum(expon, axis=-1, keepdims=True)
            probs = (expon * (1.0 / summed)).astype(BF16)
            outs.append(dot(probs, value))
            logs.append(largest + jnp.log(summed))
        third = jnp.where(low, 0.0, pltpu.roll(outs[2], HEAD_WIDTH, 1))
        out[rows, 0:128] = third.astype(BF16)
        out[rows, 128:256] = jnp.where(low, outs[0], outs[1]).astype(BF16)
        lse[rows, :] = jnp.where(lane == 0, logs[0], jnp.where(lane == 1, logs[1], logs[2]))
    out.flush()
    lse.flush()
    total = dot_t(out[...], w[:, 512:768])
    proj[...] = plus(total, *(b[...] for b in before)).astype(BF16)


def middle_kernel(info, block, mine, peer, h1, a2, a2_t):
    both = plus(mine[...], peer[...])
    middle = block[...].astype(F32) + (both + info.bias(2))
    h1[...] = middle
    h1.flush()
    xhat, _ = normalize(middle)
    normed = (xhat * info.gain(1) + info.bias(1)).astype(BF16)
    a2[...] = normed
    a2.flush()
    a2_t[...] = normed.T


def split_rows(info, total, scratch, share, keep, send, before, at=0):
    start = pl.multiple_of(info.core * share, 8)
    scratch[...] = total
    kept = scratch[pl.ds(start, share), :]
    keep[:share, :] = plus(kept, *(b[:share, :] for b in before[:1])).astype(keep.dtype)
    theirs = scratch[pl.ds(pl.multiple_of(share - start, 8), share), :]
    sent = plus(theirs, *(b[at : at + share, :] for b in before[1:]))
    send[at : at + share, :] = sent.astype(send.dtype)


def mlp_kernel(
    info, a2, a2_t, dy, dy_t, order, *rest, rels, out_rels, group_mask, added, share
):
    before, rest = rest[:added], rest[added:]
    count, outs = len(rels), len(out_rels)
    pieces, rest = rest[:count], rest[count:]
    parts, (keep, send, dbias, w1, w2, dw1, dw2, rows, sems) = rest[:outs], rest[outs:]
    first = piece_copies(info, pieces, rels, w1, sems.at[0], at=(0,))
    second = piece_copies(info, pieces, rels, w2, sems.at[1], at=(1,))
    start_all((dy, dy_t, a2_t, *before))
    wait_all(first)
    bias = info.params.ready()[pl.ds(BIASES + 6 + (info.member ^ group_mask), 1), :]
    u = dot(a2[...], w1[...]) + bias
    phi = 0.5 + 0.5 * lax.erf(u * (2.0**-0.5))
    hidden = (u * phi).astype(BF16)
    slope = phi + u * (jnp.exp(-0.5 * u * u) * 0.3989422804014327)
    wait_all(second)
    dpre = (dot(dy[...], w2[...]) * slope).astype(BF16)
    dw2[...] = dot(dy_t[...], hidden).astype(BF16)
    second = piece_copies(info, parts, out_rels, dw2, sems.at[1], out=True, at=(1,))
    dw1[...] = dot(a2_t[...], dpre).astype(BF16)
    first = piece_copies(info, parts, out_rels, dw1, sems.at[0], out=True, at=(0,))
    da2 = plus(dot_t(dpre, w1[...]), *(b[:SLOT_PATCHES, :] for b in before[1:]))
    send[:SLOT_PATCHES, :] = da2.astype(BF16)
    split_rows(info, dot_t(hidden, w2[...]), rows, share, keep, send, before, SLOT_PATCHES)
    dbias[0:1, :] = column_sum(dpre.astype(F32))
    wait_all(first)
    wait_all(second)


def middle_back(info, h1, dy, mine, peer, kept, e, e_t, dh1_rows, block_out, sums, rows):
    share = block_out.shape[0]
    start = pl.multiple_of(info.core * share, 8)
    xhat, inv_std = normalize(h1[...])
    da2 = plus(mine[:SLOT_PATCHES, :], peer[:SLOT_PATCHES, :])
    dh1 = dy[...].astype(F32) + norm_back(da2, xhat, inv_std, info.gain(1))
    low = dh1.astype(BF16)
    e[...] = low
    e.flush()
    e_t[...] = low.T
    e_t.flush()
    rows[...] = dh1
    dh1_rows[...] = rows[pl.ds(start, share), :]
    dh1_rows.flush()
    sums[0:1, :] = column_sum(da2 * xhat)
    sums[1:2, :] = column_sum(da2)
    sums[2:3, :] = column_sum(dh1)
    sums.flush()
    mlp = plus(kept[:share, :], peer[SLOT_PATCHES : SLOT_PATCHES + share, :])
    block_out[...] = ((h1.ready()[pl.ds(start, share), :] + mlp) + info.bias(3)).astype(BF16)


def first_back_kernel(
    info, h1, dy, mine, peer, kept, a1_t, qkv, out, lse, *rest, rels, out_rels, share
):
    count, outs = len(rels), len(out_rels)
    pieces, rest = rest[:count], rest[count:]
    parts, rest = rest[:outs], rest[outs:]
    keep, send, sums, e, e_t, dh1_rows, block_out, mid, w, dw, grads, rows, sems = rest
    copies = piece_copies(info, pieces, rels, w, sems)
    start_all((qkv, lse, out, a1_t))
    middle_back(info, h1, dy, mine, peer, kept, e, e_t, dh1_rows, block_out, mid, rows)
    wait_all(copies)
    attend_back(
        info, e, e_t, a1_t, qkv, out, lse, (), parts, out_rels, share, keep, send, sums,
        w, dw, grads, rows, sems,
    )


def second_back_kernel(
    info, e, e_t, a1_t, qkv, out, lse, kept, sent, *rest, rels, out_rels, share
):
    count, outs = len(rels), len(out_rels)
    pieces, rest = rest[:count], rest[count:]
    parts, (keep, send, sums, w, dw, grads, rows, sems) = rest[:outs], rest[outs:]
    copies = piece_copies(info, pieces, rels, w, sems)
    start_all((qkv, lse, out, a1_t, e_t, kept, sent))
    wait_all(copies)
    attend_back(
        info, e, e_t, a1_t, qkv, out, lse, (kept, sent), parts, out_rels, share, keep, send, sums,
        w, dw, grads, rows, sems,
    )


def attend_back(
    info, e, e_t, a1_t, qkv, out, lse, before, parts, out_rels, share, keep, send, sums,
    w, dw, grads, rows, sems,
):
    low = lanes() < HEAD_WIDTH
    zero = jnp.zeros((), BF16)
    dout = dot(e[...], w[:, 512:768])
    do2 = jnp.where(low, pltpu.roll(dout[:, 0:128], HEAD_WIDTH, 1), 0.0).astype(BF16)
    do01 = dout[:, 128:256].astype(BF16)
    q01, k01, v01 = qkv[:, 0:128], qkv[:, 128:256], qkv[:, 256:384]
    q2, k2, v2 = qkv[:, 384:512], qkv[:, 512:640], qkv[:, 640:768]
    lse_t = jnp.transpose(lse[...], (1, 0))
    seen = segments((SLOT_PATCHES, 1), 0, 0, info) == segments((1, SLOT_PATCHES), 1, 0, info)
    dq, dk, dv = [], [], []
    for head, (query, keys, value, dcontext) in enumerate(
        (
            (q01, jnp.where(low, k01, zero), jnp.where(low, v01, zero), do01),
            (q01, jnp.where(low, zero, k01), jnp.where(low, zero, v01), do01),
            (q2, k2, jnp.where(low, v2, zero), do2),
        )
    ):
        scores = jnp.where(seen, dot_t(keys, query), MASKED)
        probs = jnp.exp(scores - lse_t[head : head + 1, :])
        dprob = dot_t(value, dcontext)
        row_dot = column_sum(probs * dprob)
        dscore = (probs * (dprob - row_dot)).astype(BF16)
        dv.append(dot(probs.astype(BF16), dcontext))
        dk.append(dot(dscore, query))
        dq.append(t_dot(dscore, keys))
    grads[:, 0:128] = (jnp.where(low, dq[0], dq[1]) * SCALE).astype(BF16)
    grads[:, 128:256] = jnp.where(low, dk[0], dk[1]).astype(BF16)
    grads[:, 256:384] = jnp.where(low, dv[0], dv[1]).astype(BF16)
    shifted = pltpu.roll(dk[2], HEAD_WIDTH, 1)
    grads[:, 384:512] = jnp.where(low, dq[2] * SCALE, shifted).astype(BF16)
    grads[:, 512:640] = jnp.where(low, dv[2], 0.0).astype(BF16)
    dw[:, 0:512] = dot(a1_t[...], grads[:, 0:512]).astype(BF16)
    dw[:, 512:640] = (dot(a1_t[...], grads[:, 512:640]) + dot(e_t[...], out[:, 0:128])).astype(BF16)
    dw[:, 640:768] = dot(e_t[...], out[:, 128:256]).astype(BF16)
    copies = piece_copies(info, parts, out_rels, dw, sems, out=True)
    split_rows(info, dot_t(grads[...], w[:, 0:640]), rows, share, keep, send, before)
    sums[0:1, :] = column_sum(grads[...].astype(F32))
    wait_all(copies)


def last_kernel(
    info, x_rows, dh1_rows, mine, kept, peer, mid, db0, db1, s0, s1, input_grad, small
):
    share = x_rows.shape[0]
    xhat, inv_std = normalize(x_rows[...])
    da1 = plus(kept[:share, :], peer[:share, :])
    input_grad[...] = dh1_rows[...] + norm_back(da1, xhat, inv_std, info.gain(0))
    input_grad.flush()
    once = jnp.where(info.core == 0, 1.0, 0.0)
    member = info.member
    small[...] = jnp.zeros(small.shape, F32)
    small[0:1, :] = column_sum(da1 * xhat)
    small[1:2, :] = once * mid[0:1, :]
    small[2:3, :] = column_sum(da1)
    small[3:4, :] = once * mid[1:2, :]
    small[4:5, :] = once * mid[2:3, :]
    small[5:6, :] = mine[0:1, :]
    low = lanes() < HEAD_WIDTH
    for row, pair, single in ((6, 0, 384), (7, 256, 512)):
        for group in range(0, 4, 2):
            even, odd = (
                tuple(
                    jnp.where(
                        member == which,
                        s0[0:1, at : at + 128],
                        jnp.where(member == which ^ 2, s1[0:1, at : at + 128], 0.0),
                    )
                    for at in (pair, single)
                )
                for which in (group, group + 1)
            )
            turned = pltpu.roll(odd[0], HEAD_WIDTH, 1)
            at = group * 192
            small[row : row + 1, at : at + 128] = even[0]
            small[row : row + 1, at + 128 : at + 256] = jnp.where(low, even[1], turned)
            small[row : row + 1, at + 256 : at + 384] = jnp.where(
                low, turned, pltpu.roll(odd[1], HEAD_WIDTH, 1)
            )
    small[pl.ds(8 + member, 1), :] = db0[0:1, :]
    small[pl.ds(8 + (member ^ 2), 1), :] = db1[0:1, :]


def step(weight, gradient, moment, average, outs, rate):
    for ref, value in zip(
        outs, (gradient, *update(weight, gradient, moment, average, rate, WEIGHT_DECAY))
    ):
        ref[...] = value.reshape(ref.shape)


def finish_mlp_kernel(w1, m1, a1, w2, m2, a2, *rest):
    terms, outs = rest[:-8], rest[-8:]
    first, second = (plus(*(t[0, i] for t in terms)) for i in range(2))
    step(w1[...], first, m1[...], a1[...], outs[:4], RATE_FC1)
    step(w2[...], second, m2[...], a2[...], outs[4:], RATE_FC2)


def finish_attn_kernel(w1, m1, a1, w2, m2, a2, *rest):
    terms, outs = rest[:-8], rest[-8:]
    total = plus(*(t[0] for t in terms))
    wide = 2 * HEAD_WIDTH
    for i in range(3):
        single = 3 * wide + i * HEAD_WIDTH
        gradient = jnp.concatenate(
            [total[:, i * wide : (i + 1) * wide], total[:, single : single + HEAD_WIDTH]], axis=1
        )
        step(w1[i], gradient, m1[i], a1[i], [o.at[i] for o in outs[:4]], RATE_QKV)
    gradient = jnp.concatenate(
        [total[:, 5 * wide :], total[:, 5 * wide - HEAD_WIDTH : 5 * wide]], axis=1
    ).T
    step(w2[...], gradient, m2[...], a2[...], outs[4:], RATE_PROJ)


def call(kernel, name, outs, inputs, specs=None, scratch=(), flops=0, lazy=(), views=None, **fixed):
    results = [jax.ShapeDtypeStruct(s, d) for s, d, *_ in outs]
    specs, views = specs or {}, views or {}
    brought = [i for i in range(len(inputs)) if i not in specs]
    sent = [i for i, entry in enumerate(outs) if len(entry) == 2]
    moved = [jax.ShapeDtypeStruct(views[i][0], v.dtype) if i in views else v for i, v in enumerate(inputs)]
    moved = [moved[i] for i in brought] + [results[i] for i in sent]
    extra = [pltpu.VMEM(v.shape, v.dtype) for v in moved] + [pltpu.SemaphoreType.DMA((len(moved),))]
    size = sum(v.size * v.dtype.itemsize for v in (*inputs, *results))

    def body(*refs):
        refs = list(refs)
        cut = len(refs) - len(extra)
        here, sems = refs[cut:], refs[-1]
        info = Info(None)
        for n, i in enumerate(brought):
            source = views[i][1](refs[i], info) if i in views else refs[i]
            refs[i] = Lazy(source, here[n], sems.at[n])
            if i not in lazy:
                refs[i].start()
        leaving = []
        for n, i in enumerate(sent, len(brought)):
            refs[len(inputs) + i] = Early(refs[len(inputs) + i], here[n], sems.at[n])
            leaving.append(refs[len(inputs) + i])
        info.params = refs[0]
        kernel(info, *refs[1:cut], **fixed)
        info.params.ready()
        for value in leaving:
            value.flush()
        for value in leaving:
            value.copy.wait()

    body.__name__ = name
    return pl.pallas_call(
        body,
        out_shape=results,
        in_specs=[specs.get(i, ANYWHERE) for i in range(len(inputs))],
        out_specs=[entry[2] if len(entry) > 2 else ANYWHERE for entry in outs],
        scratch_shapes=[*scratch, *extra],
        compiler_params=pltpu.CompilerParams(vmem_limit_bytes=VMEM_LIMIT),
        cost_estimate=pl.CostEstimate(flops=flops // COST, bytes_accessed=size // COST, transcendentals=0),
        name=name,
    )(*inputs)


def block_call(kernel, name, outs, inputs):
    return pl.pallas_call(
        kernel,
        out_shape=[jax.ShapeDtypeStruct(s, d) for s, d in outs],
        in_specs=[IN_VMEM] * len(inputs),
        out_specs=[IN_VMEM] * len(outs),
        compiler_params=pltpu.CompilerParams(vmem_limit_bytes=VMEM_LIMIT),
        cost_estimate=pl.CostEstimate(flops=0, bytes_accessed=1 << 20, transcendentals=0),
        name=name,
    )(*inputs)


def shards(
    block_in,
    resolution,
    cotangent,
    w_qkv,
    w_proj,
    w_fc1,
    w_fc2,
    mom_qkv,
    mom_proj,
    mom_fc1,
    mom_fc2,
    avg_qkv,
    avg_proj,
    avg_fc1,
    avg_fc2,
    gains,
    gain_mom,
    gain_avg,
    biases,
    bias_mom,
    bias_avg,
):
    members = lax.axis_size("head")
    count = lax.axis_size("dp")
    member = lax.axis_index("head")
    me = lax.axis_index("dp")
    slot = member // 2
    width = block_in.shape[1]
    head_cols = w_qkv.shape[2]
    hidden_cols = w_fc1.shape[1]
    share = cotangent.shape[0]
    padded = -(-share // 16) * 16
    shard_rows = w_qkv.shape[0]
    aligned = shard_rows % 16 == 0
    paired = 2 * HEAD_WIDTH
    kind = lax.dynamic_index_in_dim(resolution, slot, keepdims=False)
    bias_rows = biases.reshape(-1, width)
    params = jnp.concatenate(
        [
            gains,
            bias_rows,
            jnp.full((PARAM_ROWS - KIND, width), kind.astype(F32)),
        ]
    )

    attn_shard, mlp_shard = block_call(
        cast_kernel,
        "cast",
        [((shard_rows, width), BF16), ((2, shard_rows, width), BF16)],
        (jnp.swapaxes(w_qkv, 0, 1), w_proj, w_fc1, w_fc2.T),
    )
    attn_w, mlp_w = Gather(attn_shard, count), Gather(mlp_shard, count)
    attn_w.far()

    def settle(pieces, stacked):
        if aligned:
            return pieces
        whole = joined(pieces, count, me)
        if stacked:
            whole = jnp.swapaxes(whole, 0, 1).reshape(1, 2, width, width)
        else:
            whole = whole.reshape(1, width, width)
        return ((whole, (None,)),)

    own_rels, other_rels = part_rels(count)
    part_rows = shard_rows if aligned else width

    def written(rels):
        return rels if aligned else ((None,),)

    def parts(stacked, pieces, rels):
        if aligned:
            return tuple(pieces)
        whole = pieces[0][0]
        if stacked:
            whole = jnp.swapaxes(whole.reshape(2, count, shard_rows, width), 0, 1)
        else:
            whole = whole.reshape(count, shard_rows, width)
        return parted(whole, rels, me)

    q_bias, v_bias = (bias_rows[i].reshape(members, head_cols) for i in (4, 5))
    none = jnp.zeros_like(q_bias)
    group_bias = jnp.concatenate(
        [
            q_bias[:, :paired],
            none[:, :paired],
            v_bias[:, :paired],
            q_bias[:, paired:],
            none[:, paired:],
            v_bias[:, paired:],
            none[:, paired:],
        ],
        axis=1,
    )
    group_bias = jnp.concatenate([group_bias, group_bias])
    tall, turned = (SLOT_PATCHES, width), (width, SLOT_PATCHES)

    def of_slot(ref, info):
        return ref.at[pl.ds(pl.multiple_of(info.slot * SLOT_PATCHES, 16), SLOT_PATCHES)]

    a1, a1_t, x_rows = call(
        prepare_kernel,
        "prepare",
        [(tall, BF16), (turned, BF16), ((share, width), F32)],
        (params, block_in),
        views={1: (tall, of_slot)},
        scratch=[pltpu.VMEM(tall, F32)],
    )
    dy, dy_t, dy_sum = call(
        join_kernel,
        "join",
        [(tall, BF16), (turned, BF16), ((8, width), F32)],
        (params, cotangent, swap(cotangent, "head", 1)),
        specs={1: IN_VMEM, 2: IN_VMEM},
        scratch=[pltpu.VMEM(tall, F32)],
    )

    attn_w.near(a1)
    attn_w.rest_own()
    attn_w.rest_other()
    mlp_w.far(attn_w.d_first)
    attn_own, attn_other = (settle(p, False) for p in attn_w.pieces())

    def attend(pieces, group_mask, a1, *before):
        return call(
            attend_kernel,
            "attend",
            [
                (tall, BF16),
                ((SLOT_PATCHES, 2 * paired), BF16),
                ((SLOT_PATCHES, paired), F32),
                (tall, BF16),
            ],
            (params, a1, group_bias, *before, *(a for a, _ in pieces)),
            specs={i + len(before): ANYWHERE for i in range(3, 3 + len(pieces))},
            lazy=range(3, 3 + len(before)),
            scratch=[pltpu.VMEM((width, width), BF16), pltpu.SemaphoreType.DMA((count,))],
            flops=2 * SLOT_PATCHES * (width * width + 12 * SLOT_PATCHES * HEAD_WIDTH),
            rels=[r for _, r in pieces],
            added=len(before),
            group_mask=group_mask,
        )

    own_saved = attend(attn_own, 0, a1)
    mlp_w.near(own_saved[3], attn_w.x_second, attn_w.d_second)
    other_saved = attend(attn_other, 2, after(a1, mlp_w.first), own_saved[3])
    mlp_w.rest_own(other_saved[3])
    proj = after(other_saved[3], mlp_w.second, mlp_w.x_first, mlp_w.y_first)
    h1, a2, a2_t = call(
        middle_kernel,
        "middle",
        [(tall, F32), (tall, BF16), (turned, BF16)],
        (
            params,
            block_in,
            proj,
            swap(proj, "head", 1),
        ),
        views={1: (tall, of_slot)},
    )

    def mlp(pieces, group_mask, rels, order, *before):
        first = 6 + len(before)
        *grads, keep, send, dbias = call(
            mlp_kernel,
            "mlp",
            [((len(r), 2, part_rows, width), BF16, ANYWHERE) for r in written(rels)]
            + [
                ((padded, width), BF16),
                ((SLOT_PATCHES + padded, width), BF16),
                ((8, hidden_cols), F32),
            ],
            (params, a2, a2_t, dy, dy_t, order, *before, *(a for a, _ in pieces)),
            specs={i: ANYWHERE for i in (5, *range(first, first + len(pieces)))},
            lazy=(2, 3, 4, *range(6, first)),
            scratch=[pltpu.VMEM((width, hidden_cols), BF16) for _ in range(4)]
            + [pltpu.VMEM(tall, F32), pltpu.SemaphoreType.DMA((2, count))],
            flops=12 * SLOT_PATCHES * width * hidden_cols,
            rels=[r for _, r in pieces],
            out_rels=written(rels),
            group_mask=group_mask,
            added=len(before),
            share=share,
        )
        return parts(True, grads, rels), keep, send, dbias

    mlp_w.rest_other(a2, dy_t)
    mlp_own, mlp_other = (settle(p, True) for p in mlp_w.pieces())
    mlp_sum, attn_sum = Scatter(count), Scatter(count)
    own_mlp = mlp(mlp_own, 0, own_rels, after(params, mlp_w.d_first))
    mlp_sum.own(own_mlp[0])
    mlp_sum.own_rest()
    other_mlp = mlp(mlp_other, 2, other_rels, own_mlp[3], own_mlp[1], own_mlp[2])
    peer_mlp = swap(other_mlp[2], "head", 1)
    mlp_sum.other(other_mlp[0], peer_mlp)
    back_outs = [((padded, width), BF16), ((padded, width), BF16), ((8, 5 * paired), F32)]
    back_scratch = [
        pltpu.VMEM((width, width), BF16),
        pltpu.VMEM((width, width), BF16),
        pltpu.VMEM((SLOT_PATCHES, 5 * paired), BF16),
        pltpu.VMEM(tall, F32),
        pltpu.SemaphoreType.DMA((count,)),
    ]
    back_flops = 2 * SLOT_PATCHES * (2 * width * width + 60 * SLOT_PATCHES * HEAD_WIDTH)

    def back_parts(rels):
        return [((len(r), part_rows, width), BF16, ANYWHERE) for r in written(rels)]

    *grads, keep, send, sums, e, e_t, dh1_rows, block_out, mid_sums = call(
        first_back_kernel,
        "first_back",
        back_parts(other_rels)
        + back_outs
        + [
            (tall, BF16),
            (turned, BF16),
            ((share, width), F32),
            ((share, width), BF16, IN_VMEM),
            ((8, width), F32),
        ],
        (
            params,
            h1,
            dy,
            other_mlp[2],
            peer_mlp,
            other_mlp[1],
            a1_t,
            *other_saved[:3],
            *(a for a, _ in attn_other),
        ),
        specs={i: ANYWHERE for i in range(10, 10 + len(attn_other))},
        lazy=(6, 7, 8, 9),
        scratch=back_scratch,
        flops=back_flops,
        rels=[r for _, r in attn_other],
        out_rels=written(other_rels),
        share=share,
    )
    other_back = parts(False, grads, other_rels), keep, send, sums
    attn_sum.other(other_back[0])
    mlp_sum.turn(e)
    mlp_sum.near_sum(other_back[3], mlp_sum.from_y)
    *grads, keep, send, sums = call(
        second_back_kernel,
        "second_back",
        back_parts(own_rels) + back_outs,
        (
            params,
            e,
            e_t,
            a1_t,
            *own_saved[:3],
            *other_back[1:3],
            *(a for a, _ in attn_own),
        ),
        specs={i: ANYWHERE for i in range(9, 9 + len(attn_own))},
        lazy=(2, 3, 4, 5, 6, 7, 8),
        scratch=back_scratch,
        flops=back_flops,
        rels=[r for _, r in attn_own],
        out_rels=written(own_rels),
        share=share,
    )
    own_back = parts(False, grads, own_rels), keep, send, sums
    done = (mlp_sum.from_near, mlp_sum.from_both, attn_sum.from_x, attn_sum.from_d)
    mlp_sum.far()
    peer_back = swap(after(own_back[2], *done, mlp_sum.away_total), "head", 1)
    attn_sum.own(own_back[0], peer_back)
    input_grad, small = call(
        last_kernel,
        "last",
        [((share, width), F32), ((PARAM_ROWS, width), F32)],
        (
            params,
            x_rows,
            dh1_rows,
            dy_sum,
            own_back[1],
            peer_back,
            mid_sums,
            own_mlp[3],
            other_mlp[3],
            own_back[3],
            other_back[3],
        ),
    )
    attn_sum.turn(input_grad)
    attn_sum.own_rest(input_grad)
    attn_sum.near_sum(input_grad)
    by_row = (3, shard_rows, head_cols)
    fc1, fc2 = w_fc1.shape, w_fc2.T.shape
    *fc1_outs, fc2_grad, fc2_mom, fc2_new, fc2_avg = block_call(
        finish_mlp_kernel,
        "finish_mlp",
        [(fc1, F32)] * 4 + [(fc2, F32)] * 4,
        (
            w_fc1,
            mom_fc1,
            avg_fc1,
            w_fc2.T,
            mom_fc2.T,
            avg_fc2.T,
            *mlp_sum.terms(),
        ),
    )
    fc1_grad, fc1_mom, fc1_new, fc1_avg = fc1_outs
    attn_sum.far(fc1_grad)
    fc2_grad, fc2_mom, fc2_new, fc2_avg = (v.T for v in (fc2_grad, fc2_mom, fc2_new, fc2_avg))
    small = small + swap(small, "head", 1)
    small = after(small, mlp_sum.from_away)
    over = over_x(small), over_y(small), over_both(small)
    small = (small + over[0]) + (over[1] + over[2])
    for mask in line_masks(count):
        if mask == 2:
            small = after(small, attn_sum.from_away)
        small = small + swap(small, "dp", mask)
    gain_grad = small[:2]
    bias_grad = small[2:12].reshape(biases.shape)

    *qkv_outs, proj_grad, proj_mom, proj_new, proj_avg = block_call(
        finish_attn_kernel,
        "finish_attn",
        [(by_row, F32)] * 4 + [(w_proj.shape, F32)] * 4,
        (
            *(jnp.swapaxes(v, 0, 1) for v in (w_qkv, mom_qkv, avg_qkv)),
            w_proj,
            mom_proj,
            avg_proj,
            *attn_sum.terms(),
        ),
    )
    qkv_grad, qkv_mom, qkv_new, qkv_avg = (jnp.swapaxes(v, 0, 1) for v in qkv_outs)

    gain_mom_new, gain_new, gain_avg_new = update(
        gains, gain_grad, gain_mom, gain_avg, RATE_SMALL, 0.0
    )
    bias_mom_new, bias_new, bias_avg_new = update(
        biases, bias_grad, bias_mom, bias_avg, RATE_SMALL, 0.0
    )
    return (
        block_out,
        input_grad,
        qkv_grad,
        qkv_mom,
        qkv_new,
        qkv_avg,
        proj_grad,
        proj_mom,
        proj_new,
        proj_avg,
        fc1_grad,
        fc1_mom,
        fc1_new,
        fc1_avg,
        fc2_grad,
        fc2_mom,
        fc2_new,
        fc2_avg,
        gain_grad,
        gain_mom_new,
        gain_new,
        gain_avg_new,
        bias_grad,
        bias_mom_new,
        bias_new,
        bias_avg_new,
    )
def solution(mesh):
    return jax.shard_map(
        shards,
        mesh=mesh,
        in_specs=(
            P("dp", None),
            P("dp"),
            P(("dp", "head"), None),
            P("dp", None, "head"),
            P("head", "dp"),
            P("dp", "head"),
            P("head", "dp"),
            P("dp", None, "head"),
            P("head", "dp"),
            P("dp", "head"),
            P("head", "dp"),
            P("dp", None, "head"),
            P("head", "dp"),
            P("dp", "head"),
            P("head", "dp"),
            P(),
            P(),
            P(),
            P(),
            P(),
            P(),
        ),
        out_specs=(
            P(("dp", "head"), None),
            P(("dp", "head"), None),
            P("dp", None, "head"),
            P("dp", None, "head"),
            P("dp", None, "head"),
            P("dp", None, "head"),
            P("head", "dp"),
            P("head", "dp"),
            P("head", "dp"),
            P("head", "dp"),
            P("dp", "head"),
            P("dp", "head"),
            P("dp", "head"),
            P("dp", "head"),
            P("head", "dp"),
            P("head", "dp"),
            P("head", "dp"),
            P("head", "dp"),
            P(),
            P(),
            P(),
            P(),
            P(),
            P(),
            P(),
            P(),
        ),
        check_vma=False,
    )
```

```python
import jax
import jax.numpy as jnp
from jax import lax
from jax.experimental import pallas as pl
from jax.experimental.pallas import tpu as pltpu
from jax.sharding import PartitionSpec as P

HEAD_WIDTH = 64
SLOT_PATCHES = 784
LOWRES = 196


EPSILON = 1e-06
MOMENTUM_RATE = 0.9
AVERAGING = 0.75
WEIGHT_DECAY = 0.05
RATE_QKV = 0.001
RATE_PROJ = 0.01
RATE_FC1 = 0.0006
RATE_FC2 = 0.0003
RATE_SMALL = 0.003
MASKED = -1e30
SCALE = HEAD_WIDTH**-0.5
F32 = jnp.float32
BF16 = jnp.bfloat16
QUERY_ROWS = SLOT_PATCHES // 2
VMEM_LIMIT = 60 << 20
COST = 16
GAINS, BIASES, KIND, PARAM_ROWS = 0, 2, 12, 16

IN_VMEM = pl.BlockSpec(memory_space=pltpu.VMEM)
ANYWHERE = pl.BlockSpec(memory_space=pl.ANY)


def update(weight, gradient, moment, average, step_rate, decay_rate):
    step_grad = gradient + decay_rate * weight
    moment_new = MOMENTUM_RATE * moment + step_grad
    weight_new = weight - step_rate * (step_grad + MOMENTUM_RATE * moment_new)
    return (moment_new, weight_new, AVERAGING * average + (1.0 - AVERAGING) * weight_new)


def swap(value, axis, mask):
    return lax.ppermute(value, axis, [(i, i ^ mask) for i in range(lax.axis_size(axis))])


def line_masks(count):
    masks, mask = [], count // 2
    while mask > 1:
        masks.append(mask)
        mask //= 2
    return masks


def line_order(count):
    order = [0]
    for mask in line_masks(count):
        order = order + [r ^ mask for r in order]
    return order


def z_sets(count):
    order = line_order(count)
    eighth = count // 8
    return order[:eighth], order[eighth : 2 * eighth], order[2 * eighth :]


def flip(order):
    return [r ^ 1 for r in order]


def after(value, *others):
    return lax.optimization_barrier((value, *others))[0]


def both_after(values, *others):
    return lax.optimization_barrier((*values, *others))[: len(values)] if others else values


def over_x(value):
    return swap(value, "head", 2)


def over_y(value):
    return swap(value, "dp", 1)


def over_both(value):
    members = lax.axis_size("head")
    total = members * lax.axis_size("dp")
    return lax.ppermute(value, ("dp", "head"), [(i, i ^ members ^ 2) for i in range(total)])


def over_z(value):
    return swap(value, "dp", 2)


def over_far(value, count):
    return swap(value, "dp", line_masks(count)[-2])


class Gather:
    def __init__(self, shard, count):
        base = shard[None]
        for mask in line_masks(count)[:-2]:
            base = jnp.concatenate([base, swap(base, "dp", mask)])
        self.base, self.count = base, count

    def far(self, *later):
        self.base = both_after((self.base,), *later)[0]
        self.first = jnp.concatenate([self.base, over_far(self.base, self.count)])

    def near(self, *later):
        self.first = both_after((self.first,), *later)[0]
        self.second = over_z(self.first)
        self.x_first, self.y_first = over_x(self.first), over_y(self.first)

    def rest_own(self, *later):
        second, y_first = both_after((self.second, self.y_first), *later)
        self.y_second, self.d_first = over_y(second), over_x(after(y_first, self.x_first))

    def rest_other(self, *later):
        second, d_first = both_after((self.second, self.d_first), self.d_first, *later)
        self.x_second, self.d_second = over_x(second), over_z(d_first)

    def pieces(self):
        base, away, near = z_sets(self.count)
        rels = base + away, near
        own = (self.first, self.second, self.y_first, self.y_second)
        other = (self.x_first, self.x_second, self.d_first, self.d_second)
        turned = tuple(flip(r) for r in rels)
        return tuple(zip(own, rels + turned)), tuple(zip(other, rels + turned))


def joined(pieces, count, me):
    order = [r for _, rel in pieces for r in rel]
    place = jnp.array([order.index(r) for r in range(count)], jnp.int32)
    return jnp.concatenate([a for a, _ in pieces])[place[jnp.arange(count, dtype=jnp.int32) ^ me]]


def part_rels(count):
    base, away, near = z_sets(count)
    own = (base, away, near, flip(near), flip(base + away))
    other = (base + away + near, flip(near), flip(base + away))
    return own, other


def parted(whole, rels, me):
    return tuple(whole[jnp.array(rel, jnp.int32) ^ me] for rel in rels)


def plus(*terms):
    return sum(t.astype(F32) for t in terms)


def low_plus(*terms):
    return plus(*terms).astype(BF16)


class Scatter:
    def __init__(self, count):
        self.count = count

    def own(self, parts, *later):
        self.base, self.away, self.near, y_near, y_rest = parts
        y_near, y_rest = both_after((y_near, y_rest), *later)
        self.from_y_near, self.y_rest = over_y(y_near), y_rest

    def own_rest(self, *later):
        self.from_y = over_y(both_after((self.y_rest,), *later)[0])

    def turn_by_x(self, *later):
        rest, from_d = both_after((self.d_rest, self.from_d), *later)
        self.from_both, self.to_y = None, over_x(low_plus(rest, from_d))

    def own_rest_joined(self, *later):
        rest, to_y = both_after((self.y_rest, self.to_y), *later)
        self.from_y = over_y(low_plus(rest, to_y))

    def arrived(self):
        every = (self.from_y, self.from_both, self.from_near, self.from_x)
        return tuple(v for v in every if v is not None)

    def other(self, parts, *later):
        xs, d_near, self.d_rest = parts
        xs, d_near = both_after((xs, d_near), *later)
        self.from_d, self.from_x = over_z(d_near), over_x(xs)

    def turn(self, *later):
        rest, from_d = both_after((self.d_rest, self.from_d), *later)
        self.from_both = over_both(low_plus(rest, from_d))

    def near_sum(self, *later):
        near = both_after((self.near,), *later)[0]
        cut = 2 * self.base.shape[0]
        self.near_total = low_plus(near, self.from_y_near, self.from_x[cut:])
        self.from_near = over_z(self.near_total)

    def far(self, *later):
        cut = self.base.shape[0]
        away = both_after((self.away,), *later)[0]
        rest = self.arrived()
        self.away_total = low_plus(away, *(r[cut : 2 * cut] for r in rest))
        self.from_away = over_far(self.away_total, self.count)

    def terms(self):
        cut = self.base.shape[0]
        rest = self.arrived()
        terms = (self.base, self.from_away, *(r[:cut] for r in rest))
        masks = line_masks(self.count)[:-2]
        if not masks:
            return (self.base, self.from_away, *rest)
        total = plus(*terms)
        for mask in reversed(masks):
            keep = total.shape[0] // 2
            total = total[:keep] + swap(total[keep:].astype(BF16), "dp", mask)
        return (total[:1],)


def dot(a, b):
    return jnp.dot(a, b, preferred_element_type=F32)


def dot_t(a, b):
    return lax.dot_general(a, b, (((1,), (1,)), ((), ())), preferred_element_type=F32)


def t_dot(a, b):
    return lax.dot_general(a, b, (((0,), (0,)), ((), ())), preferred_element_type=F32)


def normalize(inputs):
    mean_row = jnp.mean(inputs, axis=-1, keepdims=True)
    centred = inputs - mean_row
    spread = jnp.mean(centred * centred, axis=-1, keepdims=True)
    inv_std = lax.rsqrt(spread + EPSILON)
    return (centred * inv_std, inv_std)


def norm_back(grad_out, centred, inv_std, gain_row):
    scaled = grad_out * gain_row
    return inv_std * (
        scaled
        - jnp.mean(scaled, axis=-1, keepdims=True)
        - centred * jnp.mean(scaled * centred, axis=-1, keepdims=True)
    )


def piece_copies(info, refs, rels, dest, sems, out=False, at=()):
    copies = []
    for ref, rel in zip(refs, rels):
        for j, r in enumerate(rel):
            rows = ref.shape[-2]
            start = 0 if r is None else pl.multiple_of((info.me ^ r) * rows, rows)
            there, here = ref.at[(j, *at)], dest.at[pl.ds(start, rows)]
            copies.append((here, there) if out else (there, here))
    copies = [
        pltpu.make_async_copy(a, b, sems.at[i]) for i, (a, b) in enumerate(copies)
    ]
    for copy in copies:
        copy.start()
    return copies


def wait_all(copies):
    for copy in copies:
        copy.wait()


class Info:
    def __init__(self, params):
        self.me, self.member = lax.axis_index("dp"), lax.axis_index("head")
        self.slot, self.core = self.member // 2, lax.rem(self.member, 2)
        self.params = params

    def kind(self):
        return self.params[KIND : KIND + 1, 0:1]

    def gain(self, i):
        return self.params[GAINS + i : GAINS + i + 1, :]

    def bias(self, i):
        return self.params[BIASES + i : BIASES + i + 1, :]


class Lazy:
    def __init__(self, source, here, sem):
        self.here, self.shape, self.waits = here, here.shape, True
        self.copy = pltpu.make_async_copy(source, here, sem)

    def start(self):
        self.copy.start()

    def ready(self):
        if self.waits:
            self.copy.wait()
            self.waits = False
        return self.here

    def __getitem__(self, at):
        return self.ready()[at]


class Early:
    def __init__(self, target, here, sem):
        self.here, self.shape, self.dtype, self.stays = here, here.shape, here.dtype, True
        self.copy = pltpu.make_async_copy(here, target, sem)

    def flush(self):
        if self.stays:
            self.copy.start()
            self.stays = False

    def __setitem__(self, at, value):
        self.here[at] = value

    def __getitem__(self, at):
        return self.here[at]


def start_all(values):
    for value in values:
        value.start()


def lanes():
    return lax.broadcasted_iota(jnp.int32, (1, 2 * HEAD_WIDTH), 1)


def segments(shape, axis, start, info):
    run = (lax.broadcasted_iota(jnp.int32, shape, axis) + start) // LOWRES
    return jnp.where(info.kind() > 0.0, 0, run)


def column_sum(rows):
    return jnp.sum(rows, axis=0, keepdims=True)


def cast_kernel(w_qkv, w_proj, w_fc1, w_fc2, attn, mlp):
    wide = 2 * HEAD_WIDTH
    for i in range(3):
        attn[:, i * wide : (i + 1) * wide] = w_qkv[i, :, :wide].astype(BF16)
    single = [w_qkv[i, :, wide:] for i in range(3)]
    proj = w_proj[...].T
    attn[:, 3 * wide : 4 * wide] = jnp.concatenate(single[:2], axis=1).astype(BF16)
    attn[:, 4 * wide : 5 * wide] = jnp.concatenate([single[2], proj[:, wide:]], axis=1).astype(BF16)
    attn[:, 5 * wide : 6 * wide] = proj[:, :wide].astype(BF16)
    mlp[0] = w_fc1[...].astype(BF16)
    mlp[1] = w_fc2[...].astype(BF16)


def prepare_kernel(info, block, a1, a1_t, x_rows, rows):
    share = x_rows.shape[0]
    x = block[...].astype(F32)
    rows[...] = x
    x_rows[...] = rows[pl.ds(pl.multiple_of(info.core * share, 8), share), :]
    x_rows.flush()
    xhat, _ = normalize(x)
    normed = (xhat * info.gain(0) + info.bias(0)).astype(BF16)
    a1[...] = normed
    a1.flush()
    a1_t[...] = normed.T


def join_kernel(info, mine, peer, dy, dy_t, total, rows):
    share = mine.shape[0]
    start = pl.multiple_of(info.core * share, 8)
    own = mine[...].astype(F32)
    rows[pl.ds(start, share), :] = own
    rows[pl.ds(pl.multiple_of(share - start, 8), share), :] = peer[...].astype(F32)
    low = rows[...].astype(BF16)
    dy[...] = low
    dy.flush()
    total[0:1, :] = column_sum(own)
    dy_t[...] = low.T


def attend_kernel(info, a1, bias, *rest, rels, added, group_mask):
    before, rest = rest[:added], rest[added:]
    count = len(rels)
    pieces, (qkv, out, lse, proj, w, sems) = rest[:count], rest[count:]
    copies = piece_copies(info, pieces, rels, w, sems)
    start_all(before)
    wait_all(copies)
    lane = lanes()
    low = lane < HEAD_WIDTH
    zero = jnp.zeros((), BF16)
    bias = bias.ready()[pl.ds(info.member ^ group_mask, 1), :]
    m = dot(a1[...], w[:, :640]) + bias
    k01, v01 = m[:, 128:256].astype(BF16), m[:, 256:384].astype(BF16)
    pair = m[:, 384:512]
    k2 = pltpu.roll(pair, HEAD_WIDTH, 1).astype(BF16)
    v2 = m[:, 512:640].astype(BF16)
    qkv[:, 0:128] = (m[:, 0:128] * SCALE).astype(BF16)
    qkv[:, 128:256] = k01
    qkv[:, 256:384] = v01
    qkv[:, 384:512] = jnp.where(low, pair * SCALE, 0.0).astype(BF16)
    qkv[:, 512:640] = k2
    qkv[:, 640:768] = v2
    qkv.flush()
    columns = segments((1, SLOT_PATCHES), 1, 0, info)
    for start in range(0, SLOT_PATCHES, QUERY_ROWS):
        rows = slice(start, start + QUERY_ROWS)
        seen = segments((QUERY_ROWS, 1), 0, start, info) == columns
        q01 = qkv[rows, 0:128]
        outs, logs = [], []
        for query, keys, value in (
            (jnp.where(low, q01, zero), k01, v01),
            (jnp.where(low, zero, q01), k01, v01),
            (qkv[rows, 384:512], k2, v2),
        ):
            scores = jnp.where(seen, dot_t(query, keys), MASKED)
            largest = jnp.max(scores, axis=-1, keepdims=True)
            expon = jnp.exp(scores - largest)
            summed = jnp.sum(expon, axis=-1, keepdims=True)
            probs = (expon * (1.0 / summed)).astype(BF16)
            outs.append(dot(probs, value))
            logs.append(largest + jnp.log(summed))
        third = jnp.where(low, 0.0, pltpu.roll(outs[2], HEAD_WIDTH, 1))
        out[rows, 0:128] = third.astype(BF16)
        out[rows, 128:256] = jnp.where(low, outs[0], outs[1]).astype(BF16)
        lse[rows, :] = jnp.where(lane == 0, logs[0], jnp.where(lane == 1, logs[1], logs[2]))
    out.flush()
    lse.flush()
    total = dot_t(out[...], w[:, 512:768])
    proj[...] = plus(total, *(b[...] for b in before)).astype(BF16)


def middle_kernel(info, block, mine, peer, h1, a2, a2_t):
    both = plus(mine[...], peer[...])
    middle = block[...].astype(F32) + (both + info.bias(2))
    h1[...] = middle
    h1.flush()
    xhat, _ = normalize(middle)
    normed = (xhat * info.gain(1) + info.bias(1)).astype(BF16)
    a2[...] = normed
    a2.flush()
    a2_t[...] = normed.T


def split_rows(info, total, scratch, share, keep, send, before, at=0):
    start = pl.multiple_of(info.core * share, 8)
    scratch[...] = total
    kept = scratch[pl.ds(start, share), :]
    keep[:share, :] = plus(kept, *(b[:share, :] for b in before[:1])).astype(keep.dtype)
    theirs = scratch[pl.ds(pl.multiple_of(share - start, 8), share), :]
    sent = plus(theirs, *(b[at : at + share, :] for b in before[1:]))
    send[at : at + share, :] = sent.astype(send.dtype)


def mlp_kernel(
    info, a2, a2_t, dy, dy_t, order, *rest, rels, out_rels, group_mask, added, share
):
    before, rest = rest[:added], rest[added:]
    count, outs = len(rels), len(out_rels)
    pieces, rest = rest[:count], rest[count:]
    parts, (keep, send, da2, dbias, w1, w2, dw1, dw2, rows, sems) = rest[:outs], rest[outs:]
    first = piece_copies(info, pieces, rels, w1, sems.at[0], at=(0,))
    second = piece_copies(info, pieces, rels, w2, sems.at[1], at=(1,))
    start_all((dy, dy_t, a2_t, *before))
    wait_all(first)
    bias = info.params.ready()[pl.ds(BIASES + 6 + (info.member ^ group_mask), 1), :]
    u = dot(a2[...], w1[...]) + bias
    phi = 0.5 + 0.5 * lax.erf(u * (2.0**-0.5))
    hidden = (u * phi).astype(BF16)
    slope = phi + u * (jnp.exp(-0.5 * u * u) * 0.3989422804014327)
    wait_all(second)
    dpre = (dot(dy[...], w2[...]) * slope).astype(BF16)
    dw2[...] = dot(dy_t[...], hidden).astype(BF16)
    second = piece_copies(info, parts, out_rels, dw2, sems.at[1], out=True, at=(1,))
    dw1[...] = dot(a2_t[...], dpre).astype(BF16)
    first = piece_copies(info, parts, out_rels, dw1, sems.at[0], out=True, at=(0,))
    da2[...] = plus(dot_t(dpre, w1[...]), *(b[...] for b in before[2:])).astype(BF16)
    da2.flush()
    split_rows(info, dot_t(hidden, w2[...]), rows, share, keep, send, before[:2])
    dbias[0:1, :] = column_sum(dpre.astype(F32))
    wait_all(first)
    wait_all(second)


def middle_back(info, h1, dy, mine, peer, kept, peer_rows, e, e_t, dh1_rows, block_out, sums, rows):
    share = block_out.shape[0]
    start = pl.multiple_of(info.core * share, 8)
    xhat, inv_std = normalize(h1[...])
    da2 = plus(mine[...], peer[...])
    dh1 = dy[...].astype(F32) + norm_back(da2, xhat, inv_std, info.gain(1))
    low = dh1.astype(BF16)
    e[...] = low
    e.flush()
    e_t[...] = low.T
    e_t.flush()
    rows[...] = dh1
    dh1_rows[...] = rows[pl.ds(start, share), :]
    dh1_rows.flush()
    sums[0:1, :] = column_sum(da2 * xhat)
    sums[1:2, :] = column_sum(da2)
    sums[2:3, :] = column_sum(dh1)
    sums.flush()
    mlp = plus(kept[:share, :], peer_rows[:share, :])
    block_out[...] = ((h1.ready()[pl.ds(start, share), :] + mlp) + info.bias(3)).astype(BF16)


def first_back_kernel(
    info, h1, dy, mine, peer, kept, peer_rows, a1_t, qkv, out, lse, *rest, rels, out_rels, share
):
    count, outs = len(rels), len(out_rels)
    pieces, rest = rest[:count], rest[count:]
    parts, rest = rest[:outs], rest[outs:]
    keep, send, sums, e, e_t, dh1_rows, block_out, mid, w, dw, grads, rows, sems = rest
    copies = piece_copies(info, pieces, rels, w, sems)
    start_all((qkv, lse, out, a1_t))
    middle_back(
        info, h1, dy, mine, peer, kept, peer_rows, e, e_t, dh1_rows, block_out, mid, rows
    )
    wait_all(copies)
    attend_back(
        info, e, e_t, a1_t, qkv, out, lse, (), parts, out_rels, share, keep, send, sums,
        w, dw, grads, rows, sems,
    )


def second_back_kernel(
    info, e, e_t, a1_t, qkv, out, lse, kept, sent, *rest, rels, out_rels, share
):
    count, outs = len(rels), len(out_rels)
    pieces, rest = rest[:count], rest[count:]
    parts, (keep, send, sums, w, dw, grads, rows, sems) = rest[:outs], rest[outs:]
    copies = piece_copies(info, pieces, rels, w, sems)
    start_all((qkv, lse, out, a1_t, e_t, kept, sent))
    wait_all(copies)
    attend_back(
        info, e, e_t, a1_t, qkv, out, lse, (kept, sent), parts, out_rels, share, keep, send, sums,
        w, dw, grads, rows, sems,
    )


def attend_back(
    info, e, e_t, a1_t, qkv, out, lse, before, parts, out_rels, share, keep, send, sums,
    w, dw, grads, rows, sems,
):
    low = lanes() < HEAD_WIDTH
    zero = jnp.zeros((), BF16)
    dout = dot(e[...], w[:, 512:768])
    do2 = jnp.where(low, pltpu.roll(dout[:, 0:128], HEAD_WIDTH, 1), 0.0).astype(BF16)
    do01 = dout[:, 128:256].astype(BF16)
    q01, k01, v01 = qkv[:, 0:128], qkv[:, 128:256], qkv[:, 256:384]
    q2, k2, v2 = qkv[:, 384:512], qkv[:, 512:640], qkv[:, 640:768]
    lse_t = jnp.transpose(lse[...], (1, 0))
    seen = segments((SLOT_PATCHES, 1), 0, 0, info) == segments((1, SLOT_PATCHES), 1, 0, info)
    dq, dk, dv = [], [], []
    for head, (query, keys, value, dcontext) in enumerate(
        (
            (q01, jnp.where(low, k01, zero), jnp.where(low, v01, zero), do01),
            (q01, jnp.where(low, zero, k01), jnp.where(low, zero, v01), do01),
            (q2, k2, jnp.where(low, v2, zero), do2),
        )
    ):
        scores = jnp.where(seen, dot_t(keys, query), MASKED)
        probs = jnp.exp(scores - lse_t[head : head + 1, :])
        dprob = dot_t(value, dcontext)
        row_dot = column_sum(probs * dprob)
        dscore = (probs * (dprob - row_dot)).astype(BF16)
        dv.append(dot(probs.astype(BF16), dcontext))
        dk.append(dot(dscore, query))
        dq.append(t_dot(dscore, keys))
    grads[:, 0:128] = (jnp.where(low, dq[0], dq[1]) * SCALE).astype(BF16)
    grads[:, 128:256] = jnp.where(low, dk[0], dk[1]).astype(BF16)
    grads[:, 256:384] = jnp.where(low, dv[0], dv[1]).astype(BF16)
    shifted = pltpu.roll(dk[2], HEAD_WIDTH, 1)
    grads[:, 384:512] = jnp.where(low, dq[2] * SCALE, shifted).astype(BF16)
    grads[:, 512:640] = jnp.where(low, dv[2], 0.0).astype(BF16)
    dw[:, 0:512] = dot(a1_t[...], grads[:, 0:512]).astype(BF16)
    dw[:, 512:640] = (dot(a1_t[...], grads[:, 512:640]) + dot(e_t[...], out[:, 0:128])).astype(BF16)
    dw[:, 640:768] = dot(e_t[...], out[:, 128:256]).astype(BF16)
    copies = piece_copies(info, parts, out_rels, dw, sems, out=True)
    split_rows(info, dot_t(grads[...], w[:, 0:640]), rows, share, keep, send, before)
    sums[0:1, :] = column_sum(grads[...].astype(F32))
    wait_all(copies)


def last_kernel(
    info, x_rows, dh1_rows, mine, kept, peer, mid, db0, db1, s0, s1, input_grad, small
):
    share = x_rows.shape[0]
    xhat, inv_std = normalize(x_rows[...])
    da1 = plus(kept[:share, :], peer[:share, :])
    input_grad[...] = dh1_rows[...] + norm_back(da1, xhat, inv_std, info.gain(0))
    input_grad.flush()
    once = jnp.where(info.core == 0, 1.0, 0.0)
    member = info.member
    small[...] = jnp.zeros(small.shape, F32)
    small[0:1, :] = column_sum(da1 * xhat)
    small[1:2, :] = once * mid[0:1, :]
    small[2:3, :] = column_sum(da1)
    small[3:4, :] = once * mid[1:2, :]
    small[4:5, :] = once * mid[2:3, :]
    small[5:6, :] = mine[0:1, :]
    low = lanes() < HEAD_WIDTH
    for row, pair, single in ((6, 0, 384), (7, 256, 512)):
        for group in range(0, 4, 2):
            even, odd = (
                tuple(
                    jnp.where(
                        member == which,
                        s0[0:1, at : at + 128],
                        jnp.where(member == which ^ 2, s1[0:1, at : at + 128], 0.0),
                    )
                    for at in (pair, single)
                )
                for which in (group, group + 1)
            )
            turned = pltpu.roll(odd[0], HEAD_WIDTH, 1)
            at = group * 192
            small[row : row + 1, at : at + 128] = even[0]
            small[row : row + 1, at + 128 : at + 256] = jnp.where(low, even[1], turned)
            small[row : row + 1, at + 256 : at + 384] = jnp.where(
                low, turned, pltpu.roll(odd[1], HEAD_WIDTH, 1)
            )
    small[pl.ds(8 + member, 1), :] = db0[0:1, :]
    small[pl.ds(8 + (member ^ 2), 1), :] = db1[0:1, :]


def step(weight, gradient, moment, average, outs, rate):
    for ref, value in zip(
        outs, (gradient, *update(weight, gradient, moment, average, rate, WEIGHT_DECAY))
    ):
        ref[...] = value.reshape(ref.shape)


def finish_mlp_kernel(w1, m1, a1, w2, m2, a2, *rest):
    terms, outs = rest[:-8], rest[-8:]
    first, second = (plus(*(t[0, i] for t in terms)) for i in range(2))
    step(w1[...], first, m1[...], a1[...], outs[:4], RATE_FC1)
    step(w2[...], second, m2[...], a2[...], outs[4:], RATE_FC2)


def finish_attn_kernel(w1, m1, a1, w2, m2, a2, *rest):
    terms, outs = rest[:-8], rest[-8:]
    total = plus(*(t[0] for t in terms))
    wide = 2 * HEAD_WIDTH
    for i in range(3):
        single = 3 * wide + i * HEAD_WIDTH
        gradient = jnp.concatenate(
            [total[:, i * wide : (i + 1) * wide], total[:, single : single + HEAD_WIDTH]], axis=1
        )
        step(w1[i], gradient, m1[i], a1[i], [o.at[i] for o in outs[:4]], RATE_QKV)
    gradient = jnp.concatenate(
        [total[:, 5 * wide :], total[:, 5 * wide - HEAD_WIDTH : 5 * wide]], axis=1
    ).T
    step(w2[...], gradient, m2[...], a2[...], outs[4:], RATE_PROJ)


def call(kernel, name, outs, inputs, specs=None, scratch=(), flops=0, lazy=(), views=None, **fixed):
    results = [jax.ShapeDtypeStruct(s, d) for s, d, *_ in outs]
    specs, views = specs or {}, views or {}
    brought = [i for i in range(len(inputs)) if i not in specs]
    sent = [i for i, entry in enumerate(outs) if len(entry) == 2]
    moved = [jax.ShapeDtypeStruct(views[i][0], v.dtype) if i in views else v for i, v in enumerate(inputs)]
    moved = [moved[i] for i in brought] + [results[i] for i in sent]
    extra = [pltpu.VMEM(v.shape, v.dtype) for v in moved] + [pltpu.SemaphoreType.DMA((len(moved),))]
    size = sum(v.size * v.dtype.itemsize for v in (*inputs, *results))

    def body(*refs):
        refs = list(refs)
        cut = len(refs) - len(extra)
        here, sems = refs[cut:], refs[-1]
        info = Info(None)
        for n, i in enumerate(brought):
            source = views[i][1](refs[i], info) if i in views else refs[i]
            refs[i] = Lazy(source, here[n], sems.at[n])
            if i not in lazy:
                refs[i].start()
        leaving = []
        for n, i in enumerate(sent, len(brought)):
            refs[len(inputs) + i] = Early(refs[len(inputs) + i], here[n], sems.at[n])
            leaving.append(refs[len(inputs) + i])
        info.params = refs[0]
        kernel(info, *refs[1:cut], **fixed)
        info.params.ready()
        for value in leaving:
            value.flush()
        for value in leaving:
            value.copy.wait()

    body.__name__ = name
    return pl.pallas_call(
        body,
        out_shape=results,
        in_specs=[specs.get(i, ANYWHERE) for i in range(len(inputs))],
        out_specs=[entry[2] if len(entry) > 2 else ANYWHERE for entry in outs],
        scratch_shapes=[*scratch, *extra],
        compiler_params=pltpu.CompilerParams(vmem_limit_bytes=VMEM_LIMIT),
        cost_estimate=pl.CostEstimate(flops=flops // COST, bytes_accessed=size // COST, transcendentals=0),
        name=name,
    )(*inputs)


def block_call(kernel, name, outs, inputs):
    return pl.pallas_call(
        kernel,
        out_shape=[jax.ShapeDtypeStruct(s, d) for s, d in outs],
        in_specs=[IN_VMEM] * len(inputs),
        out_specs=[IN_VMEM] * len(outs),
        compiler_params=pltpu.CompilerParams(vmem_limit_bytes=VMEM_LIMIT),
        cost_estimate=pl.CostEstimate(flops=0, bytes_accessed=1 << 20, transcendentals=0),
        name=name,
    )(*inputs)


def shards(
    block_in,
    resolution,
    cotangent,
    w_qkv,
    w_proj,
    w_fc1,
    w_fc2,
    mom_qkv,
    mom_proj,
    mom_fc1,
    mom_fc2,
    avg_qkv,
    avg_proj,
    avg_fc1,
    avg_fc2,
    gains,
    gain_mom,
    gain_avg,
    biases,
    bias_mom,
    bias_avg,
):
    members = lax.axis_size("head")
    count = lax.axis_size("dp")
    member = lax.axis_index("head")
    me = lax.axis_index("dp")
    slot = member // 2
    width = block_in.shape[1]
    head_cols = w_qkv.shape[2]
    hidden_cols = w_fc1.shape[1]
    share = cotangent.shape[0]
    padded = -(-share // 16) * 16
    shard_rows = w_qkv.shape[0]
    aligned = shard_rows % 16 == 0
    paired = 2 * HEAD_WIDTH
    kind = lax.dynamic_index_in_dim(resolution, slot, keepdims=False)
    bias_rows = biases.reshape(-1, width)
    params = jnp.concatenate(
        [
            gains,
            bias_rows,
            jnp.full((PARAM_ROWS - KIND, width), kind.astype(F32)),
        ]
    )

    attn_shard, mlp_shard = block_call(
        cast_kernel,
        "cast",
        [((shard_rows, width), BF16), ((2, shard_rows, width), BF16)],
        (jnp.swapaxes(w_qkv, 0, 1), w_proj, w_fc1, w_fc2.T),
    )
    attn_w, mlp_w = Gather(attn_shard, count), Gather(mlp_shard, count)
    attn_w.far()

    def settle(pieces, stacked):
        if aligned:
            return pieces
        whole = joined(pieces, count, me)
        if stacked:
            whole = jnp.swapaxes(whole, 0, 1).reshape(1, 2, width, width)
        else:
            whole = whole.reshape(1, width, width)
        return ((whole, (None,)),)

    own_rels, other_rels = part_rels(count)
    part_rows = shard_rows if aligned else width

    def written(rels):
        return rels if aligned else ((None,),)

    def parts(stacked, pieces, rels):
        if aligned:
            return tuple(pieces)
        whole = pieces[0][0]
        if stacked:
            whole = jnp.swapaxes(whole.reshape(2, count, shard_rows, width), 0, 1)
        else:
            whole = whole.reshape(count, shard_rows, width)
        return parted(whole, rels, me)

    q_bias, v_bias = (bias_rows[i].reshape(members, head_cols) for i in (4, 5))
    none = jnp.zeros_like(q_bias)
    group_bias = jnp.concatenate(
        [
            q_bias[:, :paired],
            none[:, :paired],
            v_bias[:, :paired],
            q_bias[:, paired:],
            none[:, paired:],
            v_bias[:, paired:],
            none[:, paired:],
        ],
        axis=1,
    )
    group_bias = jnp.concatenate([group_bias, group_bias])
    tall, turned = (SLOT_PATCHES, width), (width, SLOT_PATCHES)

    def of_slot(ref, info):
        return ref.at[pl.ds(pl.multiple_of(info.slot * SLOT_PATCHES, 16), SLOT_PATCHES)]

    a1, a1_t, x_rows = call(
        prepare_kernel,
        "prepare",
        [(tall, BF16), (turned, BF16), ((share, width), F32)],
        (params, block_in),
        views={1: (tall, of_slot)},
        scratch=[pltpu.VMEM(tall, F32)],
    )
    dy, dy_t, dy_sum = call(
        join_kernel,
        "join",
        [(tall, BF16), (turned, BF16), ((8, width), F32)],
        (params, cotangent, swap(cotangent, "head", 1)),
        specs={1: IN_VMEM, 2: IN_VMEM},
        scratch=[pltpu.VMEM(tall, F32)],
    )

    attn_w.near(a1)
    attn_w.rest_own()
    attn_w.rest_other()
    mlp_w.far(attn_w.d_first)
    attn_own, attn_other = (settle(p, False) for p in attn_w.pieces())

    def attend(pieces, group_mask, a1, *before):
        return call(
            attend_kernel,
            "attend",
            [
                (tall, BF16),
                ((SLOT_PATCHES, 2 * paired), BF16),
                ((SLOT_PATCHES, paired), F32),
                (tall, BF16),
            ],
            (params, a1, group_bias, *before, *(a for a, _ in pieces)),
            specs={i + len(before): ANYWHERE for i in range(3, 3 + len(pieces))},
            lazy=range(3, 3 + len(before)),
            scratch=[pltpu.VMEM((width, width), BF16), pltpu.SemaphoreType.DMA((count,))],
            flops=2 * SLOT_PATCHES * (width * width + 12 * SLOT_PATCHES * HEAD_WIDTH),
            rels=[r for _, r in pieces],
            added=len(before),
            group_mask=group_mask,
        )

    own_saved = attend(attn_own, 0, a1)
    mlp_w.near(own_saved[3], attn_w.x_second, attn_w.d_second)
    other_saved = attend(attn_other, 2, after(a1, mlp_w.first), own_saved[3])
    mlp_w.rest_own(other_saved[3])
    proj = after(other_saved[3], mlp_w.second, mlp_w.x_first, mlp_w.y_first)
    h1, a2, a2_t = call(
        middle_kernel,
        "middle",
        [(tall, F32), (tall, BF16), (turned, BF16)],
        (
            params,
            block_in,
            proj,
            swap(proj, "head", 1),
        ),
        views={1: (tall, of_slot)},
    )

    def mlp(pieces, group_mask, rels, order, *before):
        first = 6 + len(before)
        *grads, keep, send, da2, dbias = call(
            mlp_kernel,
            "mlp",
            [((len(r), 2, part_rows, width), BF16, ANYWHERE) for r in written(rels)]
            + [
                ((padded, width), BF16),
                ((padded, width), BF16),
                (tall, BF16),
                ((8, hidden_cols), F32),
            ],
            (params, a2, a2_t, dy, dy_t, order, *before, *(a for a, _ in pieces)),
            specs={i: ANYWHERE for i in (5, *range(first, first + len(pieces)))},
            lazy=(2, 3, 4, *range(6, first)),
            scratch=[pltpu.VMEM((width, hidden_cols), BF16) for _ in range(4)]
            + [pltpu.VMEM(tall, F32), pltpu.SemaphoreType.DMA((2, count))],
            flops=12 * SLOT_PATCHES * width * hidden_cols,
            rels=[r for _, r in pieces],
            out_rels=written(rels),
            group_mask=group_mask,
            added=len(before),
            share=share,
        )
        return parts(True, grads, rels), keep, send, da2, dbias

    mlp_w.rest_other(a2, dy_t)
    mlp_own, mlp_other = (settle(p, True) for p in mlp_w.pieces())
    mlp_sum, attn_sum = Scatter(count), Scatter(count)
    own_mlp = mlp(mlp_own, 0, own_rels, after(params, mlp_w.d_first))
    mlp_sum.own(own_mlp[0])
    mlp_sum.own_rest()
    other_mlp = mlp(mlp_other, 2, other_rels, own_mlp[4], *own_mlp[1:4])
    peer_rows = swap(other_mlp[2], "head", 1)
    peer_mlp = swap(other_mlp[3], "head", 1)
    mlp_sum.other(other_mlp[0], peer_rows)
    back_outs = [((padded, width), BF16), ((padded, width), BF16), ((8, 5 * paired), F32)]
    back_scratch = [
        pltpu.VMEM((width, width), BF16),
        pltpu.VMEM((width, width), BF16),
        pltpu.VMEM((SLOT_PATCHES, 5 * paired), BF16),
        pltpu.VMEM(tall, F32),
        pltpu.SemaphoreType.DMA((count,)),
    ]
    back_flops = 2 * SLOT_PATCHES * (2 * width * width + 60 * SLOT_PATCHES * HEAD_WIDTH)

    def back_parts(rels):
        return [((len(r), part_rows, width), BF16, ANYWHERE) for r in written(rels)]

    *grads, keep, send, sums, e, e_t, dh1_rows, block_out, mid_sums = call(
        first_back_kernel,
        "first_back",
        back_parts(other_rels)
        + back_outs
        + [
            (tall, BF16),
            (turned, BF16),
            ((share, width), F32),
            ((share, width), BF16, IN_VMEM),
            ((8, width), F32),
        ],
        (
            params,
            h1,
            dy,
            other_mlp[3],
            peer_mlp,
            other_mlp[1],
            peer_rows,
            a1_t,
            *other_saved[:3],
            *(a for a, _ in attn_other),
        ),
        specs={i: ANYWHERE for i in range(11, 11 + len(attn_other))},
        lazy=(7, 8, 9, 10),
        scratch=back_scratch,
        flops=back_flops,
        rels=[r for _, r in attn_other],
        out_rels=written(other_rels),
        share=share,
    )
    other_back = parts(False, grads, other_rels), keep, send, sums
    attn_sum.other(other_back[0])
    mlp_sum.turn(e)
    mlp_sum.near_sum(other_back[3], mlp_sum.from_y)
    *grads, keep, send, sums = call(
        second_back_kernel,
        "second_back",
        back_parts(own_rels) + back_outs,
        (
            params,
            e,
            e_t,
            a1_t,
            *own_saved[:3],
            *other_back[1:3],
            *(a for a, _ in attn_own),
        ),
        specs={i: ANYWHERE for i in range(9, 9 + len(attn_own))},
        lazy=(2, 3, 4, 5, 6, 7, 8),
        scratch=back_scratch,
        flops=back_flops,
        rels=[r for _, r in attn_own],
        out_rels=written(own_rels),
        share=share,
    )
    own_back = parts(False, grads, own_rels), keep, send, sums
    done = (mlp_sum.from_near, mlp_sum.from_both, attn_sum.from_d, attn_sum.from_x)
    mlp_sum.far()
    peer_back = swap(own_back[2], "head", 1)
    attn_sum.own(own_back[0], *done, mlp_sum.away_total)
    attn_sum.turn_by_x(own_back[3])
    input_grad, small = call(
        last_kernel,
        "last",
        [((share, width), F32), ((PARAM_ROWS, width), F32)],
        (
            params,
            x_rows,
            dh1_rows,
            dy_sum,
            own_back[1],
            peer_back,
            mid_sums,
            own_mlp[4],
            other_mlp[4],
            own_back[3],
            other_back[3],
        ),
    )
    attn_sum.own_rest_joined(mlp_sum.away_total)
    attn_sum.near_sum(mlp_sum.away_total)
    attn_sum.far()
    by_row = (3, shard_rows, head_cols)
    fc1, fc2 = w_fc1.shape, w_fc2.T.shape
    *fc1_outs, fc2_grad, fc2_mom, fc2_new, fc2_avg = block_call(
        finish_mlp_kernel,
        "finish_mlp",
        [(fc1, F32)] * 4 + [(fc2, F32)] * 4,
        (
            after(w_fc1, attn_sum.away_total),
            mom_fc1,
            avg_fc1,
            w_fc2.T,
            mom_fc2.T,
            avg_fc2.T,
            *mlp_sum.terms(),
        ),
    )
    fc1_grad, fc1_mom, fc1_new, fc1_avg = fc1_outs
    fc2_grad, fc2_mom, fc2_new, fc2_avg = (v.T for v in (fc2_grad, fc2_mom, fc2_new, fc2_avg))
    small = small + swap(small, "head", 1)
    small = after(small, mlp_sum.from_away)
    over = over_x(small), over_y(small), over_both(small)
    small = (small + over[0]) + (over[1] + over[2])
    small = after(small, fc1_grad)
    for mask in line_masks(count):
        if mask == 2:
            small = after(small, attn_sum.from_away)
        small = small + swap(small, "dp", mask)
    gain_grad = small[:2]
    bias_grad = small[2:12].reshape(biases.shape)

    *qkv_outs, proj_grad, proj_mom, proj_new, proj_avg = block_call(
        finish_attn_kernel,
        "finish_attn",
        [(by_row, F32)] * 4 + [(w_proj.shape, F32)] * 4,
        (
            *(jnp.swapaxes(v, 0, 1) for v in (w_qkv, mom_qkv, avg_qkv)),
            w_proj,
            mom_proj,
            avg_proj,
            *attn_sum.terms(),
        ),
    )
    qkv_grad, qkv_mom, qkv_new, qkv_avg = (jnp.swapaxes(v, 0, 1) for v in qkv_outs)

    gain_mom_new, gain_new, gain_avg_new = update(
        gains, gain_grad, gain_mom, gain_avg, RATE_SMALL, 0.0
    )
    bias_mom_new, bias_new, bias_avg_new = update(
        biases, bias_grad, bias_mom, bias_avg, RATE_SMALL, 0.0
    )
    return (
        block_out,
        input_grad,
        qkv_grad,
        qkv_mom,
        qkv_new,
        qkv_avg,
        proj_grad,
        proj_mom,
        proj_new,
        proj_avg,
        fc1_grad,
        fc1_mom,
        fc1_new,
        fc1_avg,
        fc2_grad,
        fc2_mom,
        fc2_new,
        fc2_avg,
        gain_grad,
        gain_mom_new,
        gain_new,
        gain_avg_new,
        bias_grad,
        bias_mom_new,
        bias_new,
        bias_avg_new,
    )
def solution(mesh):
    return jax.shard_map(
        shards,
        mesh=mesh,
        in_specs=(
            P("dp", None),
            P("dp"),
            P(("dp", "head"), None),
            P("dp", None, "head"),
            P("head", "dp"),
            P("dp", "head"),
            P("head", "dp"),
            P("dp", None, "head"),
            P("head", "dp"),
            P("dp", "head"),
            P("head", "dp"),
            P("dp", None, "head"),
            P("head", "dp"),
            P("dp", "head"),
            P("head", "dp"),
            P(),
            P(),
            P(),
            P(),
            P(),
            P(),
        ),
        out_specs=(
            P(("dp", "head"), None),
            P(("dp", "head"), None),
            P("dp", None, "head"),
            P("dp", None, "head"),
            P("dp", None, "head"),
            P("dp", None, "head"),
            P("head", "dp"),
            P("head", "dp"),
            P("head", "dp"),
            P("head", "dp"),
            P("dp", "head"),
            P("dp", "head"),
            P("dp", "head"),
            P("dp", "head"),
            P("head", "dp"),
            P("head", "dp"),
            P("head", "dp"),
            P("head", "dp"),
            P(),
            P(),
            P(),
            P(),
            P(),
            P(),
            P(),
            P(),
        ),
        check_vma=False,
    )
```

```python
import jax
import jax.numpy as jnp
from jax import lax
from jax.experimental import pallas as pl
from jax.experimental.pallas import tpu as pltpu
from jax.sharding import PartitionSpec as P

HEAD_WIDTH = 64
SLOT_PATCHES = 784
LOWRES = 196


EPSILON = 1e-06
MOMENTUM_RATE = 0.9
AVERAGING = 0.75
WEIGHT_DECAY = 0.05
RATE_QKV = 0.001
RATE_PROJ = 0.01
RATE_FC1 = 0.0006
RATE_FC2 = 0.0003
RATE_SMALL = 0.003
MASKED = -1e30
SCALE = HEAD_WIDTH**-0.5
F32 = jnp.float32
BF16 = jnp.bfloat16
QUERY_ROWS = SLOT_PATCHES // 2
VMEM_LIMIT = 60 << 20
COST = 16
GAINS, BIASES, KIND, PARAM_ROWS = 0, 2, 12, 16

IN_VMEM = pl.BlockSpec(memory_space=pltpu.VMEM)
ANYWHERE = pl.BlockSpec(memory_space=pl.ANY)


def update(weight, gradient, moment, average, step_rate, decay_rate):
    step_grad = gradient + decay_rate * weight
    moment_new = MOMENTUM_RATE * moment + step_grad
    weight_new = weight - step_rate * (step_grad + MOMENTUM_RATE * moment_new)
    return (moment_new, weight_new, AVERAGING * average + (1.0 - AVERAGING) * weight_new)


def swap(value, axis, mask):
    return lax.ppermute(value, axis, [(i, i ^ mask) for i in range(lax.axis_size(axis))])


def line_masks(count):
    masks, mask = [], count // 2
    while mask > 1:
        masks.append(mask)
        mask //= 2
    return masks


def line_order(count):
    order = [0]
    for mask in line_masks(count):
        order = order + [r ^ mask for r in order]
    return order


def z_sets(count):
    order = line_order(count)
    eighth = count // 8
    return order[:eighth], order[eighth : 2 * eighth], order[2 * eighth :]


def flip(order):
    return [r ^ 1 for r in order]


def after(value, *others):
    return lax.optimization_barrier((value, *others))[0]


def both_after(values, *others):
    return lax.optimization_barrier((*values, *others))[: len(values)] if others else values


def over_x(value):
    return swap(value, "head", 2)


def over_y(value):
    return swap(value, "dp", 1)


def over_both(value):
    members = lax.axis_size("head")
    total = members * lax.axis_size("dp")
    return lax.ppermute(value, ("dp", "head"), [(i, i ^ members ^ 2) for i in range(total)])


def over_z(value):
    return swap(value, "dp", 2)


def over_far(value, count):
    return swap(value, "dp", line_masks(count)[-2])


class Gather:
    def __init__(self, shard, count):
        base = shard[None]
        for mask in line_masks(count)[:-2]:
            base = jnp.concatenate([base, swap(base, "dp", mask)])
        self.base, self.count = base, count

    def far(self, *later):
        self.base = both_after((self.base,), *later)[0]
        self.first = jnp.concatenate([self.base, over_far(self.base, self.count)])

    def near(self, *later):
        self.first = both_after((self.first,), *later)[0]
        self.second = over_z(self.first)
        self.x_first, self.y_first = over_x(self.first), over_y(self.first)

    def rest_own(self, *later):
        second, y_first = both_after((self.second, self.y_first), *later)
        self.y_second, self.d_first = over_y(second), over_x(after(y_first, self.x_first))

    def rest_x(self, *later):
        second = both_after((self.second,), *later)[0]
        self.x_second, self.d_second = over_x(second), over_x(self.y_second)

    def rest_other(self, *later):
        second, d_first = both_after((self.second, self.d_first), self.d_first, *later)
        self.x_second, self.d_second = over_x(second), over_z(d_first)

    def pieces(self):
        base, away, near = z_sets(self.count)
        rels = base + away, near
        own = (self.first, self.second, self.y_first, self.y_second)
        other = (self.x_first, self.x_second, self.d_first, self.d_second)
        turned = tuple(flip(r) for r in rels)
        return tuple(zip(own, rels + turned)), tuple(zip(other, rels + turned))


def joined(pieces, count, me):
    order = [r for _, rel in pieces for r in rel]
    place = jnp.array([order.index(r) for r in range(count)], jnp.int32)
    return jnp.concatenate([a for a, _ in pieces])[place[jnp.arange(count, dtype=jnp.int32) ^ me]]


def part_rels(count):
    base, away, near = z_sets(count)
    own = (base, away, near, flip(near), flip(base + away))
    other = (base + away + near, flip(near), flip(base + away))
    return own, other


def parted(whole, rels, me):
    return tuple(whole[jnp.array(rel, jnp.int32) ^ me] for rel in rels)


def plus(*terms):
    return sum(t.astype(F32) for t in terms)


def low_plus(*terms):
    return plus(*terms).astype(BF16)


class Scatter:
    def __init__(self, count):
        self.count = count

    def own(self, parts, *later):
        self.base, self.away, self.near, y_near, y_rest = parts
        y_near, y_rest = both_after((y_near, y_rest), *later)
        self.from_y_near, self.y_rest = over_y(y_near), y_rest

    def own_rest(self, *later):
        self.from_y = over_y(both_after((self.y_rest,), *later)[0])

    def turn_by_x(self, *later):
        rest, from_d = both_after((self.d_rest, self.from_d), *later)
        self.from_both, self.to_y = None, over_x(low_plus(rest, from_d))

    def own_rest_joined(self, *later):
        rest, to_y = both_after((self.y_rest, self.to_y), *later)
        self.from_y = over_y(low_plus(rest, to_y))

    def arrived(self):
        every = (self.from_y, self.from_both, self.from_near, self.from_x)
        return tuple(v for v in every if v is not None)

    def other(self, parts, *later):
        xs, d_near, self.d_rest = parts
        xs, d_near = both_after((xs, d_near), *later)
        self.from_d, self.from_x = over_z(d_near), over_x(xs)

    def turn(self, *later):
        rest, from_d = both_after((self.d_rest, self.from_d), *later)
        self.from_both = over_both(low_plus(rest, from_d))

    def near_sum(self, *later):
        near = both_after((self.near,), *later)[0]
        cut = 2 * self.base.shape[0]
        self.near_total = low_plus(near, self.from_y_near, self.from_x[cut:])
        self.from_near = over_z(self.near_total)

    def far(self, *later):
        cut = self.base.shape[0]
        away = both_after((self.away,), *later)[0]
        rest = self.arrived()
        self.away_total = low_plus(away, *(r[cut : 2 * cut] for r in rest))
        self.from_away = over_far(self.away_total, self.count)

    def terms(self):
        cut = self.base.shape[0]
        rest = self.arrived()
        terms = (self.base, self.from_away, *(r[:cut] for r in rest))
        masks = line_masks(self.count)[:-2]
        if not masks:
            return (self.base, self.from_away, *rest)
        total = plus(*terms)
        for mask in reversed(masks):
            keep = total.shape[0] // 2
            total = total[:keep] + swap(total[keep:].astype(BF16), "dp", mask)
        return (total[:1],)


def dot(a, b):
    return jnp.dot(a, b, preferred_element_type=F32)


def dot_t(a, b):
    return lax.dot_general(a, b, (((1,), (1,)), ((), ())), preferred_element_type=F32)


def t_dot(a, b):
    return lax.dot_general(a, b, (((0,), (0,)), ((), ())), preferred_element_type=F32)


def normalize(inputs):
    mean_row = jnp.mean(inputs, axis=-1, keepdims=True)
    centred = inputs - mean_row
    spread = jnp.mean(centred * centred, axis=-1, keepdims=True)
    inv_std = lax.rsqrt(spread + EPSILON)
    return (centred * inv_std, inv_std)


def norm_back(grad_out, centred, inv_std, gain_row):
    scaled = grad_out * gain_row
    return inv_std * (
        scaled
        - jnp.mean(scaled, axis=-1, keepdims=True)
        - centred * jnp.mean(scaled * centred, axis=-1, keepdims=True)
    )


def piece_copies(info, refs, rels, dest, sems, out=False, at=()):
    copies = []
    for ref, rel in zip(refs, rels):
        for j, r in enumerate(rel):
            rows = ref.shape[-2]
            start = 0 if r is None else pl.multiple_of((info.me ^ r) * rows, rows)
            there, here = ref.at[(j, *at)], dest.at[pl.ds(start, rows)]
            copies.append((here, there) if out else (there, here))
    copies = [
        pltpu.make_async_copy(a, b, sems.at[i]) for i, (a, b) in enumerate(copies)
    ]
    for copy in copies:
        copy.start()
    return copies


def wait_all(copies):
    for copy in copies:
        copy.wait()


class Info:
    def __init__(self, params):
        self.me, self.member = lax.axis_index("dp"), lax.axis_index("head")
        self.slot, self.core = self.member // 2, lax.rem(self.member, 2)
        self.params = params

    def kind(self):
        return self.params[KIND : KIND + 1, 0:1]

    def gain(self, i):
        return self.params[GAINS + i : GAINS + i + 1, :]

    def bias(self, i):
        return self.params[BIASES + i : BIASES + i + 1, :]


class Lazy:
    def __init__(self, source, here, sem):
        self.here, self.shape, self.waits = here, here.shape, True
        self.copy = pltpu.make_async_copy(source, here, sem)

    def start(self):
        self.copy.start()

    def ready(self):
        if self.waits:
            self.copy.wait()
            self.waits = False
        return self.here

    def __getitem__(self, at):
        return self.ready()[at]


class Early:
    def __init__(self, target, here, sem):
        self.here, self.shape, self.dtype, self.stays = here, here.shape, here.dtype, True
        self.copy = pltpu.make_async_copy(here, target, sem)

    def flush(self):
        if self.stays:
            self.copy.start()
            self.stays = False

    def __setitem__(self, at, value):
        self.here[at] = value

    def __getitem__(self, at):
        return self.here[at]


def start_all(values):
    for value in values:
        value.start()


def lanes():
    return lax.broadcasted_iota(jnp.int32, (1, 2 * HEAD_WIDTH), 1)


def segments(shape, axis, start, info):
    run = (lax.broadcasted_iota(jnp.int32, shape, axis) + start) // LOWRES
    return jnp.where(info.kind() > 0.0, 0, run)


def column_sum(rows):
    return jnp.sum(rows, axis=0, keepdims=True)


def cast_kernel(w_qkv, w_proj, w_fc1, w_fc2, attn, mlp):
    wide = 2 * HEAD_WIDTH
    for i in range(3):
        attn[:, i * wide : (i + 1) * wide] = w_qkv[i, :, :wide].astype(BF16)
    single = [w_qkv[i, :, wide:] for i in range(3)]
    proj = w_proj[...].T
    attn[:, 3 * wide : 4 * wide] = jnp.concatenate(single[:2], axis=1).astype(BF16)
    attn[:, 4 * wide : 5 * wide] = jnp.concatenate([single[2], proj[:, wide:]], axis=1).astype(BF16)
    attn[:, 5 * wide : 6 * wide] = proj[:, :wide].astype(BF16)
    mlp[0] = w_fc1[...].astype(BF16)
    mlp[1] = w_fc2[...].astype(BF16)


def prepare_kernel(info, block, a1, a1_t, x_rows, rows):
    share = x_rows.shape[0]
    x = block[...].astype(F32)
    rows[...] = x
    x_rows[...] = rows[pl.ds(pl.multiple_of(info.core * share, 8), share), :]
    x_rows.flush()
    xhat, _ = normalize(x)
    normed = (xhat * info.gain(0) + info.bias(0)).astype(BF16)
    a1[...] = normed
    a1.flush()
    a1_t[...] = normed.T


def join_kernel(info, mine, peer, dy, dy_t, total, rows):
    share = mine.shape[0]
    start = pl.multiple_of(info.core * share, 8)
    own = mine[...].astype(F32)
    rows[pl.ds(start, share), :] = own
    rows[pl.ds(pl.multiple_of(share - start, 8), share), :] = peer[...].astype(F32)
    low = rows[...].astype(BF16)
    dy[...] = low
    dy.flush()
    total[0:1, :] = column_sum(own)
    dy_t[...] = low.T


def attend_kernel(info, a1, bias, *rest, rels, added, group_mask):
    before, rest = rest[:added], rest[added:]
    count = len(rels)
    pieces, (qkv, out, lse, proj, w, sems) = rest[:count], rest[count:]
    copies = piece_copies(info, pieces, rels, w, sems)
    start_all(before)
    wait_all(copies)
    lane = lanes()
    low = lane < HEAD_WIDTH
    zero = jnp.zeros((), BF16)
    bias = bias.ready()[pl.ds(info.member ^ group_mask, 1), :]
    m = dot(a1[...], w[:, :640]) + bias
    k01, v01 = m[:, 128:256].astype(BF16), m[:, 256:384].astype(BF16)
    pair = m[:, 384:512]
    k2 = pltpu.roll(pair, HEAD_WIDTH, 1).astype(BF16)
    v2 = m[:, 512:640].astype(BF16)
    qkv[:, 0:128] = (m[:, 0:128] * SCALE).astype(BF16)
    qkv[:, 128:256] = k01
    qkv[:, 256:384] = v01
    qkv[:, 384:512] = jnp.where(low, pair * SCALE, 0.0).astype(BF16)
    qkv[:, 512:640] = k2
    qkv[:, 640:768] = v2
    qkv.flush()
    columns = segments((1, SLOT_PATCHES), 1, 0, info)
    for start in range(0, SLOT_PATCHES, QUERY_ROWS):
        rows = slice(start, start + QUERY_ROWS)
        seen = segments((QUERY_ROWS, 1), 0, start, info) == columns
        q01 = qkv[rows, 0:128]
        outs, logs = [], []
        for query, keys, value in (
            (jnp.where(low, q01, zero), k01, v01),
            (jnp.where(low, zero, q01), k01, v01),
            (qkv[rows, 384:512], k2, v2),
        ):
            scores = jnp.where(seen, dot_t(query, keys), MASKED)
            largest = jnp.max(scores, axis=-1, keepdims=True)
            expon = jnp.exp(scores - largest)
            summed = jnp.sum(expon, axis=-1, keepdims=True)
            probs = (expon * (1.0 / summed)).astype(BF16)
            outs.append(dot(probs, value))
            logs.append(largest + jnp.log(summed))
        third = jnp.where(low, 0.0, pltpu.roll(outs[2], HEAD_WIDTH, 1))
        out[rows, 0:128] = third.astype(BF16)
        out[rows, 128:256] = jnp.where(low, outs[0], outs[1]).astype(BF16)
        lse[rows, :] = jnp.where(lane == 0, logs[0], jnp.where(lane == 1, logs[1], logs[2]))
    out.flush()
    lse.flush()
    total = dot_t(out[...], w[:, 512:768])
    proj[...] = plus(total, *(b[...] for b in before)).astype(BF16)


def middle_kernel(info, block, mine, peer, h1, a2, a2_t):
    both = plus(mine[...], peer[...])
    middle = block[...].astype(F32) + (both + info.bias(2))
    h1[...] = middle
    h1.flush()
    xhat, _ = normalize(middle)
    normed = (xhat * info.gain(1) + info.bias(1)).astype(BF16)
    a2[...] = normed
    a2.flush()
    a2_t[...] = normed.T


def split_rows(info, total, scratch, share, keep, send, before, at=0):
    start = pl.multiple_of(info.core * share, 8)
    scratch[...] = total
    kept = scratch[pl.ds(start, share), :]
    keep[:share, :] = plus(kept, *(b[:share, :] for b in before[:1])).astype(keep.dtype)
    theirs = scratch[pl.ds(pl.multiple_of(share - start, 8), share), :]
    sent = plus(theirs, *(b[at : at + share, :] for b in before[1:]))
    send[at : at + share, :] = sent.astype(send.dtype)


def mlp_kernel(
    info, a2, a2_t, dy, dy_t, order, *rest, rels, out_rels, group_mask, added, share
):
    before, rest = rest[:added], rest[added:]
    count, outs = len(rels), len(out_rels)
    pieces, rest = rest[:count], rest[count:]
    parts, (keep, send, da2, dbias, w1, w2, dw1, dw2, rows, sems) = rest[:outs], rest[outs:]
    first = piece_copies(info, pieces, rels, w1, sems.at[0], at=(0,))
    second = piece_copies(info, pieces, rels, w2, sems.at[1], at=(1,))
    start_all((dy, dy_t, a2_t, *before))
    wait_all(first)
    bias = info.params.ready()[pl.ds(BIASES + 6 + (info.member ^ group_mask), 1), :]
    u = dot(a2[...], w1[...]) + bias
    phi = 0.5 + 0.5 * lax.erf(u * (2.0**-0.5))
    hidden = (u * phi).astype(BF16)
    slope = phi + u * (jnp.exp(-0.5 * u * u) * 0.3989422804014327)
    wait_all(second)
    dpre = (dot(dy[...], w2[...]) * slope).astype(BF16)
    dw2[...] = dot(dy_t[...], hidden).astype(BF16)
    second = piece_copies(info, parts, out_rels, dw2, sems.at[1], out=True, at=(1,))
    dw1[...] = dot(a2_t[...], dpre).astype(BF16)
    first = piece_copies(info, parts, out_rels, dw1, sems.at[0], out=True, at=(0,))
    da2[...] = plus(dot_t(dpre, w1[...]), *(b[...] for b in before[2:])).astype(BF16)
    da2.flush()
    split_rows(info, dot_t(hidden, w2[...]), rows, share, keep, send, before[:2])
    dbias[0:1, :] = column_sum(dpre.astype(F32))
    wait_all(first)
    wait_all(second)


def middle_back(info, h1, dy, mine, peer, kept, peer_rows, e, e_t, dh1_rows, block_out, sums, rows):
    share = block_out.shape[0]
    start = pl.multiple_of(info.core * share, 8)
    xhat, inv_std = normalize(h1[...])
    da2 = plus(mine[...], peer[...])
    dh1 = dy[...].astype(F32) + norm_back(da2, xhat, inv_std, info.gain(1))
    low = dh1.astype(BF16)
    e[...] = low
    e.flush()
    e_t[...] = low.T
    e_t.flush()
    rows[...] = dh1
    dh1_rows[...] = rows[pl.ds(start, share), :]
    dh1_rows.flush()
    sums[0:1, :] = column_sum(da2 * xhat)
    sums[1:2, :] = column_sum(da2)
    sums[2:3, :] = column_sum(dh1)
    sums.flush()
    mlp = plus(kept[:share, :], peer_rows[:share, :])
    block_out[...] = ((h1.ready()[pl.ds(start, share), :] + mlp) + info.bias(3)).astype(BF16)


def first_back_kernel(
    info, h1, dy, mine, peer, kept, peer_rows, a1_t, qkv, out, lse, *rest, rels, out_rels, share
):
    count, outs = len(rels), len(out_rels)
    pieces, rest = rest[:count], rest[count:]
    parts, rest = rest[:outs], rest[outs:]
    keep, send, sums, e, e_t, dh1_rows, block_out, mid, w, dw, grads, rows, sems = rest
    copies = piece_copies(info, pieces, rels, w, sems)
    start_all((qkv, lse, out, a1_t))
    middle_back(
        info, h1, dy, mine, peer, kept, peer_rows, e, e_t, dh1_rows, block_out, mid, rows
    )
    wait_all(copies)
    attend_back(
        info, e, e_t, a1_t, qkv, out, lse, (), parts, out_rels, share, keep, send, sums,
        w, dw, grads, rows, sems,
    )


def second_back_kernel(
    info, e, e_t, a1_t, qkv, out, lse, kept, sent, *rest, rels, out_rels, share
):
    count, outs = len(rels), len(out_rels)
    pieces, rest = rest[:count], rest[count:]
    parts, (keep, send, sums, w, dw, grads, rows, sems) = rest[:outs], rest[outs:]
    copies = piece_copies(info, pieces, rels, w, sems)
    start_all((qkv, lse, out, a1_t, e_t, kept, sent))
    wait_all(copies)
    attend_back(
        info, e, e_t, a1_t, qkv, out, lse, (kept, sent), parts, out_rels, share, keep, send, sums,
        w, dw, grads, rows, sems,
    )


def attend_back(
    info, e, e_t, a1_t, qkv, out, lse, before, parts, out_rels, share, keep, send, sums,
    w, dw, grads, rows, sems,
):
    low = lanes() < HEAD_WIDTH
    zero = jnp.zeros((), BF16)
    dout = dot(e[...], w[:, 512:768])
    do2 = jnp.where(low, pltpu.roll(dout[:, 0:128], HEAD_WIDTH, 1), 0.0).astype(BF16)
    do01 = dout[:, 128:256].astype(BF16)
    q01, k01, v01 = qkv[:, 0:128], qkv[:, 128:256], qkv[:, 256:384]
    q2, k2, v2 = qkv[:, 384:512], qkv[:, 512:640], qkv[:, 640:768]
    lse_t = jnp.transpose(lse[...], (1, 0))
    seen = segments((SLOT_PATCHES, 1), 0, 0, info) == segments((1, SLOT_PATCHES), 1, 0, info)
    dq, dk, dv = [], [], []
    for head, (query, keys, value, dcontext) in enumerate(
        (
            (q01, jnp.where(low, k01, zero), jnp.where(low, v01, zero), do01),
            (q01, jnp.where(low, zero, k01), jnp.where(low, zero, v01), do01),
            (q2, k2, jnp.where(low, v2, zero), do2),
        )
    ):
        scores = jnp.where(seen, dot_t(keys, query), MASKED)
        probs = jnp.exp(scores - lse_t[head : head + 1, :])
        dprob = dot_t(value, dcontext)
        row_dot = column_sum(probs * dprob)
        dscore = (probs * (dprob - row_dot)).astype(BF16)
        dv.append(dot(probs.astype(BF16), dcontext))
        dk.append(dot(dscore, query))
        dq.append(t_dot(dscore, keys))
    grads[:, 0:128] = (jnp.where(low, dq[0], dq[1]) * SCALE).astype(BF16)
    grads[:, 128:256] = jnp.where(low, dk[0], dk[1]).astype(BF16)
    grads[:, 256:384] = jnp.where(low, dv[0], dv[1]).astype(BF16)
    shifted = pltpu.roll(dk[2], HEAD_WIDTH, 1)
    grads[:, 384:512] = jnp.where(low, dq[2] * SCALE, shifted).astype(BF16)
    grads[:, 512:640] = jnp.where(low, dv[2], 0.0).astype(BF16)
    dw[:, 0:512] = dot(a1_t[...], grads[:, 0:512]).astype(BF16)
    dw[:, 512:640] = (dot(a1_t[...], grads[:, 512:640]) + dot(e_t[...], out[:, 0:128])).astype(BF16)
    dw[:, 640:768] = dot(e_t[...], out[:, 128:256]).astype(BF16)
    copies = piece_copies(info, parts, out_rels, dw, sems, out=True)
    split_rows(info, dot_t(grads[...], w[:, 0:640]), rows, share, keep, send, before)
    sums[0:1, :] = column_sum(grads[...].astype(F32))
    wait_all(copies)


def last_kernel(
    info, x_rows, dh1_rows, mine, kept, peer, mid, db0, db1, s0, s1, input_grad, small
):
    share = x_rows.shape[0]
    xhat, inv_std = normalize(x_rows[...])
    da1 = plus(kept[:share, :], peer[:share, :])
    input_grad[...] = dh1_rows[...] + norm_back(da1, xhat, inv_std, info.gain(0))
    input_grad.flush()
    once = jnp.where(info.core == 0, 1.0, 0.0)
    member = info.member
    small[...] = jnp.zeros(small.shape, F32)
    small[0:1, :] = column_sum(da1 * xhat)
    small[1:2, :] = once * mid[0:1, :]
    small[2:3, :] = column_sum(da1)
    small[3:4, :] = once * mid[1:2, :]
    small[4:5, :] = once * mid[2:3, :]
    small[5:6, :] = mine[0:1, :]
    low = lanes() < HEAD_WIDTH
    for row, pair, single in ((6, 0, 384), (7, 256, 512)):
        for group in range(0, 4, 2):
            even, odd = (
                tuple(
                    jnp.where(
                        member == which,
                        s0[0:1, at : at + 128],
                        jnp.where(member == which ^ 2, s1[0:1, at : at + 128], 0.0),
                    )
                    for at in (pair, single)
                )
                for which in (group, group + 1)
            )
            turned = pltpu.roll(odd[0], HEAD_WIDTH, 1)
            at = group * 192
            small[row : row + 1, at : at + 128] = even[0]
            small[row : row + 1, at + 128 : at + 256] = jnp.where(low, even[1], turned)
            small[row : row + 1, at + 256 : at + 384] = jnp.where(
                low, turned, pltpu.roll(odd[1], HEAD_WIDTH, 1)
            )
    small[pl.ds(8 + member, 1), :] = db0[0:1, :]
    small[pl.ds(8 + (member ^ 2), 1), :] = db1[0:1, :]


def step(weight, gradient, moment, average, outs, rate):
    for ref, value in zip(
        outs, (gradient, *update(weight, gradient, moment, average, rate, WEIGHT_DECAY))
    ):
        ref[...] = value.reshape(ref.shape)


def finish_mlp_kernel(w1, m1, a1, w2, m2, a2, *rest):
    terms, outs = rest[:-8], rest[-8:]
    first, second = (plus(*(t[0, i] for t in terms)) for i in range(2))
    step(w1[...], first, m1[...], a1[...], outs[:4], RATE_FC1)
    step(w2[...], second, m2[...], a2[...], outs[4:], RATE_FC2)


def finish_attn_kernel(w1, m1, a1, w2, m2, a2, *rest):
    terms, outs = rest[:-8], rest[-8:]
    total = plus(*(t[0] for t in terms))
    wide = 2 * HEAD_WIDTH
    for i in range(3):
        single = 3 * wide + i * HEAD_WIDTH
        gradient = jnp.concatenate(
            [total[:, i * wide : (i + 1) * wide], total[:, single : single + HEAD_WIDTH]], axis=1
        )
        step(w1[i], gradient, m1[i], a1[i], [o.at[i] for o in outs[:4]], RATE_QKV)
    gradient = jnp.concatenate(
        [total[:, 5 * wide :], total[:, 5 * wide - HEAD_WIDTH : 5 * wide]], axis=1
    ).T
    step(w2[...], gradient, m2[...], a2[...], outs[4:], RATE_PROJ)


def call(kernel, name, outs, inputs, specs=None, scratch=(), flops=0, lazy=(), views=None, **fixed):
    results = [jax.ShapeDtypeStruct(s, d) for s, d, *_ in outs]
    specs, views = specs or {}, views or {}
    brought = [i for i in range(len(inputs)) if i not in specs]
    sent = [i for i, entry in enumerate(outs) if len(entry) == 2]
    moved = [jax.ShapeDtypeStruct(views[i][0], v.dtype) if i in views else v for i, v in enumerate(inputs)]
    moved = [moved[i] for i in brought] + [results[i] for i in sent]
    extra = [pltpu.VMEM(v.shape, v.dtype) for v in moved] + [pltpu.SemaphoreType.DMA((len(moved),))]
    size = sum(v.size * v.dtype.itemsize for v in (*inputs, *results))

    def body(*refs):
        refs = list(refs)
        cut = len(refs) - len(extra)
        here, sems = refs[cut:], refs[-1]
        info = Info(None)
        for n, i in enumerate(brought):
            source = views[i][1](refs[i], info) if i in views else refs[i]
            refs[i] = Lazy(source, here[n], sems.at[n])
            if i not in lazy:
                refs[i].start()
        leaving = []
        for n, i in enumerate(sent, len(brought)):
            refs[len(inputs) + i] = Early(refs[len(inputs) + i], here[n], sems.at[n])
            leaving.append(refs[len(inputs) + i])
        info.params = refs[0]
        kernel(info, *refs[1:cut], **fixed)
        info.params.ready()
        for value in leaving:
            value.flush()
        for value in leaving:
            value.copy.wait()

    body.__name__ = name
    return pl.pallas_call(
        body,
        out_shape=results,
        in_specs=[specs.get(i, ANYWHERE) for i in range(len(inputs))],
        out_specs=[entry[2] if len(entry) > 2 else ANYWHERE for entry in outs],
        scratch_shapes=[*scratch, *extra],
        compiler_params=pltpu.CompilerParams(vmem_limit_bytes=VMEM_LIMIT),
        cost_estimate=pl.CostEstimate(flops=flops // COST, bytes_accessed=size // COST, transcendentals=0),
        name=name,
    )(*inputs)


def block_call(kernel, name, outs, inputs):
    return pl.pallas_call(
        kernel,
        out_shape=[jax.ShapeDtypeStruct(s, d) for s, d in outs],
        in_specs=[IN_VMEM] * len(inputs),
        out_specs=[IN_VMEM] * len(outs),
        compiler_params=pltpu.CompilerParams(vmem_limit_bytes=VMEM_LIMIT),
        cost_estimate=pl.CostEstimate(flops=0, bytes_accessed=1 << 20, transcendentals=0),
        name=name,
    )(*inputs)


def shards(
    block_in,
    resolution,
    cotangent,
    w_qkv,
    w_proj,
    w_fc1,
    w_fc2,
    mom_qkv,
    mom_proj,
    mom_fc1,
    mom_fc2,
    avg_qkv,
    avg_proj,
    avg_fc1,
    avg_fc2,
    gains,
    gain_mom,
    gain_avg,
    biases,
    bias_mom,
    bias_avg,
):
    members = lax.axis_size("head")
    count = lax.axis_size("dp")
    member = lax.axis_index("head")
    me = lax.axis_index("dp")
    slot = member // 2
    width = block_in.shape[1]
    head_cols = w_qkv.shape[2]
    hidden_cols = w_fc1.shape[1]
    share = cotangent.shape[0]
    padded = -(-share // 16) * 16
    shard_rows = w_qkv.shape[0]
    aligned = shard_rows % 16 == 0
    paired = 2 * HEAD_WIDTH
    kind = jnp.where(slot == 0, resolution[0], resolution[1])
    bias_rows = biases.reshape(-1, width)
    params = jnp.concatenate(
        [
            gains,
            bias_rows,
            jnp.full((PARAM_ROWS - KIND, width), kind.astype(F32)),
        ]
    )

    attn_shard, mlp_shard = block_call(
        cast_kernel,
        "cast",
        [((shard_rows, width), BF16), ((2, shard_rows, width), BF16)],
        (jnp.swapaxes(w_qkv, 0, 1), w_proj, w_fc1, w_fc2.T),
    )
    attn_w, mlp_w = Gather(attn_shard, count), Gather(mlp_shard, count)
    attn_w.far()

    def settle(pieces, stacked):
        if aligned:
            return pieces
        whole = joined(pieces, count, me)
        if stacked:
            whole = jnp.swapaxes(whole, 0, 1).reshape(1, 2, width, width)
        else:
            whole = whole.reshape(1, width, width)
        return ((whole, (None,)),)

    own_rels, other_rels = part_rels(count)
    part_rows = shard_rows if aligned else width

    def written(rels):
        return rels if aligned else ((None,),)

    def parts(stacked, pieces, rels):
        if aligned:
            return tuple(pieces)
        whole = pieces[0][0]
        if stacked:
            whole = jnp.swapaxes(whole.reshape(2, count, shard_rows, width), 0, 1)
        else:
            whole = whole.reshape(count, shard_rows, width)
        return parted(whole, rels, me)

    q_bias, v_bias = (bias_rows[i].reshape(members, head_cols) for i in (4, 5))
    none = jnp.zeros_like(q_bias)
    group_bias = jnp.concatenate(
        [
            q_bias[:, :paired],
            none[:, :paired],
            v_bias[:, :paired],
            q_bias[:, paired:],
            none[:, paired:],
            v_bias[:, paired:],
            none[:, paired:],
        ],
        axis=1,
    )
    group_bias = jnp.concatenate([group_bias, group_bias])
    tall, turned = (SLOT_PATCHES, width), (width, SLOT_PATCHES)

    def of_slot(ref, info):
        return ref.at[pl.ds(pl.multiple_of(info.slot * SLOT_PATCHES, 16), SLOT_PATCHES)]

    a1, a1_t, x_rows = call(
        prepare_kernel,
        "prepare",
        [(tall, BF16), (turned, BF16), ((share, width), F32)],
        (params, block_in),
        views={1: (tall, of_slot)},
        scratch=[pltpu.VMEM(tall, F32)],
    )
    dy, dy_t, dy_sum = call(
        join_kernel,
        "join",
        [(tall, BF16), (turned, BF16), ((8, width), F32)],
        (params, cotangent, swap(cotangent, "head", 1)),
        specs={1: IN_VMEM, 2: IN_VMEM},
        scratch=[pltpu.VMEM(tall, F32)],
    )

    attn_w.near(a1)
    attn_w.rest_own()
    attn_w.rest_x(attn_w.d_first)
    mlp_w.far(attn_w.d_first)
    attn_own, attn_other = (settle(p, False) for p in attn_w.pieces())

    def attend(pieces, group_mask, a1, *before):
        return call(
            attend_kernel,
            "attend",
            [
                (tall, BF16),
                ((SLOT_PATCHES, 2 * paired), BF16),
                ((SLOT_PATCHES, paired), F32),
                (tall, BF16),
            ],
            (params, a1, group_bias, *before, *(a for a, _ in pieces)),
            specs={i + len(before): ANYWHERE for i in range(3, 3 + len(pieces))},
            lazy=range(3, 3 + len(before)),
            scratch=[pltpu.VMEM((width, width), BF16), pltpu.SemaphoreType.DMA((count,))],
            flops=2 * SLOT_PATCHES * (width * width + 12 * SLOT_PATCHES * HEAD_WIDTH),
            rels=[r for _, r in pieces],
            added=len(before),
            group_mask=group_mask,
        )

    own_saved = attend(attn_own, 0, a1)
    mlp_w.near(own_saved[3], attn_w.x_second, attn_w.d_second)
    other_saved = attend(attn_other, 2, after(a1, mlp_w.first), own_saved[3])
    mlp_w.rest_own(other_saved[3])
    proj = after(other_saved[3], mlp_w.second, mlp_w.x_first, mlp_w.y_first)
    h1, a2, a2_t = call(
        middle_kernel,
        "middle",
        [(tall, F32), (tall, BF16), (turned, BF16)],
        (
            params,
            block_in,
            proj,
            swap(proj, "head", 1),
        ),
        views={1: (tall, of_slot)},
    )

    def mlp(pieces, group_mask, rels, order, *before):
        first = 6 + len(before)
        *grads, keep, send, da2, dbias = call(
            mlp_kernel,
            "mlp",
            [((len(r), 2, part_rows, width), BF16, ANYWHERE) for r in written(rels)]
            + [
                ((padded, width), BF16),
                ((padded, width), BF16),
                (tall, BF16),
                ((8, hidden_cols), F32),
            ],
            (params, a2, a2_t, dy, dy_t, order, *before, *(a for a, _ in pieces)),
            specs={i: ANYWHERE for i in (5, *range(first, first + len(pieces)))},
            lazy=(2, 3, 4, *range(6, first)),
            scratch=[pltpu.VMEM((width, hidden_cols), BF16) for _ in range(4)]
            + [pltpu.VMEM(tall, F32), pltpu.SemaphoreType.DMA((2, count))],
            flops=12 * SLOT_PATCHES * width * hidden_cols,
            rels=[r for _, r in pieces],
            out_rels=written(rels),
            group_mask=group_mask,
            added=len(before),
            share=share,
        )
        return parts(True, grads, rels), keep, send, da2, dbias

    mlp_w.rest_other(a2, dy_t)
    mlp_own, mlp_other = (settle(p, True) for p in mlp_w.pieces())
    mlp_sum, attn_sum = Scatter(count), Scatter(count)
    own_mlp = mlp(mlp_own, 0, own_rels, after(params, mlp_w.d_first))
    mlp_sum.own(own_mlp[0])
    mlp_sum.own_rest()
    other_mlp = mlp(mlp_other, 2, other_rels, own_mlp[4], *own_mlp[1:4])
    peer_rows = swap(other_mlp[2], "head", 1)
    peer_mlp = swap(other_mlp[3], "head", 1)
    mlp_sum.other(other_mlp[0], peer_rows)
    back_outs = [((padded, width), BF16), ((padded, width), BF16), ((8, 5 * paired), F32)]
    back_scratch = [
        pltpu.VMEM((width, width), BF16),
        pltpu.VMEM((width, width), BF16),
        pltpu.VMEM((SLOT_PATCHES, 5 * paired), BF16),
        pltpu.VMEM(tall, F32),
        pltpu.SemaphoreType.DMA((count,)),
    ]
    back_flops = 2 * SLOT_PATCHES * (2 * width * width + 60 * SLOT_PATCHES * HEAD_WIDTH)

    def back_parts(rels):
        return [((len(r), part_rows, width), BF16, ANYWHERE) for r in written(rels)]

    *grads, keep, send, sums, e, e_t, dh1_rows, block_out, mid_sums = call(
        first_back_kernel,
        "first_back",
        back_parts(other_rels)
        + back_outs
        + [
            (tall, BF16),
            (turned, BF16),
            ((share, width), F32),
            ((share, width), BF16, IN_VMEM),
            ((8, width), F32),
        ],
        (
            params,
            h1,
            dy,
            other_mlp[3],
            peer_mlp,
            other_mlp[1],
            peer_rows,
            a1_t,
            *other_saved[:3],
            *(a for a, _ in attn_other),
        ),
        specs={i: ANYWHERE for i in range(11, 11 + len(attn_other))},
        lazy=(7, 8, 9, 10),
        scratch=back_scratch,
        flops=back_flops,
        rels=[r for _, r in attn_other],
        out_rels=written(other_rels),
        share=share,
    )
    other_back = parts(False, grads, other_rels), keep, send, sums
    attn_sum.other(other_back[0])
    mlp_sum.turn(e)
    mlp_sum.near_sum(other_back[3])
    *grads, keep, send, sums = call(
        second_back_kernel,
        "second_back",
        back_parts(own_rels) + back_outs,
        (
            params,
            e,
            e_t,
            a1_t,
            *own_saved[:3],
            *other_back[1:3],
            *(a for a, _ in attn_own),
        ),
        specs={i: ANYWHERE for i in range(9, 9 + len(attn_own))},
        lazy=(2, 3, 4, 5, 6, 7, 8),
        scratch=back_scratch,
        flops=back_flops,
        rels=[r for _, r in attn_own],
        out_rels=written(own_rels),
        share=share,
    )
    own_back = parts(False, grads, own_rels), keep, send, sums
    done = (mlp_sum.from_near, mlp_sum.from_both, attn_sum.from_d, attn_sum.from_x)
    mlp_sum.far()
    peer_back = swap(own_back[2], "head", 1)
    attn_sum.own(own_back[0], *done, mlp_sum.away_total)
    attn_sum.turn_by_x(own_back[3])
    input_grad, small = call(
        last_kernel,
        "last",
        [((share, width), F32), ((PARAM_ROWS, width), F32)],
        (
            params,
            x_rows,
            dh1_rows,
            dy_sum,
            own_back[1],
            peer_back,
            mid_sums,
            own_mlp[4],
            other_mlp[4],
            own_back[3],
            other_back[3],
        ),
    )
    attn_sum.own_rest_joined(mlp_sum.away_total)
    attn_sum.near_sum(mlp_sum.away_total)
    attn_sum.far()
    by_row = (3, shard_rows, head_cols)
    fc1, fc2 = w_fc1.shape, w_fc2.T.shape
    *fc1_outs, fc2_grad, fc2_mom, fc2_new, fc2_avg = block_call(
        finish_mlp_kernel,
        "finish_mlp",
        [(fc1, F32)] * 4 + [(fc2, F32)] * 4,
        (
            after(w_fc1, attn_sum.away_total),
            mom_fc1,
            avg_fc1,
            w_fc2.T,
            mom_fc2.T,
            avg_fc2.T,
            *mlp_sum.terms(),
        ),
    )
    fc1_grad, fc1_mom, fc1_new, fc1_avg = fc1_outs
    fc2_grad, fc2_mom, fc2_new, fc2_avg = (v.T for v in (fc2_grad, fc2_mom, fc2_new, fc2_avg))
    small = small + swap(small, "head", 1)
    small = after(small, mlp_sum.from_away)
    over = over_x(small), over_y(small), over_both(small)
    small = (small + over[0]) + (over[1] + over[2])
    small = after(small, fc1_grad)
    for mask in line_masks(count):
        if mask == 2:
            small = after(small, attn_sum.from_away)
        small = small + swap(small, "dp", mask)
    gain_grad = small[:2]
    bias_grad = small[2:12].reshape(biases.shape)

    *qkv_outs, proj_grad, proj_mom, proj_new, proj_avg = block_call(
        finish_attn_kernel,
        "finish_attn",
        [(by_row, F32)] * 4 + [(w_proj.shape, F32)] * 4,
        (
            *(jnp.swapaxes(v, 0, 1) for v in (w_qkv, mom_qkv, avg_qkv)),
            w_proj,
            mom_proj,
            avg_proj,
            *attn_sum.terms(),
        ),
    )
    qkv_grad, qkv_mom, qkv_new, qkv_avg = (jnp.swapaxes(v, 0, 1) for v in qkv_outs)

    gain_mom_new, gain_new, gain_avg_new = update(
        gains, gain_grad, gain_mom, gain_avg, RATE_SMALL, 0.0
    )
    bias_mom_new, bias_new, bias_avg_new = update(
        biases, bias_grad, bias_mom, bias_avg, RATE_SMALL, 0.0
    )
    return (
        block_out,
        input_grad,
        qkv_grad,
        qkv_mom,
        qkv_new,
        qkv_avg,
        proj_grad,
        proj_mom,
        proj_new,
        proj_avg,
        fc1_grad,
        fc1_mom,
        fc1_new,
        fc1_avg,
        fc2_grad,
        fc2_mom,
        fc2_new,
        fc2_avg,
        gain_grad,
        gain_mom_new,
        gain_new,
        gain_avg_new,
        bias_grad,
        bias_mom_new,
        bias_new,
        bias_avg_new,
    )
def solution(mesh):
    return jax.shard_map(
        shards,
        mesh=mesh,
        in_specs=(
            P("dp", None),
            P("dp"),
            P(("dp", "head"), None),
            P("dp", None, "head"),
            P("head", "dp"),
            P("dp", "head"),
            P("head", "dp"),
            P("dp", None, "head"),
            P("head", "dp"),
            P("dp", "head"),
            P("head", "dp"),
            P("dp", None, "head"),
            P("head", "dp"),
            P("dp", "head"),
            P("head", "dp"),
            P(),
            P(),
            P(),
            P(),
            P(),
            P(),
        ),
        out_specs=(
            P(("dp", "head"), None),
            P(("dp", "head"), None),
            P("dp", None, "head"),
            P("dp", None, "head"),
            P("dp", None, "head"),
            P("dp", None, "head"),
            P("head", "dp"),
            P("head", "dp"),
            P("head", "dp"),
            P("head", "dp"),
            P("dp", "head"),
            P("dp", "head"),
            P("dp", "head"),
            P("dp", "head"),
            P("head", "dp"),
            P("head", "dp"),
            P("head", "dp"),
            P("head", "dp"),
            P(),
            P(),
            P(),
            P(),
            P(),
            P(),
            P(),
            P(),
        ),
        check_vma=False,
    )
```

```python
import jax
import jax.numpy as jnp
from jax import lax
from jax.experimental import pallas as pl
from jax.experimental.pallas import tpu as pltpu
from jax.sharding import PartitionSpec as P

HEAD_WIDTH = 64
SLOT_PATCHES = 784
LOWRES = 196


EPSILON = 1e-06
MOMENTUM_RATE = 0.9
AVERAGING = 0.75
WEIGHT_DECAY = 0.05
RATE_QKV = 0.001
RATE_PROJ = 0.01
RATE_FC1 = 0.0006
RATE_FC2 = 0.0003
RATE_SMALL = 0.003
MASKED = -1e30
SCALE = HEAD_WIDTH**-0.5
F32 = jnp.float32
BF16 = jnp.bfloat16
QUERY_ROWS = SLOT_PATCHES // 2
VMEM_LIMIT = 60 << 20
COST = 16
GAINS, BIASES, KIND, PARAM_ROWS = 0, 2, 12, 16

IN_VMEM = pl.BlockSpec(memory_space=pltpu.VMEM)
ANYWHERE = pl.BlockSpec(memory_space=pl.ANY)


def update(weight, gradient, moment, average, step_rate, decay_rate):
    step_grad = gradient + decay_rate * weight
    moment_new = MOMENTUM_RATE * moment + step_grad
    weight_new = weight - step_rate * (step_grad + MOMENTUM_RATE * moment_new)
    return (moment_new, weight_new, AVERAGING * average + (1.0 - AVERAGING) * weight_new)


def swap(value, axis, mask):
    return lax.ppermute(value, axis, [(i, i ^ mask) for i in range(lax.axis_size(axis))])


def line_masks(count):
    masks, mask = [], count // 2
    while mask > 1:
        masks.append(mask)
        mask //= 2
    return masks


def line_order(count):
    order = [0]
    for mask in line_masks(count):
        order = order + [r ^ mask for r in order]
    return order


def z_sets(count):
    order = line_order(count)
    eighth = count // 8
    return order[:eighth], order[eighth : 2 * eighth], order[2 * eighth :]


def flip(order):
    return [r ^ 1 for r in order]


def after(value, *others):
    return lax.optimization_barrier((value, *others))[0]


def both_after(values, *others):
    return lax.optimization_barrier((*values, *others))[: len(values)] if others else values


def over_x(value):
    return swap(value, "head", 2)


def over_y(value):
    return swap(value, "dp", 1)


def over_both(value):
    members = lax.axis_size("head")
    total = members * lax.axis_size("dp")
    return lax.ppermute(value, ("dp", "head"), [(i, i ^ members ^ 2) for i in range(total)])


def over_z(value):
    return swap(value, "dp", 2)


def over_far(value, count):
    return swap(value, "dp", line_masks(count)[-2])


class Gather:
    def __init__(self, shard, count):
        base = shard[None]
        for mask in line_masks(count)[:-2]:
            base = jnp.concatenate([base, swap(base, "dp", mask)])
        self.base, self.count = base, count

    def far(self, *later):
        self.base = both_after((self.base,), *later)[0]
        self.first = jnp.concatenate([self.base, over_far(self.base, self.count)])

    def near(self, *later):
        self.first = both_after((self.first,), *later)[0]
        self.second = over_z(self.first)
        self.x_first, self.y_first = over_x(self.first), over_y(self.first)

    def rest_own(self, *later):
        second, y_first = both_after((self.second, self.y_first), *later)
        self.y_second, self.d_first = over_y(second), over_x(after(y_first, self.x_first))

    def rest_x(self, *later):
        second = both_after((self.second,), *later)[0]
        self.x_second, self.d_second = over_x(second), over_x(self.y_second)

    def rest_other(self, *later):
        second, d_first = both_after((self.second, self.d_first), self.d_first, *later)
        self.x_second, self.d_second = over_x(second), over_z(d_first)

    def pieces(self):
        base, away, near = z_sets(self.count)
        rels = base + away, near
        own = (self.first, self.second, self.y_first, self.y_second)
        other = (self.x_first, self.x_second, self.d_first, self.d_second)
        turned = tuple(flip(r) for r in rels)
        return tuple(zip(own, rels + turned)), tuple(zip(other, rels + turned))


def joined(pieces, count, me):
    order = [r for _, rel in pieces for r in rel]
    place = jnp.array([order.index(r) for r in range(count)], jnp.int32)
    return jnp.concatenate([a for a, _ in pieces])[place[jnp.arange(count, dtype=jnp.int32) ^ me]]


def part_rels(count):
    base, away, near = z_sets(count)
    own = (base, away, near, flip(near), flip(base + away))
    other = (base + away + near, flip(near), flip(base + away))
    return own, other


def parted(whole, rels, me):
    return tuple(whole[jnp.array(rel, jnp.int32) ^ me] for rel in rels)


def plus(*terms):
    return sum(t.astype(F32) for t in terms)


def low_plus(*terms):
    return plus(*terms).astype(BF16)


class Scatter:
    def __init__(self, count):
        self.count = count

    def own(self, parts, *later):
        self.base, self.away, self.near, y_near, y_rest = parts
        y_near, y_rest = both_after((y_near, y_rest), *later)
        self.from_y_near, self.y_rest = over_y(y_near), y_rest

    def own_rest(self, *later):
        self.from_y = over_y(both_after((self.y_rest,), *later)[0])

    def turn_by_x(self, *later):
        rest, from_d = both_after((self.d_rest, self.from_d), *later)
        self.from_both, self.to_y = None, over_x(low_plus(rest, from_d))

    def own_rest_joined(self, *later):
        rest, to_y = both_after((self.y_rest, self.to_y), *later)
        self.from_y = over_y(low_plus(rest, to_y))

    def arrived(self):
        every = (self.from_y, self.from_both, self.from_near, self.from_x)
        return tuple(v for v in every if v is not None)

    def other(self, parts, *later):
        xs, d_near, self.d_rest = parts
        xs, d_near = both_after((xs, d_near), *later)
        self.from_d, self.from_x = over_z(d_near), over_x(xs)

    def turn(self, *later):
        rest, from_d = both_after((self.d_rest, self.from_d), *later)
        self.from_both = over_both(low_plus(rest, from_d))

    def near_sum(self, *later):
        near = both_after((self.near,), *later)[0]
        cut = 2 * self.base.shape[0]
        self.near_total = low_plus(near, self.from_y_near, self.from_x[cut:])
        self.from_near = over_z(self.near_total)

    def far(self, *later):
        cut = self.base.shape[0]
        away = both_after((self.away,), *later)[0]
        rest = self.arrived()
        self.away_total = low_plus(away, *(r[cut : 2 * cut] for r in rest))
        self.from_away = over_far(self.away_total, self.count)

    def terms(self):
        cut = self.base.shape[0]
        rest = self.arrived()
        terms = (self.base, self.from_away, *(r[:cut] for r in rest))
        masks = line_masks(self.count)[:-2]
        if not masks:
            return (self.base, self.from_away, *rest)
        total = plus(*terms)
        for mask in reversed(masks):
            keep = total.shape[0] // 2
            total = total[:keep] + swap(total[keep:].astype(BF16), "dp", mask)
        return (total[:1],)


def dot(a, b):
    return jnp.dot(a, b, preferred_element_type=F32)


def dot_t(a, b):
    return lax.dot_general(a, b, (((1,), (1,)), ((), ())), preferred_element_type=F32)


def t_dot(a, b):
    return lax.dot_general(a, b, (((0,), (0,)), ((), ())), preferred_element_type=F32)


def normalize(inputs):
    mean_row = jnp.mean(inputs, axis=-1, keepdims=True)
    centred = inputs - mean_row
    spread = jnp.mean(centred * centred, axis=-1, keepdims=True)
    inv_std = lax.rsqrt(spread + EPSILON)
    return (centred * inv_std, inv_std)


def norm_back(grad_out, centred, inv_std, gain_row):
    scaled = grad_out * gain_row
    return inv_std * (
        scaled
        - jnp.mean(scaled, axis=-1, keepdims=True)
        - centred * jnp.mean(scaled * centred, axis=-1, keepdims=True)
    )


def piece_copies(info, refs, rels, dest, sems, out=False, at=()):
    copies = []
    for ref, rel in zip(refs, rels):
        for j, r in enumerate(rel):
            rows = ref.shape[-2]
            start = 0 if r is None else pl.multiple_of((info.me ^ r) * rows, rows)
            there, here = ref.at[(j, *at)], dest.at[pl.ds(start, rows)]
            copies.append((here, there) if out else (there, here))
    copies = [
        pltpu.make_async_copy(a, b, sems.at[i]) for i, (a, b) in enumerate(copies)
    ]
    for copy in copies:
        copy.start()
    return copies


def wait_all(copies):
    for copy in copies:
        copy.wait()


class Info:
    def __init__(self, params):
        self.me, self.member = lax.axis_index("dp"), lax.axis_index("head")
        self.slot, self.core = self.member // 2, lax.rem(self.member, 2)
        self.params = params

    def kind(self):
        return self.params[KIND : KIND + 1, 0:1]

    def gain(self, i):
        return self.params[GAINS + i : GAINS + i + 1, :]

    def bias(self, i):
        return self.params[BIASES + i : BIASES + i + 1, :]


class Lazy:
    def __init__(self, source, here, sem):
        self.here, self.shape, self.waits = here, here.shape, True
        self.copy = pltpu.make_async_copy(source, here, sem)

    def start(self):
        self.copy.start()

    def ready(self):
        if self.waits:
            self.copy.wait()
            self.waits = False
        return self.here

    def __getitem__(self, at):
        return self.ready()[at]


class Early:
    def __init__(self, target, here, sem):
        self.here, self.shape, self.dtype, self.stays = here, here.shape, here.dtype, True
        self.copy = pltpu.make_async_copy(here, target, sem)

    def flush(self):
        if self.stays:
            self.copy.start()
            self.stays = False

    def __setitem__(self, at, value):
        self.here[at] = value

    def __getitem__(self, at):
        return self.here[at]


def start_all(values):
    for value in values:
        value.start()


def lanes():
    return lax.broadcasted_iota(jnp.int32, (1, 2 * HEAD_WIDTH), 1)


def segments(shape, axis, start, info):
    run = (lax.broadcasted_iota(jnp.int32, shape, axis) + start) // LOWRES
    return jnp.where(info.kind() > 0.0, 0, run)


def column_sum(rows):
    return jnp.sum(rows, axis=0, keepdims=True)


def cast_kernel(w_qkv, w_proj, w_fc1, w_fc2, attn, mlp):
    wide = 2 * HEAD_WIDTH
    for i in range(3):
        attn[:, i * wide : (i + 1) * wide] = w_qkv[i, :, :wide].astype(BF16)
    single = [w_qkv[i, :, wide:] for i in range(3)]
    proj = w_proj[...].T
    attn[:, 3 * wide : 4 * wide] = jnp.concatenate(single[:2], axis=1).astype(BF16)
    attn[:, 4 * wide : 5 * wide] = jnp.concatenate([single[2], proj[:, wide:]], axis=1).astype(BF16)
    attn[:, 5 * wide : 6 * wide] = proj[:, :wide].astype(BF16)
    mlp[0] = w_fc1[...].astype(BF16)
    mlp[1] = w_fc2[...].astype(BF16)


def prepare_kernel(info, block, a1, a1_t, x_rows, rows):
    share = x_rows.shape[0]
    x = block[...].astype(F32)
    rows[...] = x
    x_rows[...] = rows[pl.ds(pl.multiple_of(info.core * share, 8), share), :]
    x_rows.flush()
    xhat, _ = normalize(x)
    normed = (xhat * info.gain(0) + info.bias(0)).astype(BF16)
    a1[...] = normed
    a1.flush()
    a1_t[...] = normed.T


def join_kernel(info, mine, peer, dy, dy_t, total, rows):
    share = mine.shape[0]
    start = pl.multiple_of(info.core * share, 8)
    own = mine[...].astype(F32)
    rows[pl.ds(start, share), :] = own
    rows[pl.ds(pl.multiple_of(share - start, 8), share), :] = peer[...].astype(F32)
    low = rows[...].astype(BF16)
    dy[...] = low
    dy.flush()
    total[0:1, :] = column_sum(own)
    dy_t[...] = low.T


def attend_kernel(info, a1, bias, *rest, rels, added, group_mask):
    before, rest = rest[:added], rest[added:]
    count = len(rels)
    pieces, (qkv, out, lse, proj, w, sems) = rest[:count], rest[count:]
    copies = piece_copies(info, pieces, rels, w, sems)
    start_all(before)
    wait_all(copies)
    lane = lanes()
    low = lane < HEAD_WIDTH
    zero = jnp.zeros((), BF16)
    bias = bias.ready()[pl.ds(info.member ^ group_mask, 1), :]
    m = dot(a1[...], w[:, :640]) + bias
    k01, v01 = m[:, 128:256].astype(BF16), m[:, 256:384].astype(BF16)
    pair = m[:, 384:512]
    k2 = pltpu.roll(pair, HEAD_WIDTH, 1).astype(BF16)
    v2 = m[:, 512:640].astype(BF16)
    qkv[:, 0:128] = (m[:, 0:128] * SCALE).astype(BF16)
    qkv[:, 128:256] = k01
    qkv[:, 256:384] = v01
    qkv[:, 384:512] = jnp.where(low, pair * SCALE, 0.0).astype(BF16)
    qkv[:, 512:640] = k2
    qkv[:, 640:768] = v2
    qkv.flush()
    columns = segments((1, SLOT_PATCHES), 1, 0, info)
    for start in range(0, SLOT_PATCHES, QUERY_ROWS):
        rows = slice(start, start + QUERY_ROWS)
        seen = segments((QUERY_ROWS, 1), 0, start, info) == columns
        q01 = qkv[rows, 0:128]
        outs, logs = [], []
        for query, keys, value in (
            (jnp.where(low, q01, zero), k01, v01),
            (jnp.where(low, zero, q01), k01, v01),
            (qkv[rows, 384:512], k2, v2),
        ):
            scores = jnp.where(seen, dot_t(query, keys), MASKED)
            largest = jnp.max(scores, axis=-1, keepdims=True)
            expon = jnp.exp(scores - largest)
            summed = jnp.sum(expon, axis=-1, keepdims=True)
            probs = (expon * (1.0 / summed)).astype(BF16)
            outs.append(dot(probs, value))
            logs.append(largest + jnp.log(summed))
        third = jnp.where(low, 0.0, pltpu.roll(outs[2], HEAD_WIDTH, 1))
        out[rows, 0:128] = third.astype(BF16)
        out[rows, 128:256] = jnp.where(low, outs[0], outs[1]).astype(BF16)
        lse[rows, :] = jnp.where(lane == 0, logs[0], jnp.where(lane == 1, logs[1], logs[2]))
    out.flush()
    lse.flush()
    total = dot_t(out[...], w[:, 512:768])
    proj[...] = plus(total, *(b[...] for b in before)).astype(BF16)


def middle_kernel(info, block, mine, peer, h1, a2, a2_t):
    both = plus(mine[...], peer[...])
    middle = block[...].astype(F32) + (both + info.bias(2))
    h1[...] = middle
    h1.flush()
    xhat, _ = normalize(middle)
    normed = (xhat * info.gain(1) + info.bias(1)).astype(BF16)
    a2[...] = normed
    a2.flush()
    a2_t[...] = normed.T


def split_rows(info, total, scratch, share, keep, send, before, at=0):
    start = pl.multiple_of(info.core * share, 8)
    scratch[...] = total
    kept = scratch[pl.ds(start, share), :]
    keep[:share, :] = plus(kept, *(b[:share, :] for b in before[:1])).astype(keep.dtype)
    theirs = scratch[pl.ds(pl.multiple_of(share - start, 8), share), :]
    sent = plus(theirs, *(b[at : at + share, :] for b in before[1:]))
    send[at : at + share, :] = sent.astype(send.dtype)


def mlp_kernel(
    info, a2, a2_t, dy, dy_t, order, *rest, rels, out_rels, group_mask, added, share
):
    before, rest = rest[:added], rest[added:]
    count, outs = len(rels), len(out_rels)
    pieces, rest = rest[:count], rest[count:]
    parts, (keep, send, da2, dbias, w1, w2, dw1, dw2, rows, sems) = rest[:outs], rest[outs:]
    first = piece_copies(info, pieces, rels, w1, sems.at[0], at=(0,))
    second = piece_copies(info, pieces, rels, w2, sems.at[1], at=(1,))
    start_all((dy, dy_t, a2_t, *before))
    wait_all(first)
    bias = info.params.ready()[pl.ds(BIASES + 6 + (info.member ^ group_mask), 1), :]
    u = dot(a2[...], w1[...]) + bias
    phi = 0.5 + 0.5 * lax.erf(u * (2.0**-0.5))
    hidden = (u * phi).astype(BF16)
    slope = phi + u * (jnp.exp(-0.5 * u * u) * 0.3989422804014327)
    wait_all(second)
    dpre = (dot(dy[...], w2[...]) * slope).astype(BF16)
    dw2[...] = dot(dy_t[...], hidden).astype(BF16)
    second = piece_copies(info, parts, out_rels, dw2, sems.at[1], out=True, at=(1,))
    dw1[...] = dot(a2_t[...], dpre).astype(BF16)
    first = piece_copies(info, parts, out_rels, dw1, sems.at[0], out=True, at=(0,))
    da2[...] = plus(dot_t(dpre, w1[...]), *(b[...] for b in before[2:])).astype(BF16)
    da2.flush()
    split_rows(info, dot_t(hidden, w2[...]), rows, share, keep, send, before[:2])
    dbias[0:1, :] = column_sum(dpre.astype(F32))
    wait_all(first)
    wait_all(second)


def middle_back(info, h1, dy, mine, peer, kept, peer_rows, e, e_t, dh1_rows, block_out, sums, rows):
    share = block_out.shape[0]
    start = pl.multiple_of(info.core * share, 8)
    xhat, inv_std = normalize(h1[...])
    da2 = plus(mine[...], peer[...])
    dh1 = dy[...].astype(F32) + norm_back(da2, xhat, inv_std, info.gain(1))
    low = dh1.astype(BF16)
    e[...] = low
    e.flush()
    e_t[...] = low.T
    e_t.flush()
    rows[...] = dh1
    dh1_rows[...] = rows[pl.ds(start, share), :]
    dh1_rows.flush()
    sums[0:1, :] = column_sum(da2 * xhat)
    sums[1:2, :] = column_sum(da2)
    sums[2:3, :] = column_sum(dh1)
    sums.flush()
    mlp = plus(kept[:share, :], peer_rows[:share, :])
    block_out[...] = ((h1.ready()[pl.ds(start, share), :] + mlp) + info.bias(3)).astype(BF16)


def first_back_kernel(
    info, h1, dy, mine, peer, kept, peer_rows, a1_t, qkv, out, lse, *rest, rels, out_rels, share
):
    count, outs = len(rels), len(out_rels)
    pieces, rest = rest[:count], rest[count:]
    parts, rest = rest[:outs], rest[outs:]
    keep, send, sums, e, e_t, dh1_rows, block_out, mid, w, dw, grads, rows, sems = rest
    copies = piece_copies(info, pieces, rels, w, sems)
    start_all((qkv, lse, out, a1_t))
    middle_back(
        info, h1, dy, mine, peer, kept, peer_rows, e, e_t, dh1_rows, block_out, mid, rows
    )
    wait_all(copies)
    attend_back(
        info, e, e_t, a1_t, qkv, out, lse, (), parts, out_rels, share, keep, send, sums,
        w, dw, grads, rows, sems,
    )


def second_back_kernel(
    info, e, e_t, a1_t, qkv, out, lse, kept, sent, *rest, rels, out_rels, share
):
    count, outs = len(rels), len(out_rels)
    pieces, rest = rest[:count], rest[count:]
    parts, (keep, send, sums, w, dw, grads, rows, sems) = rest[:outs], rest[outs:]
    copies = piece_copies(info, pieces, rels, w, sems)
    start_all((qkv, lse, out, a1_t, e_t, kept, sent))
    wait_all(copies)
    attend_back(
        info, e, e_t, a1_t, qkv, out, lse, (kept, sent), parts, out_rels, share, keep, send, sums,
        w, dw, grads, rows, sems,
    )


def attend_back(
    info, e, e_t, a1_t, qkv, out, lse, before, parts, out_rels, share, keep, send, sums,
    w, dw, grads, rows, sems,
):
    low = lanes() < HEAD_WIDTH
    zero = jnp.zeros((), BF16)
    dout = dot(e[...], w[:, 512:768])
    do2 = jnp.where(low, pltpu.roll(dout[:, 0:128], HEAD_WIDTH, 1), 0.0).astype(BF16)
    do01 = dout[:, 128:256].astype(BF16)
    q01, k01, v01 = qkv[:, 0:128], qkv[:, 128:256], qkv[:, 256:384]
    q2, k2, v2 = qkv[:, 384:512], qkv[:, 512:640], qkv[:, 640:768]
    lse_t = jnp.transpose(lse[...], (1, 0))
    seen = segments((SLOT_PATCHES, 1), 0, 0, info) == segments((1, SLOT_PATCHES), 1, 0, info)
    dq, dk, dv = [], [], []
    for head, (query, keys, value, dcontext) in enumerate(
        (
            (q01, jnp.where(low, k01, zero), jnp.where(low, v01, zero), do01),
            (q01, jnp.where(low, zero, k01), jnp.where(low, zero, v01), do01),
            (q2, k2, jnp.where(low, v2, zero), do2),
        )
    ):
        scores = jnp.where(seen, dot_t(keys, query), MASKED)
        probs = jnp.exp(scores - lse_t[head : head + 1, :])
        dprob = dot_t(value, dcontext)
        row_dot = column_sum(probs * dprob)
        dscore = (probs * (dprob - row_dot)).astype(BF16)
        dv.append(dot(probs.astype(BF16), dcontext))
        dk.append(dot(dscore, query))
        dq.append(t_dot(dscore, keys))
    grads[:, 0:128] = (jnp.where(low, dq[0], dq[1]) * SCALE).astype(BF16)
    grads[:, 128:256] = jnp.where(low, dk[0], dk[1]).astype(BF16)
    grads[:, 256:384] = jnp.where(low, dv[0], dv[1]).astype(BF16)
    shifted = pltpu.roll(dk[2], HEAD_WIDTH, 1)
    grads[:, 384:512] = jnp.where(low, dq[2] * SCALE, shifted).astype(BF16)
    grads[:, 512:640] = jnp.where(low, dv[2], 0.0).astype(BF16)
    dw[:, 0:512] = dot(a1_t[...], grads[:, 0:512]).astype(BF16)
    dw[:, 512:640] = (dot(a1_t[...], grads[:, 512:640]) + dot(e_t[...], out[:, 0:128])).astype(BF16)
    dw[:, 640:768] = dot(e_t[...], out[:, 128:256]).astype(BF16)
    copies = piece_copies(info, parts, out_rels, dw, sems, out=True)
    split_rows(info, dot_t(grads[...], w[:, 0:640]), rows, share, keep, send, before)
    sums[0:1, :] = column_sum(grads[...].astype(F32))
    wait_all(copies)


def last_kernel(
    info, x_rows, dh1_rows, mine, kept, peer, mid, db0, db1, s0, s1, input_grad, small
):
    share = x_rows.shape[0]
    xhat, inv_std = normalize(x_rows[...])
    da1 = plus(kept[:share, :], peer[:share, :])
    input_grad[...] = dh1_rows[...] + norm_back(da1, xhat, inv_std, info.gain(0))
    input_grad.flush()
    once = jnp.where(info.core == 0, 1.0, 0.0)
    member = info.member
    small[...] = jnp.zeros(small.shape, F32)
    small[0:1, :] = column_sum(da1 * xhat)
    small[1:2, :] = once * mid[0:1, :]
    small[2:3, :] = column_sum(da1)
    small[3:4, :] = once * mid[1:2, :]
    small[4:5, :] = once * mid[2:3, :]
    small[5:6, :] = mine[0:1, :]
    low = lanes() < HEAD_WIDTH
    for row, pair, single in ((6, 0, 384), (7, 256, 512)):
        for group in range(0, 4, 2):
            even, odd = (
                tuple(
                    jnp.where(
                        member == which,
                        s0[0:1, at : at + 128],
                        jnp.where(member == which ^ 2, s1[0:1, at : at + 128], 0.0),
                    )
                    for at in (pair, single)
                )
                for which in (group, group + 1)
            )
            turned = pltpu.roll(odd[0], HEAD_WIDTH, 1)
            at = group * 192
            small[row : row + 1, at : at + 128] = even[0]
            small[row : row + 1, at + 128 : at + 256] = jnp.where(low, even[1], turned)
            small[row : row + 1, at + 256 : at + 384] = jnp.where(
                low, turned, pltpu.roll(odd[1], HEAD_WIDTH, 1)
            )
    small[pl.ds(8 + member, 1), :] = db0[0:1, :]
    small[pl.ds(8 + (member ^ 2), 1), :] = db1[0:1, :]


def step(weight, gradient, moment, average, outs, rate):
    for ref, value in zip(
        outs, (gradient, *update(weight, gradient, moment, average, rate, WEIGHT_DECAY))
    ):
        ref[...] = value
        if isinstance(ref, Early):
            ref.flush()


def finish_mlp_kernel(info, w1, m1, a1, w2, m2, a2, *rest):
    terms, outs = rest[:-8], rest[-8:]
    first, second = (plus(*(t[0, i] for t in terms)) for i in range(2))
    step(w1[...], first, m1[...], a1[...], outs[:4], RATE_FC1)
    step(w2[...], second, m2[...], a2[...], outs[4:], RATE_FC2)


def finish_attn_kernel(info, w1, m1, a1, w2, m2, a2, *rest):
    terms, outs = rest[:-8], rest[-8:]
    total = plus(*(t[0] for t in terms))
    wide = 2 * HEAD_WIDTH
    for i in range(3):
        single = 3 * wide + i * HEAD_WIDTH
        gradient = jnp.concatenate(
            [total[:, i * wide : (i + 1) * wide], total[:, single : single + HEAD_WIDTH]], axis=1
        )
        values = gradient, *update(w1[i], gradient, m1[i], a1[i], RATE_QKV, WEIGHT_DECAY)
        for out, value in zip(outs[:4], values):
            out[i] = value
    for out in outs[:4]:
        if isinstance(out, Early):
            out.flush()
    gradient = jnp.concatenate(
        [total[:, 5 * wide :], total[:, 5 * wide - HEAD_WIDTH : 5 * wide]], axis=1
    ).T
    step(w2[...], gradient, m2[...], a2[...], outs[4:], RATE_PROJ)


def call(kernel, name, outs, inputs, specs=None, scratch=(), flops=0, lazy=(), views=None, **fixed):
    results = [jax.ShapeDtypeStruct(s, d) for s, d, *_ in outs]
    specs, views = specs or {}, views or {}
    brought = [i for i in range(len(inputs)) if i not in specs]
    sent = [i for i, entry in enumerate(outs) if len(entry) == 2]
    moved = [jax.ShapeDtypeStruct(views[i][0], v.dtype) if i in views else v for i, v in enumerate(inputs)]
    moved = [moved[i] for i in brought] + [results[i] for i in sent]
    extra = [pltpu.VMEM(v.shape, v.dtype) for v in moved] + [pltpu.SemaphoreType.DMA((len(moved),))]
    size = sum(v.size * v.dtype.itemsize for v in (*inputs, *results))

    def body(*refs):
        refs = list(refs)
        cut = len(refs) - len(extra)
        here, sems = refs[cut:], refs[-1]
        info = Info(None)
        for n, i in enumerate(brought):
            source = views[i][1](refs[i], info) if i in views else refs[i]
            refs[i] = Lazy(source, here[n], sems.at[n])
            if i not in lazy:
                refs[i].start()
        leaving = []
        for n, i in enumerate(sent, len(brought)):
            refs[len(inputs) + i] = Early(refs[len(inputs) + i], here[n], sems.at[n])
            leaving.append(refs[len(inputs) + i])
        info.params = refs[0]
        kernel(info, *refs[1:cut], **fixed)
        info.params.ready()
        for value in leaving:
            value.flush()
        for value in leaving:
            value.copy.wait()

    body.__name__ = name
    return pl.pallas_call(
        body,
        out_shape=results,
        in_specs=[specs.get(i, ANYWHERE) for i in range(len(inputs))],
        out_specs=[entry[2] if len(entry) > 2 else ANYWHERE for entry in outs],
        scratch_shapes=[*scratch, *extra],
        compiler_params=pltpu.CompilerParams(vmem_limit_bytes=VMEM_LIMIT),
        cost_estimate=pl.CostEstimate(flops=flops // COST, bytes_accessed=size // COST, transcendentals=0),
        name=name,
    )(*inputs)


def block_call(kernel, name, outs, inputs):
    return pl.pallas_call(
        kernel,
        out_shape=[jax.ShapeDtypeStruct(s, d) for s, d in outs],
        in_specs=[IN_VMEM] * len(inputs),
        out_specs=[IN_VMEM] * len(outs),
        compiler_params=pltpu.CompilerParams(vmem_limit_bytes=VMEM_LIMIT),
        cost_estimate=pl.CostEstimate(flops=0, bytes_accessed=1 << 20, transcendentals=0),
        name=name,
    )(*inputs)


def shards(
    block_in,
    resolution,
    cotangent,
    w_qkv,
    w_proj,
    w_fc1,
    w_fc2,
    mom_qkv,
    mom_proj,
    mom_fc1,
    mom_fc2,
    avg_qkv,
    avg_proj,
    avg_fc1,
    avg_fc2,
    gains,
    gain_mom,
    gain_avg,
    biases,
    bias_mom,
    bias_avg,
):
    members = lax.axis_size("head")
    count = lax.axis_size("dp")
    member = lax.axis_index("head")
    me = lax.axis_index("dp")
    slot = member // 2
    width = block_in.shape[1]
    head_cols = w_qkv.shape[2]
    hidden_cols = w_fc1.shape[1]
    share = cotangent.shape[0]
    padded = -(-share // 16) * 16
    shard_rows = w_qkv.shape[0]
    aligned = shard_rows % 16 == 0
    paired = 2 * HEAD_WIDTH
    kind = jnp.where(slot == 0, resolution[0], resolution[1])
    bias_rows = biases.reshape(-1, width)
    params = jnp.concatenate(
        [
            gains,
            bias_rows,
            jnp.full((PARAM_ROWS - KIND, width), kind.astype(F32)),
        ]
    )

    attn_shard, mlp_shard = block_call(
        cast_kernel,
        "cast",
        [((shard_rows, width), BF16), ((2, shard_rows, width), BF16)],
        (jnp.swapaxes(w_qkv, 0, 1), w_proj, w_fc1, w_fc2.T),
    )
    attn_w, mlp_w = Gather(attn_shard, count), Gather(mlp_shard, count)
    attn_w.far()

    def settle(pieces, stacked):
        if aligned:
            return pieces
        whole = joined(pieces, count, me)
        if stacked:
            whole = jnp.swapaxes(whole, 0, 1).reshape(1, 2, width, width)
        else:
            whole = whole.reshape(1, width, width)
        return ((whole, (None,)),)

    own_rels, other_rels = part_rels(count)
    part_rows = shard_rows if aligned else width

    def written(rels):
        return rels if aligned else ((None,),)

    def parts(stacked, pieces, rels):
        if aligned:
            return tuple(pieces)
        whole = pieces[0][0]
        if stacked:
            whole = jnp.swapaxes(whole.reshape(2, count, shard_rows, width), 0, 1)
        else:
            whole = whole.reshape(count, shard_rows, width)
        return parted(whole, rels, me)

    q_bias, v_bias = (bias_rows[i].reshape(members, head_cols) for i in (4, 5))
    none = jnp.zeros_like(q_bias)
    group_bias = jnp.concatenate(
        [
            q_bias[:, :paired],
            none[:, :paired],
            v_bias[:, :paired],
            q_bias[:, paired:],
            none[:, paired:],
            v_bias[:, paired:],
            none[:, paired:],
        ],
        axis=1,
    )
    group_bias = jnp.concatenate([group_bias, group_bias])
    tall, turned = (SLOT_PATCHES, width), (width, SLOT_PATCHES)

    def of_slot(ref, info):
        return ref.at[pl.ds(pl.multiple_of(info.slot * SLOT_PATCHES, 16), SLOT_PATCHES)]

    a1, a1_t, x_rows = call(
        prepare_kernel,
        "prepare",
        [(tall, BF16), (turned, BF16), ((share, width), F32)],
        (params, block_in),
        views={1: (tall, of_slot)},
        scratch=[pltpu.VMEM(tall, F32)],
    )
    dy, dy_t, dy_sum = call(
        join_kernel,
        "join",
        [(tall, BF16), (turned, BF16), ((8, width), F32)],
        (params, cotangent, swap(cotangent, "head", 1)),
        specs={1: IN_VMEM, 2: IN_VMEM},
        scratch=[pltpu.VMEM(tall, F32)],
    )

    attn_w.near(a1)
    attn_w.rest_own()
    attn_w.rest_x(attn_w.d_first)
    mlp_w.far(attn_w.d_first)
    attn_own, attn_other = (settle(p, False) for p in attn_w.pieces())

    def attend(pieces, group_mask, a1, *before):
        return call(
            attend_kernel,
            "attend",
            [
                (tall, BF16),
                ((SLOT_PATCHES, 2 * paired), BF16),
                ((SLOT_PATCHES, paired), F32),
                (tall, BF16),
            ],
            (params, a1, group_bias, *before, *(a for a, _ in pieces)),
            specs={i + len(before): ANYWHERE for i in range(3, 3 + len(pieces))},
            lazy=range(3, 3 + len(before)),
            scratch=[pltpu.VMEM((width, width), BF16), pltpu.SemaphoreType.DMA((count,))],
            flops=2 * SLOT_PATCHES * (width * width + 12 * SLOT_PATCHES * HEAD_WIDTH),
            rels=[r for _, r in pieces],
            added=len(before),
            group_mask=group_mask,
        )

    own_saved = attend(attn_own, 0, a1)
    mlp_w.near(own_saved[3], attn_w.x_second, attn_w.d_second)
    other_saved = attend(attn_other, 2, after(a1, mlp_w.first), own_saved[3])
    mlp_w.rest_own(other_saved[3])
    proj = after(other_saved[3], mlp_w.second, mlp_w.x_first, mlp_w.y_first)
    h1, a2, a2_t = call(
        middle_kernel,
        "middle",
        [(tall, F32), (tall, BF16), (turned, BF16)],
        (
            params,
            block_in,
            proj,
            swap(proj, "head", 1),
        ),
        views={1: (tall, of_slot)},
    )

    def mlp(pieces, group_mask, rels, order, *before):
        first = 6 + len(before)
        *grads, keep, send, da2, dbias = call(
            mlp_kernel,
            "mlp",
            [((len(r), 2, part_rows, width), BF16, ANYWHERE) for r in written(rels)]
            + [
                ((padded, width), BF16),
                ((padded, width), BF16),
                (tall, BF16),
                ((8, hidden_cols), F32),
            ],
            (params, a2, a2_t, dy, dy_t, order, *before, *(a for a, _ in pieces)),
            specs={i: ANYWHERE for i in (5, *range(first, first + len(pieces)))},
            lazy=(2, 3, 4, *range(6, first)),
            scratch=[pltpu.VMEM((width, hidden_cols), BF16) for _ in range(4)]
            + [pltpu.VMEM(tall, F32), pltpu.SemaphoreType.DMA((2, count))],
            flops=12 * SLOT_PATCHES * width * hidden_cols,
            rels=[r for _, r in pieces],
            out_rels=written(rels),
            group_mask=group_mask,
            added=len(before),
            share=share,
        )
        return parts(True, grads, rels), keep, send, da2, dbias

    mlp_w.rest_other(a2, dy_t)
    mlp_own, mlp_other = (settle(p, True) for p in mlp_w.pieces())
    mlp_sum, attn_sum = Scatter(count), Scatter(count)
    own_mlp = mlp(mlp_own, 0, own_rels, after(params, mlp_w.d_first))
    mlp_sum.own(own_mlp[0])
    mlp_sum.own_rest()
    other_mlp = mlp(mlp_other, 2, other_rels, own_mlp[4], *own_mlp[1:4])
    peer_rows = swap(other_mlp[2], "head", 1)
    peer_mlp = swap(other_mlp[3], "head", 1)
    mlp_sum.other(other_mlp[0], peer_rows)
    back_outs = [((padded, width), BF16), ((padded, width), BF16), ((8, 5 * paired), F32)]
    back_scratch = [
        pltpu.VMEM((width, width), BF16),
        pltpu.VMEM((width, width), BF16),
        pltpu.VMEM((SLOT_PATCHES, 5 * paired), BF16),
        pltpu.VMEM(tall, F32),
        pltpu.SemaphoreType.DMA((count,)),
    ]
    back_flops = 2 * SLOT_PATCHES * (2 * width * width + 60 * SLOT_PATCHES * HEAD_WIDTH)

    def back_parts(rels):
        return [((len(r), part_rows, width), BF16, ANYWHERE) for r in written(rels)]

    *grads, keep, send, sums, e, e_t, dh1_rows, block_out, mid_sums = call(
        first_back_kernel,
        "first_back",
        back_parts(other_rels)
        + back_outs
        + [
            (tall, BF16),
            (turned, BF16),
            ((share, width), F32),
            ((share, width), BF16, IN_VMEM),
            ((8, width), F32),
        ],
        (
            params,
            h1,
            dy,
            other_mlp[3],
            peer_mlp,
            other_mlp[1],
            peer_rows,
            a1_t,
            *other_saved[:3],
            *(a for a, _ in attn_other),
        ),
        specs={i: ANYWHERE for i in range(11, 11 + len(attn_other))},
        lazy=(7, 8, 9, 10),
        scratch=back_scratch,
        flops=back_flops,
        rels=[r for _, r in attn_other],
        out_rels=written(other_rels),
        share=share,
    )
    other_back = parts(False, grads, other_rels), keep, send, sums
    attn_sum.other(other_back[0])
    mlp_sum.turn(e)
    mlp_sum.near_sum(other_back[3])
    *grads, keep, send, sums = call(
        second_back_kernel,
        "second_back",
        back_parts(own_rels) + back_outs,
        (
            params,
            e,
            e_t,
            a1_t,
            *own_saved[:3],
            *other_back[1:3],
            *(a for a, _ in attn_own),
        ),
        specs={i: ANYWHERE for i in range(9, 9 + len(attn_own))},
        lazy=(2, 3, 4, 5, 6, 7, 8),
        scratch=back_scratch,
        flops=back_flops,
        rels=[r for _, r in attn_own],
        out_rels=written(own_rels),
        share=share,
    )
    own_back = parts(False, grads, own_rels), keep, send, sums
    done = (mlp_sum.from_near, mlp_sum.from_both, attn_sum.from_d, attn_sum.from_x)
    mlp_sum.far()
    peer_back = swap(own_back[2], "head", 1)
    attn_sum.own(own_back[0], *done, mlp_sum.away_total)
    attn_sum.turn_by_x(own_back[3])
    input_grad, small = call(
        last_kernel,
        "last",
        [((share, width), F32), ((PARAM_ROWS, width), F32)],
        (
            params,
            x_rows,
            dh1_rows,
            dy_sum,
            own_back[1],
            peer_back,
            mid_sums,
            own_mlp[4],
            other_mlp[4],
            own_back[3],
            other_back[3],
        ),
    )
    attn_sum.own_rest_joined(mlp_sum.away_total)
    attn_sum.near_sum(mlp_sum.away_total)
    attn_sum.far()
    def finish(kernel, name, outs, inputs):
        def first(ref, info):
            return ref.at[pl.ds(0, 1)]

        if aligned:
            terms = range(7, 1 + len(inputs))
            views = {i: ((1, *inputs[i - 1].shape[1:]), first) for i in terms}
            return call(kernel, name, outs, (params, *inputs), views=views)
        blocks = {i: IN_VMEM for i in range(1, 1 + len(inputs))}
        return call(kernel, name, [(*o, IN_VMEM) for o in outs], (params, *inputs), specs=blocks)

    by_row = (3, shard_rows, head_cols)
    fc1, fc2 = w_fc1.shape, w_fc2.T.shape
    *fc1_outs, fc2_grad, fc2_mom, fc2_new, fc2_avg = finish(
        finish_mlp_kernel,
        "finish_mlp",
        [(fc1, F32)] * 4 + [(fc2, F32)] * 4,
        (
            after(w_fc1, attn_sum.away_total),
            mom_fc1,
            avg_fc1,
            w_fc2.T,
            mom_fc2.T,
            avg_fc2.T,
            *mlp_sum.terms(),
        ),
    )
    fc1_grad, fc1_mom, fc1_new, fc1_avg = fc1_outs
    fc2_grad, fc2_mom, fc2_new, fc2_avg = (v.T for v in (fc2_grad, fc2_mom, fc2_new, fc2_avg))
    small = small + swap(small, "head", 1)
    small = after(small, mlp_sum.from_away)
    over = over_x(small), over_y(small), over_both(small)
    small = (small + over[0]) + (over[1] + over[2])
    small = after(small, fc1_grad)
    for mask in line_masks(count):
        if mask == 2:
            small = after(small, attn_sum.from_away)
        small = small + swap(small, "dp", mask)
    gain_grad = small[:2]
    bias_grad = small[2:12].reshape(biases.shape)

    *qkv_outs, proj_grad, proj_mom, proj_new, proj_avg = finish(
        finish_attn_kernel,
        "finish_attn",
        [(by_row, F32)] * 4 + [(w_proj.shape, F32)] * 4,
        (
            *(jnp.swapaxes(v, 0, 1) for v in (w_qkv, mom_qkv, avg_qkv)),
            w_proj,
            mom_proj,
            avg_proj,
            *attn_sum.terms(),
        ),
    )
    qkv_grad, qkv_mom, qkv_new, qkv_avg = (jnp.swapaxes(v, 0, 1) for v in qkv_outs)

    gain_mom_new, gain_new, gain_avg_new = update(
        gains, gain_grad, gain_mom, gain_avg, RATE_SMALL, 0.0
    )
    bias_mom_new, bias_new, bias_avg_new = update(
        biases, bias_grad, bias_mom, bias_avg, RATE_SMALL, 0.0
    )
    return (
        block_out,
        input_grad,
        qkv_grad,
        qkv_mom,
        qkv_new,
        qkv_avg,
        proj_grad,
        proj_mom,
        proj_new,
        proj_avg,
        fc1_grad,
        fc1_mom,
        fc1_new,
        fc1_avg,
        fc2_grad,
        fc2_mom,
        fc2_new,
        fc2_avg,
        gain_grad,
        gain_mom_new,
        gain_new,
        gain_avg_new,
        bias_grad,
        bias_mom_new,
        bias_new,
        bias_avg_new,
    )
def solution(mesh):
    return jax.shard_map(
        shards,
        mesh=mesh,
        in_specs=(
            P("dp", None),
            P("dp"),
            P(("dp", "head"), None),
            P("dp", None, "head"),
            P("head", "dp"),
            P("dp", "head"),
            P("head", "dp"),
            P("dp", None, "head"),
            P("head", "dp"),
            P("dp", "head"),
            P("head", "dp"),
            P("dp", None, "head"),
            P("head", "dp"),
            P("dp", "head"),
            P("head", "dp"),
            P(),
            P(),
            P(),
            P(),
            P(),
            P(),
        ),
        out_specs=(
            P(("dp", "head"), None),
            P(("dp", "head"), None),
            P("dp", None, "head"),
            P("dp", None, "head"),
            P("dp", None, "head"),
            P("dp", None, "head"),
            P("head", "dp"),
            P("head", "dp"),
            P("head", "dp"),
            P("head", "dp"),
            P("dp", "head"),
            P("dp", "head"),
            P("dp", "head"),
            P("dp", "head"),
            P("head", "dp"),
            P("head", "dp"),
            P("head", "dp"),
            P("head", "dp"),
            P(),
            P(),
            P(),
            P(),
            P(),
            P(),
            P(),
            P(),
        ),
        check_vma=False,
    )
```
